32 devices in a mesh: section: 4 (over y, x), tp: 8 (over z, core).
Axes of the slice: x: 2, y: 2, z: 4, core: 2. Of those that a mesh axis runs over, the one named last changes fastest.
Arguments:
- inputs: bfloat16 [2, 128, 8192], P(None, 'tp'), may hold values from -50 to 50
- cotangent: bfloat16 [2, 128, 8192], P(None, 'tp'), may hold values from -50 to 50
- gains: bfloat16 [4, 8192], P('section'), may hold values from 0.099609375 to 1.8984375
- up_blocks: bfloat16 [4, 18432, 4096], P('section', 'tp'), may hold values from -0.09375 to 0.09375
- up_index: int32 [4, 18432], P('section', 'tp'), may hold values from 0 to 4095, as said below
- up_count: int32 [4, 8], P('section', 'tp'), may hold values from 1792 to 2304, as said below
- down_blocks: bfloat16 [4, 18432, 4096], P('section', 'tp'), may hold values from -0.0625 to 0.0625
- down_index: int32 [4, 18432], P('section', 'tp'), may hold values from 0 to 4095, as said below
- down_count: int32 [4, 8], P('section', 'tp'), may hold values from 1792 to 2304, as said below
Outputs:
- section_outputs: bfloat16 [4, 2, 128, 8192], P('section', None, 'tp')
- input_grads: bfloat16 [4, 2, 128, 8192], P('section', None, 'tp')
- up_grads: bfloat16 [4, 18432, 4096], P('section', 'tp')
- down_grads: bfloat16 [4, 18432, 4096], P('section', 'tp')
The draws below stay inside these ranges and needn't reach their ends.
Inputs may be any that keep to these rules, and one draw needn't show every extreme that they name: Within one group's 2304 entries of up_index no value repeats. Within one group's 2304 entries of down_index no value repeats. `up_count`: in every layer one group has exactly 2304 live blocks and another exactly 1792. `down_count`: in every layer one group has exactly 2304 live blocks and another exactly 1792.
All inputs are finite; a program needn't handle non-finite values.
Results may differ from the reference program's by a relative error of at most 0.03.
Values may be sent and summed in bfloat16 or wider, within the bound.
No kernel may reach another device: no remote copies, remote signals or barrier semaphores. Data moves between devices by JAX's collectives and lax.ppermute only.
A program may use at most 448 MiB of HBM per device.

```python
import math
from functools import partial
import jax
import jax.numpy as jnp
from jax import lax

D = 8192
FF = 16384
BLOCK = 64
MICRO = 2
TOKENS = 128
SECTIONS = 4
SHARD_BLOCKS = 4096
CAP = 2304
LOW = 1792
SLOTS = 18432
N_TP = 8


def spread_rows(base_key, shape):
    noise_key, row_key, col_key = jax.random.split(base_key, 3)
    noise = jnp.clip(jax.random.normal(noise_key, shape, jnp.float32), -4.0, 4.0)
    row_scale = jnp.exp(jax.random.uniform(row_key, shape[:-1] + (1,), jnp.float32, math.log(0.3), math.log(3.0)))
    col_scale = jnp.exp(jax.random.uniform(col_key, shape[-1:], jnp.float32, math.log(0.3), math.log(3.0)))
    return noise * row_scale * col_scale


def block_lists(base_key):
    group_keys = jax.random.split(base_key, SECTIONS * (SLOTS // CAP))
    lists = jax.vmap(lambda one_key: jax.random.permutation(one_key, SHARD_BLOCKS)[:CAP])(group_keys)
    return lists.reshape(SECTIONS, SLOTS).astype(jnp.int32)


def block_counts(base_key):
    groups = SLOTS // CAP
    count_key, full_key = jax.random.split(base_key)
    counts = jax.random.randint(count_key, (SECTIONS, groups), LOW, CAP + 1, jnp.int32)
    fullest = jax.random.randint(full_key, (SECTIONS, 1), 0, groups, jnp.int32)
    emptiest = (fullest + 1) % groups
    positions = jnp.arange(groups, dtype=jnp.int32)[None, :]
    counts = jnp.where(positions == fullest, CAP, counts)
    counts = jnp.where(positions == emptiest, LOW, counts)
    return counts.astype(jnp.int32)


def draw_inputs(key, part):
    return spread_rows(jax.random.fold_in(key, 11), (MICRO, TOKENS, D)).astype(jnp.bfloat16)


def draw_cotangent(key, part):
    return spread_rows(jax.random.fold_in(key, 23), (MICRO, TOKENS, D)).astype(jnp.bfloat16)


def draw_up_index(key, part):
    return block_lists(jax.random.fold_in(key, 31))


def draw_down_index(key, part):
    return block_lists(jax.random.fold_in(key, 37))


def draw_up_count(key, part):
    return block_counts(jax.random.fold_in(key, 41))


def draw_down_count(key, part):
    return block_counts(jax.random.fold_in(key, 43))


def shard_levels(rng, extent, cuts, smallest, high):
    def one(position, blocks):
        steps = jax.random.uniform(jax.random.fold_in(jax.random.fold_in(rng, 6), position), (blocks,), jnp.float32, smallest / len(cuts), high / len(cuts))
        return jnp.repeat(jnp.exp(steps), extent[position] // blocks).reshape((-1,) + (1,) * (len(extent) - position - 1))

    loudness = one(*cuts[0])
    for cut in cuts[1:]:
        loudness = loudness * one(*cut)
    return loudness


def scatter_about(stream_key, extent, scale, limit, cuts=(), kind=jnp.bfloat16):
    factor_of = shard_levels(stream_key, extent, cuts, -0.22, 0.18) if cuts else 1.0
    values = jax.random.normal(stream_key, extent, jnp.float32) * scale * factor_of
    return jnp.minimum(jnp.maximum(values, -limit), limit).astype(kind)


def setup_inputs(seed: int = 0) -> dict:
    seeds = jax.random.split(jax.random.key(seed), 10)
    return {
        "inputs": draw_inputs(jax.random.fold_in(seeds[9], 71), 0),
        "cotangent": draw_cotangent(jax.random.fold_in(seeds[9], 71), 0),
        "gains": jnp.clip(1.0 + 0.18 * jax.random.normal(seeds[2], (SECTIONS, D), jnp.float32), 0.099609375, 1.8984375).astype(jnp.bfloat16),
        "up_blocks": scatter_about(seeds[3], (SECTIONS, SLOTS, BLOCK * BLOCK), (D // 2) ** -0.5, 0.09375, ((0, 4), (1, 8))),
        "up_index": draw_up_index(jax.random.fold_in(seeds[9], 71), 0),
        "up_count": draw_up_count(jax.random.fold_in(seeds[9], 71), 0),
        "down_blocks": scatter_about(seeds[6], (SECTIONS, SLOTS, BLOCK * BLOCK), (FF // 2) ** -0.5, 0.0625, ((0, 4), (1, 8))),
        "down_index": draw_down_index(jax.random.fold_in(seeds[9], 71), 0),
        "down_count": draw_down_count(jax.random.fold_in(seeds[9], 71), 0),
    }


NORM_EPSILON = 1e-05

def densify(blocks, block_index, live_count, row_blocks, col_blocks):
    side = blocks.shape[-1]
    live_slots = jnp.arange(blocks.shape[0]) < live_count
    kept_values = jnp.where(live_slots[:, None, None], blocks, jnp.zeros_like(blocks))
    block_grid = jnp.zeros((row_blocks * col_blocks, side, side), blocks.dtype).at[block_index].add(kept_values)
    block_grid = block_grid.reshape(row_blocks, col_blocks, side, side).transpose(0, 2, 1, 3)
    return block_grid.reshape(row_blocks * side, col_blocks * side)

def extract(dense_grad, block_index, live_count, row_blocks, col_blocks):
    side = dense_grad.shape[0] // row_blocks
    block_grid = dense_grad.reshape(row_blocks, side, col_blocks, side).transpose(0, 2, 1, 3)
    block_grid = block_grid.reshape(row_blocks * col_blocks, side, side)
    picked = block_grid[block_index]
    live_slots = jnp.arange(block_index.shape[0]) < live_count
    return jnp.where(live_slots[:, None, None], picked, jnp.zeros_like(picked)).astype(jnp.bfloat16)

def normalize(activ_rows, gain):
    values = activ_rows.astype(jnp.float32)
    inv_rms = lax.rsqrt(lax.optimization_barrier(jnp.mean(values * values, axis=-1, keepdims=True)) + NORM_EPSILON)
    return (values, inv_rms, (values * inv_rms * gain.astype(jnp.float32)).astype(jnp.bfloat16))

def layer_weights(blocks, block_index, live_count, row_blocks, col_blocks):
    groups = live_count.shape[0]
    slot_count = block_index.shape[0] // groups
    side = blocks.shape[-1]
    maker = partial(densify, row_blocks=row_blocks, col_blocks=col_blocks)
    return jax.vmap(maker)(blocks.reshape(groups, slot_count, side, side), block_index.reshape(groups, slot_count), live_count)

def forward_section(activ_in, gain, w_up, w_down):
    values, inv_rms, normed = normalize(activ_in, gain)
    token_rows = normed.reshape(-1, normed.shape[-1])

    def group_step(running, weight_pair):
        up_proj = jnp.dot(token_rows, weight_pair[0], preferred_element_type=jnp.float32)
        hidden = jax.nn.silu(up_proj).astype(jnp.bfloat16)
        part = jnp.dot(hidden, weight_pair[1], preferred_element_type=jnp.float32).astype(jnp.bfloat16)
        part = lax.optimization_barrier(part)
        return (running + part.astype(jnp.float32), None)
    mixed_rows, _ = lax.scan(group_step, jnp.zeros(token_rows.shape, jnp.float32), (w_up, w_down))
    return (values + mixed_rows.reshape(values.shape)).astype(jnp.bfloat16)

def backward_section(activ_in, grad_out, gain, w_up, w_down, up_index, up_count, down_index, down_count):
    values, inv_rms, normed = normalize(activ_in, gain)
    features = activ_in.shape[-1]
    token_rows = normed.reshape(-1, features)
    grad_rows = grad_out.reshape(-1, features)
    group_width = w_up.shape[-1]
    row_blocks = features // BLOCK
    group_blocks = group_width // BLOCK
    groups = up_count.shape[0]

    def group_step(running, pieces):
        weight_up, weight_down, index_up, count_up, index_down, count_down = pieces
        up_proj = jnp.dot(token_rows, weight_up, preferred_element_type=jnp.float32)
        hidden = jax.nn.silu(up_proj).astype(jnp.bfloat16)
        act_grad = jnp.dot(grad_rows, weight_down.T, preferred_element_type=jnp.float32)
        sigmoid_up = jax.nn.sigmoid(up_proj)
        up_grad = (act_grad * sigmoid_up * (1.0 + up_proj * (1.0 - sigmoid_up))).astype(jnp.bfloat16)
        back_part = jnp.dot(up_grad, weight_up.T, preferred_element_type=jnp.float32).astype(jnp.bfloat16)
        back_part = lax.optimization_barrier(back_part)
        up_dense = jnp.dot(token_rows.T, up_grad, preferred_element_type=jnp.float32)
        down_dense = jnp.dot(hidden.T, grad_rows, preferred_element_type=jnp.float32)
        up_part = extract(up_dense, index_up, count_up, row_blocks, group_blocks)
        down_part = extract(down_dense, index_down, count_down, group_blocks, row_blocks)
        return (running + back_part.astype(jnp.float32), (up_part, down_part))
    pieces = (w_up, w_down, up_index.reshape(groups, -1), up_count, down_index.reshape(groups, -1), down_count)
    norm_grad, grads = lax.scan(group_step, jnp.zeros(grad_rows.shape, jnp.float32), pieces)
    scaled_grad = norm_grad.reshape(values.shape) * gain.astype(jnp.float32)
    norm_term = inv_rms * scaled_grad - values * (inv_rms * inv_rms * inv_rms) * lax.optimization_barrier(jnp.mean(scaled_grad * values, axis=-1, keepdims=True))
    grad_in = (grad_out.astype(jnp.float32) + norm_term).astype(jnp.bfloat16)
    up_part, down_part = grads
    return (grad_in, up_part.reshape(-1, BLOCK * BLOCK), down_part.reshape(-1, BLOCK * BLOCK))

def reference(inputs, cotangent, gains, up_blocks, up_index, up_count, down_blocks, down_index, down_count):
    row_blocks = D // BLOCK
    group_blocks = FF // N_TP // BLOCK
    up_square = up_blocks.reshape(SECTIONS, SLOTS, BLOCK, BLOCK)
    down_square = down_blocks.reshape(SECTIONS, SLOTS, BLOCK, BLOCK)
    activations = [inputs]
    for section_index in range(SECTIONS):
        w_up = layer_weights(up_square[section_index], up_index[section_index], up_count[section_index], row_blocks, group_blocks)
        w_down = layer_weights(down_square[section_index], down_index[section_index], down_count[section_index], group_blocks, row_blocks)
        activations.append(forward_section(activations[-1], gains[section_index], w_up, w_down))
    grad_now = cotangent
    grads_in, grads_up, grads_down = ([], [], [])
    for section_index in reversed(range(SECTIONS)):
        w_up = layer_weights(up_square[section_index], up_index[section_index], up_count[section_index], row_blocks, group_blocks)
        w_down = layer_weights(down_square[section_index], down_index[section_index], down_count[section_index], group_blocks, row_blocks)
        grad_now, grad_up, grad_down = backward_section(activations[section_index], grad_now, gains[section_index], w_up, w_down, up_index[section_index], up_count[section_index], down_index[section_index], down_count[section_index])
        grads_in.insert(0, grad_now)
        grads_up.insert(0, grad_up)
        grads_down.insert(0, grad_down)
    return (jnp.stack(activations[1:]), jnp.stack(grads_in), jnp.stack(grads_up), jnp.stack(grads_down))
```

```python
import functools

import jax
import jax.numpy as jnp
from jax import lax
from jax.experimental import pallas as pl
from jax.experimental.pallas import tpu as pltpu
from jax.sharding import PartitionSpec as P

FF = 16384
BLOCK = 64
PAIR = 2 * BLOCK
HALF = BLOCK // 2
STRIP = 256
VMEM_BYTES = 58 * 2**20

NORM_EPSILON = 1e-05


def slot_step(slots):
    for size in (192, 128, 64, 32, 16):
        if slots % size == 0:
            return size
    return slots


def split_order(rows_split):
    first = lax.broadcasted_iota(jnp.int32, (STRIP, STRIP), 0)
    second = lax.broadcasted_iota(jnp.int32, (STRIP, STRIP), 1)
    split, natural = (first, second) if rows_split else (second, first)
    inner = split % BLOCK
    target = (split - inner) + 2 * (inner % HALF) + inner // HALF
    return (target == natural).astype(jnp.bfloat16)


def densify_kernel(slots, step_slots, index_ref, count_ref, block_ref, out_ref, held, packed, halves, order, place):
    step = pl.program_id(0)
    load_steps = slots // step_slots
    width = out_ref.shape[1]
    pairs = width // PAIR

    @pl.when(step == 0)
    def _():
        order[...] = split_order(False)
        held[slots] = jnp.zeros((HALF, PAIR), jnp.bfloat16)

        @pl.loop(0, place.shape[0] // 16)
        def _(group):
            for lane in range(16):
                place[group * 16 + lane] = slots

    @pl.when(step < load_steps)
    def _():
        first = step * step_slots
        for start in range(0, step_slots, 16):
            packed[start : start + 16] = block_ref[start : start + 16, :].reshape(16, HALF, PAIR)

        @pl.loop(0, step_slots // 16)
        def _(group):
            start = pl.multiple_of(group * 16, 16)
            for lane in range(16):
                slot = first + start + lane
                held[slot] = packed[start + lane]

                @pl.when(slot < count_ref[0])
                def _():
                    place[index_ref[slot]] = slot

    @pl.when(step >= load_steps)
    def _():
        strip = step - load_steps
        lane = lax.broadcasted_iota(jnp.int32, (HALF, PAIR), 1)
        low = lane < BLOCK
        for row in range(STRIP // BLOCK):
            for col in range(pairs):
                pair = (strip * (STRIP // BLOCK) + row) * pairs + col
                left = held[place[2 * pair]]
                right = held[place[2 * pair + 1]]
                top = row * BLOCK
                lanes = slice(col * PAIR, (col + 1) * PAIR)
                halves[top : top + HALF, lanes] = jnp.where(low, left, pltpu.roll(right, BLOCK, 1))
                halves[top + HALF : top + BLOCK, lanes] = jnp.where(low, pltpu.roll(left, BLOCK, 1), right)
        piece = min(width, 512)
        for start in range(0, width, piece):
            out_ref[:, start : start + piece] = jnp.dot(
                order[...], halves[:, start : start + piece], preferred_element_type=jnp.float32
            ).astype(jnp.bfloat16)


def densify(blocks, block_index, live_count, row_blocks, col_blocks):
    slots = blocks.shape[0]
    step_slots = slot_step(slots)
    load_steps = slots // step_slots
    width = min(col_blocks * BLOCK, 2048)
    across = col_blocks * BLOCK // width
    strips = row_blocks * BLOCK // STRIP
    if across > 1:
        piece_blocks = width // BLOCK
        row, col = block_index // col_blocks, block_index % col_blocks
        strip, row = row // 4, row % 4
        block_index = ((strip * across + col // piece_blocks) * 4 + row) * piece_blocks + col % piece_blocks

    def out_place(step, index, count):
        spot = jnp.maximum(step - load_steps, 0)
        return (spot // across, spot % across)

    return pl.pallas_call(
        functools.partial(densify_kernel, slots, step_slots),
        grid_spec=pltpu.PrefetchScalarGridSpec(
            num_scalar_prefetch=2,
            grid=(load_steps + strips * across,),
            in_specs=[
                pl.BlockSpec((step_slots, BLOCK * BLOCK), lambda step, index, count: (jnp.minimum(step, load_steps - 1), 0))
            ],
            out_specs=pl.BlockSpec((STRIP, width), out_place),
            scratch_shapes=[
                pltpu.VMEM((slots + 1, HALF, PAIR), jnp.bfloat16),
                pltpu.VMEM((step_slots, HALF, PAIR), jnp.bfloat16),
                pltpu.VMEM((STRIP, width), jnp.bfloat16),
                pltpu.VMEM((STRIP, STRIP), jnp.bfloat16),
                pltpu.SMEM((row_blocks * col_blocks,), jnp.int32),
            ],
        ),
        out_shape=jax.ShapeDtypeStruct((row_blocks * BLOCK, col_blocks * BLOCK), jnp.bfloat16),
        compiler_params=pltpu.CompilerParams(
            dimension_semantics=("arbitrary",), vmem_limit_bytes=VMEM_BYTES
        ),
        name="densify",
    )(block_index, live_count, blocks)


def block_grads_kernel(strips, step_slots, index_ref, count_ref, left_ref, right_ref, out_ref, dense, order, packed):
    step = pl.program_id(0)
    width = right_ref.shape[1]
    pairs = width // PAIR

    @pl.when(step == 0)
    def _():
        order[...] = split_order(False)

    @pl.when(step < strips)
    def _():
        left = jnp.dot(left_ref[...], order[...], preferred_element_type=jnp.float32).astype(jnp.bfloat16)
        left = left.T
        piece = min(width, 512)
        for start in range(0, width, piece):
            product = jnp.dot(
                left, right_ref[:, start : start + piece], preferred_element_type=jnp.float32
            ).astype(jnp.bfloat16)
            for row in range(STRIP // BLOCK):
                for col in range(piece // PAIR):
                    pair = (step * (STRIP // BLOCK) + row) * pairs + start // PAIR + col
                    dense[pair] = product[row * BLOCK : (row + 1) * BLOCK, col * PAIR : (col + 1) * PAIR]

    @pl.when(step >= strips)
    def _():
        first = (step - strips) * step_slots
        lane = lax.broadcasted_iota(jnp.int32, (HALF, PAIR), 1)
        low = lane < BLOCK

        @pl.loop(0, step_slots // 16)
        def _(group):
            start = pl.multiple_of(group * 16, 16)
            for one in range(16):
                slot = first + start + one
                spot = index_ref[slot]
                odd = spot % 2
                live = slot < count_ref[0]
                tile = dense[spot // 2]
                even_rows, odd_rows = tile[:HALF], tile[HALF:]
                even_swap = pltpu.roll(even_rows, BLOCK, 1)
                odd_swap = pltpu.roll(odd_rows, BLOCK, 1)
                from_left = jnp.where(low, even_rows, odd_swap)
                from_right = jnp.where(low, even_swap, odd_rows)
                picked = jnp.where(odd == 0, from_left, from_right)
                packed[one] = jnp.where(live, picked, jnp.zeros_like(picked))
            out_ref[pl.ds(start, 16), :] = packed[...].reshape(16, BLOCK * BLOCK)


def block_grads(left, right, block_index, live_count):
    tokens, rows = left.shape
    cols = right.shape[1]
    slots = block_index.shape[0]
    step_slots = slot_step(slots)
    strips = rows // STRIP
    return pl.pallas_call(
        functools.partial(block_grads_kernel, strips, step_slots),
        grid_spec=pltpu.PrefetchScalarGridSpec(
            num_scalar_prefetch=2,
            grid=(strips + slots // step_slots,),
            in_specs=[
                pl.BlockSpec((tokens, STRIP), lambda step, index, count: (0, jnp.minimum(step, strips - 1))),
                pl.BlockSpec((tokens, cols), lambda step, index, count: (0, 0)),
            ],
            out_specs=pl.BlockSpec(
                (step_slots, BLOCK * BLOCK), lambda step, index, count: (jnp.maximum(step - strips, 0), 0)
            ),
            scratch_shapes=[
                pltpu.VMEM((rows * cols // (BLOCK * PAIR), BLOCK, PAIR), jnp.bfloat16),
                pltpu.VMEM((STRIP, STRIP), jnp.bfloat16),
                pltpu.VMEM((16, HALF, PAIR), jnp.bfloat16),
            ],
        ),
        out_shape=jax.ShapeDtypeStruct((slots, BLOCK * BLOCK), jnp.bfloat16),
        compiler_params=pltpu.CompilerParams(
            dimension_semantics=("arbitrary",), vmem_limit_bytes=VMEM_BYTES
        ),
        name="block_grads",
    )(block_index, live_count, left, right)


def from_behind(array, axis, by):
    count = lax.axis_size(axis)
    pairs = [(i, i + by) for i in range(count) if 0 <= i + by < count]
    return lax.ppermute(array, axis, pairs)


def normalize(activ_rows, gain):
    values = activ_rows.astype(jnp.float32)
    inv_rms = lax.rsqrt(jnp.mean(values * values, axis=-1, keepdims=True) + NORM_EPSILON)
    return (values, inv_rms, (values * inv_rms * gain.astype(jnp.float32)).astype(jnp.bfloat16))


def all_rows(local_rows):
    return lax.all_gather(local_rows, "tp", axis=0, tiled=True)


def row_sums(term_fn, local_count):
    return lax.psum_scatter(
        term_fn(jnp.int32(0), lax.axis_size("tp") * local_count).astype(jnp.bfloat16),
        "tp",
        scatter_dimension=0,
        tiled=True,
    ).astype(jnp.float32)


def pass_along(local_rows, offset):
    return from_behind(local_rows, "section", offset)


def guarded(active, compute, out_shape):
    return lax.cond(active, compute, lambda: jnp.zeros(out_shape, jnp.float32))


def shards(
    inputs, cotangent, gains, up_blocks, up_index, up_count, down_blocks, down_index, down_count
):
    micro_count, tok_rows, features = inputs.shape
    side = BLOCK
    section_index = lax.axis_index("section")
    section_count = lax.axis_size("section")
    tick_count = section_count + micro_count - 1
    group_width = FF // lax.axis_size("tp")
    total_rows = tok_rows * lax.axis_size("tp")
    row_blocks = features // side
    group_blocks = group_width // side
    w_up = densify(up_blocks[0], up_index[0], up_count[0], row_blocks, group_blocks)
    w_down = densify(down_blocks[0], down_index[0], down_count[0], group_blocks, row_blocks)
    gain = gains[0]
    carried = jnp.zeros((tok_rows, features), jnp.bfloat16)
    kept_input, kept_rows, kept_up, layer_outs = ([], [], [], [])
    for tick_index in range(tick_count):
        active = (tick_index - section_index >= 0) & (tick_index - section_index < micro_count)
        fresh_rows = inputs[min(tick_index, micro_count - 1)]
        current = jnp.where(section_index == 0, fresh_rows, carried)
        values, inv_rms, normed = normalize(current, gain)
        token_rows = all_rows(normed)
        up_proj = guarded(
            active,
            lambda: jnp.dot(token_rows, w_up, preferred_element_type=jnp.float32),
            (total_rows, group_width),
        )
        hidden = jax.nn.silu(up_proj).astype(jnp.bfloat16)

        def forward_term(first_row, row_count):
            return guarded(
                active,
                lambda: jnp.dot(hidden, w_down, preferred_element_type=jnp.float32),
                (row_count, features),
            )

        mixed_rows = row_sums(forward_term, tok_rows)
        layer_out = (values + mixed_rows).astype(jnp.bfloat16)
        layer_outs.append(layer_out)
        kept_input.append(current)
        kept_rows.append(token_rows)
        kept_up.append(up_proj)
        carried = pass_along(layer_out, 1)
    stacked_out = jnp.stack(layer_outs)
    section_outputs = jnp.stack(
        [
            lax.dynamic_index_in_dim(stacked_out, micro_index + section_index, 0, keepdims=False)
            for micro_index in range(micro_count)
        ]
    )[None]
    stacked_input = jnp.stack(kept_input)
    stacked_rows = jnp.stack(kept_rows)
    stacked_up = jnp.stack(kept_up)
    lag = section_count - 1 - section_index
    carried = jnp.zeros((tok_rows, features), jnp.bfloat16)
    grad_list, kept_grad, kept_upgrad = ([], [], [])
    for tick_index in range(tick_count):
        micro_now = tick_index - lag
        active = (micro_now >= 0) & (micro_now < micro_count)
        slot_index = jnp.clip(micro_now, 0, micro_count - 1)
        fresh_rows = lax.dynamic_index_in_dim(cotangent, slot_index, 0, keepdims=False)
        incoming = jnp.where(section_index == section_count - 1, fresh_rows, carried)
        forward_tick = jnp.clip(micro_now + section_index, 0, tick_count - 1)
        current = lax.dynamic_index_in_dim(stacked_input, forward_tick, 0, keepdims=False)
        token_rows = lax.dynamic_index_in_dim(stacked_rows, forward_tick, 0, keepdims=False)
        up_proj = lax.dynamic_index_in_dim(stacked_up, forward_tick, 0, keepdims=False)
        values, inv_rms, normed = normalize(current, gain)
        grad_rows = all_rows(incoming)
        hidden = jax.nn.silu(up_proj).astype(jnp.bfloat16)
        act_grad = guarded(
            active,
            lambda: jnp.dot(grad_rows, w_down.T, preferred_element_type=jnp.float32),
            (total_rows, group_width),
        )
        sigmoid_up = jax.nn.sigmoid(up_proj)
        up_grad = (act_grad * sigmoid_up * (1.0 + up_proj * (1.0 - sigmoid_up))).astype(
            jnp.bfloat16
        )

        def backward_term(first_row, row_count):
            return guarded(
                active,
                lambda: jnp.dot(up_grad, w_up.T, preferred_element_type=jnp.float32),
                (row_count, features),
            )

        norm_grad = row_sums(backward_term, tok_rows)
        kept_grad.append(grad_rows)
        kept_upgrad.append(up_grad)
        scaled_grad = norm_grad * gain.astype(jnp.float32)
        norm_term = inv_rms * scaled_grad - values * (inv_rms * inv_rms * inv_rms) * jnp.mean(
            scaled_grad * values, axis=-1, keepdims=True
        )
        grad_in = (incoming.astype(jnp.float32) + norm_term).astype(jnp.bfloat16)
        grad_list.append(grad_in)
        carried = pass_along(grad_in, -1)
    grad_all = lax.dynamic_slice_in_dim(jnp.stack(kept_grad), lag, micro_count, 0).reshape(
        micro_count * total_rows, features
    )
    upgrad_all = lax.dynamic_slice_in_dim(jnp.stack(kept_upgrad), lag, micro_count, 0).reshape(
        micro_count * total_rows, group_width
    )
    rows_all = lax.dynamic_slice_in_dim(stacked_rows, section_index, micro_count, 0).reshape(
        micro_count * total_rows, features
    )
    up_all = lax.dynamic_slice_in_dim(stacked_up, section_index, micro_count, 0).reshape(
        micro_count * total_rows, group_width
    )
    hidden_all = jax.nn.silu(up_all).astype(jnp.bfloat16)
    stacked_grad = jnp.stack(grad_list)
    input_grads = jnp.stack(
        [
            lax.dynamic_index_in_dim(stacked_grad, micro_index + lag, 0, keepdims=False)
            for micro_index in range(micro_count)
        ]
    )[None]
    up_grads = block_grads(rows_all, upgrad_all, up_index[0], up_count[0])[None]
    down_grads = block_grads(hidden_all, grad_all, down_index[0], down_count[0])[None]
    return (section_outputs, input_grads, up_grads, down_grads)


def solution(mesh):
    return jax.shard_map(
        shards,
        mesh=mesh,
        in_specs=(
            P(None, "tp", None),
            P(None, "tp", None),
            P("section", None),
            P("section", "tp", None),
            P("section", "tp"),
            P("section", "tp"),
            P("section", "tp", None),
            P("section", "tp"),
            P("section", "tp"),
        ),
        out_specs=(
            P("section", None, "tp", None),
            P("section", None, "tp", None),
            P("section", "tp", None),
            P("section", "tp", None),
        ),
        check_vma=False,
    )
```

```python
import functools

import jax
import jax.numpy as jnp
from jax import lax
from jax.experimental import pallas as pl
from jax.experimental.pallas import tpu as pltpu
from jax.sharding import PartitionSpec as P

FF = 16384
BLOCK = 64
PAIR = 2 * BLOCK
HALF = BLOCK // 2
STRIP = 256
VMEM_BYTES = 58 * 2**20

NORM_EPSILON = 1e-05


def slot_step(slots):
    for size in (192, 128, 64, 32, 16):
        if slots % size == 0:
            return size
    return slots


def split_order(rows_split):
    first = lax.broadcasted_iota(jnp.int32, (STRIP, STRIP), 0)
    second = lax.broadcasted_iota(jnp.int32, (STRIP, STRIP), 1)
    split, natural = (first, second) if rows_split else (second, first)
    inner = split % BLOCK
    target = (split - inner) + 2 * (inner % HALF) + inner // HALF
    return (target == natural).astype(jnp.bfloat16)


def densify_kernel(slots, step_slots, index_ref, count_ref, block_ref, out_ref, held, packed, halves, order, place):
    step = pl.program_id(0)
    load_steps = slots // step_slots
    width = out_ref.shape[1]
    pairs = width // PAIR

    @pl.when(step == 0)
    def _():
        order[...] = split_order(False)
        held[slots] = jnp.zeros((HALF, PAIR), jnp.bfloat16)

        @pl.loop(0, place.shape[0] // 16)
        def _(group):
            for lane in range(16):
                place[group * 16 + lane] = slots

    @pl.when(step < load_steps)
    def _():
        first = step * step_slots
        for start in range(0, step_slots, 16):
            packed[start : start + 16] = block_ref[start : start + 16, :].reshape(16, HALF, PAIR)

        @pl.loop(0, step_slots // 16)
        def _(group):
            start = pl.multiple_of(group * 16, 16)
            for lane in range(16):
                slot = first + start + lane
                held[slot] = packed[start + lane]

                @pl.when(slot < count_ref[0])
                def _():
                    place[index_ref[slot]] = slot

    @pl.when(step >= load_steps)
    def _():
        strip = step - load_steps
        lane = lax.broadcasted_iota(jnp.int32, (HALF, PAIR), 1)
        low = lane < BLOCK
        for row in range(STRIP // BLOCK):
            for col in range(pairs):
                pair = (strip * (STRIP // BLOCK) + row) * pairs + col
                left = held[place[2 * pair]]
                right = held[place[2 * pair + 1]]
                top = row * BLOCK
                lanes = slice(col * PAIR, (col + 1) * PAIR)
                halves[top : top + HALF, lanes] = jnp.where(low, left, pltpu.roll(right, BLOCK, 1))
                halves[top + HALF : top + BLOCK, lanes] = jnp.where(low, pltpu.roll(left, BLOCK, 1), right)
        piece = min(width, 512)
        for start in range(0, width, piece):
            out_ref[:, start : start + piece] = jnp.dot(
                order[...], halves[:, start : start + piece], preferred_element_type=jnp.float32
            ).astype(jnp.bfloat16)


def densify(blocks, block_index, live_count, row_blocks, col_blocks):
    slots = blocks.shape[0]
    step_slots = slot_step(slots)
    load_steps = slots // step_slots
    width = min(col_blocks * BLOCK, 2048)
    across = col_blocks * BLOCK // width
    strips = row_blocks * BLOCK // STRIP
    if across > 1:
        piece_blocks = width // BLOCK
        row, col = block_index // col_blocks, block_index % col_blocks
        strip, row = row // 4, row % 4
        block_index = ((strip * across + col // piece_blocks) * 4 + row) * piece_blocks + col % piece_blocks

    def out_place(step, index, count):
        spot = jnp.maximum(step - load_steps, 0)
        return (spot // across, spot % across)

    return pl.pallas_call(
        functools.partial(densify_kernel, slots, step_slots),
        grid_spec=pltpu.PrefetchScalarGridSpec(
            num_scalar_prefetch=2,
            grid=(load_steps + strips * across,),
            in_specs=[
                pl.BlockSpec((step_slots, BLOCK * BLOCK), lambda step, index, count: (jnp.minimum(step, load_steps - 1), 0))
            ],
            out_specs=pl.BlockSpec((STRIP, width), out_place),
            scratch_shapes=[
                pltpu.VMEM((slots + 1, HALF, PAIR), jnp.bfloat16),
                pltpu.VMEM((step_slots, HALF, PAIR), jnp.bfloat16),
                pltpu.VMEM((STRIP, width), jnp.bfloat16),
                pltpu.VMEM((STRIP, STRIP), jnp.bfloat16),
                pltpu.SMEM((row_blocks * col_blocks,), jnp.int32),
            ],
        ),
        out_shape=jax.ShapeDtypeStruct((row_blocks * BLOCK, col_blocks * BLOCK), jnp.bfloat16),
        compiler_params=pltpu.CompilerParams(
            dimension_semantics=("arbitrary",), vmem_limit_bytes=VMEM_BYTES
        ),
        name="densify",
    )(block_index, live_count, blocks)


def block_grads_kernel(strips, step_slots, index_ref, count_ref, left_ref, right_ref, out_ref, dense, order, packed):
    step = pl.program_id(0)
    width = right_ref.shape[1]
    pairs = width // PAIR

    @pl.when(step == 0)
    def _():
        order[...] = split_order(False)

    @pl.when(step < strips)
    def _():
        left = jnp.dot(left_ref[...], order[...], preferred_element_type=jnp.float32).astype(jnp.bfloat16)
        left = left.T
        piece = min(width, 512)
        for start in range(0, width, piece):
            product = jnp.dot(
                left, right_ref[:, start : start + piece], preferred_element_type=jnp.float32
            ).astype(jnp.bfloat16)
            for row in range(STRIP // BLOCK):
                for col in range(piece // PAIR):
                    pair = (step * (STRIP // BLOCK) + row) * pairs + start // PAIR + col
                    dense[pair] = product[row * BLOCK : (row + 1) * BLOCK, col * PAIR : (col + 1) * PAIR]

    @pl.when(step >= strips)
    def _():
        first = (step - strips) * step_slots
        lane = lax.broadcasted_iota(jnp.int32, (HALF, PAIR), 1)
        low = lane < BLOCK

        @pl.loop(0, step_slots // 16)
        def _(group):
            start = pl.multiple_of(group * 16, 16)
            for one in range(16):
                slot = first + start + one
                spot = index_ref[slot]
                odd = spot % 2
                live = slot < count_ref[0]
                tile = dense[spot // 2]
                even_rows, odd_rows = tile[:HALF], tile[HALF:]
                even_swap = pltpu.roll(even_rows, BLOCK, 1)
                odd_swap = pltpu.roll(odd_rows, BLOCK, 1)
                from_left = jnp.where(low, even_rows, odd_swap)
                from_right = jnp.where(low, even_swap, odd_rows)
                picked = jnp.where(odd == 0, from_left, from_right)
                packed[one] = jnp.where(live, picked, jnp.zeros_like(picked))
            out_ref[pl.ds(start, 16), :] = packed[...].reshape(16, BLOCK * BLOCK)


def block_grads(left, right, block_index, live_count):
    tokens, rows = left.shape
    cols = right.shape[1]
    slots = block_index.shape[0]
    step_slots = slot_step(slots)
    strips = rows // STRIP
    return pl.pallas_call(
        functools.partial(block_grads_kernel, strips, step_slots),
        grid_spec=pltpu.PrefetchScalarGridSpec(
            num_scalar_prefetch=2,
            grid=(strips + slots // step_slots,),
            in_specs=[
                pl.BlockSpec((tokens, STRIP), lambda step, index, count: (0, jnp.minimum(step, strips - 1))),
                pl.BlockSpec((tokens, cols), lambda step, index, count: (0, 0)),
            ],
            out_specs=pl.BlockSpec(
                (step_slots, BLOCK * BLOCK), lambda step, index, count: (jnp.maximum(step - strips, 0), 0)
            ),
            scratch_shapes=[
                pltpu.VMEM((rows * cols // (BLOCK * PAIR), BLOCK, PAIR), jnp.bfloat16),
                pltpu.VMEM((STRIP, STRIP), jnp.bfloat16),
                pltpu.VMEM((16, HALF, PAIR), jnp.bfloat16),
            ],
        ),
        out_shape=jax.ShapeDtypeStruct((slots, BLOCK * BLOCK), jnp.bfloat16),
        compiler_params=pltpu.CompilerParams(
            dimension_semantics=("arbitrary",), vmem_limit_bytes=VMEM_BYTES
        ),
        name="block_grads",
    )(block_index, live_count, left, right)


def forward_kernel(up_steps, act_ref, gain_ref, up_ref, down_ref, part_ref, rows_ref, proj_ref, hidden):
    step = pl.program_id(0)

    @pl.when(step == 0)
    def _():
        values = act_ref[...].astype(jnp.float32)
        inv_rms = lax.rsqrt(jnp.mean(values * values, axis=-1, keepdims=True) + NORM_EPSILON)
        rows_ref[...] = (values * inv_rms * gain_ref[...].astype(jnp.float32)).astype(jnp.bfloat16)

    @pl.when(step < up_steps)
    def _():
        proj = jnp.dot(rows_ref[...], up_ref[...], preferred_element_type=jnp.float32)
        proj_ref[...] = proj
        hidden[step] = (proj * (1.0 / (1.0 + jnp.exp(-proj)))).astype(jnp.bfloat16)

    @pl.when(step >= up_steps)
    def _():
        width = hidden.shape[2]
        total = jnp.dot(hidden[0], down_ref[:width, :], preferred_element_type=jnp.float32)
        for piece in range(1, up_steps):
            total += jnp.dot(
                hidden[piece], down_ref[piece * width : (piece + 1) * width, :], preferred_element_type=jnp.float32
            )
        part_ref[...] = total.astype(jnp.bfloat16)


def forward_layer(activ, gain, w_up, w_down):
    tokens, features = activ.shape
    units = w_up.shape[1]
    up_width, down_width = min(units, 256), 512
    up_steps, down_steps = units // up_width, features // down_width
    return pl.pallas_call(
        functools.partial(forward_kernel, up_steps),
        grid=(up_steps + down_steps,),
        in_specs=[
            pl.BlockSpec((tokens, features), lambda step: (0, 0)),
            pl.BlockSpec((1, features), lambda step: (0, 0)),
            pl.BlockSpec((features, up_width), lambda step: (0, jnp.minimum(step, up_steps - 1))),
            pl.BlockSpec((units, down_width), lambda step: (0, jnp.maximum(step - up_steps, 0))),
        ],
        out_specs=[
            pl.BlockSpec((tokens, down_width), lambda step: (0, jnp.maximum(step - up_steps, 0))),
            pl.BlockSpec((tokens, features), lambda step: (0, 0)),
            pl.BlockSpec((tokens, up_width), lambda step: (0, jnp.minimum(step, up_steps - 1))),
        ],
        out_shape=[
            jax.ShapeDtypeStruct((tokens, features), jnp.bfloat16),
            jax.ShapeDtypeStruct((tokens, features), jnp.bfloat16),
            jax.ShapeDtypeStruct((tokens, units), jnp.float32),
        ],
        scratch_shapes=[pltpu.VMEM((up_steps, tokens, up_width), jnp.bfloat16)],
        compiler_params=pltpu.CompilerParams(
            dimension_semantics=("arbitrary",), vmem_limit_bytes=VMEM_BYTES
        ),
        name="forward_layer",
    )(activ, gain, w_up, w_down)


def backward_kernel(down_steps, grad_ref, proj_ref, down_ref, up_ref, part_ref, upgrad_ref, hidden_ref, held):
    step = pl.program_id(0)
    transposed = (((1,), (1,)), ((), ()))

    @pl.when(step < down_steps)
    def _():
        act_grad = lax.dot_general(grad_ref[...], down_ref[...], transposed, preferred_element_type=jnp.float32)
        proj = proj_ref[...]
        gate = 1.0 / (1.0 + jnp.exp(-proj))
        hidden_ref[...] = (proj * gate).astype(jnp.bfloat16)
        up_grad = (act_grad * gate * (1.0 + proj * (1.0 - gate))).astype(jnp.bfloat16)
        upgrad_ref[...] = up_grad
        held[step] = up_grad

    @pl.when(step >= down_steps)
    def _():
        width = held.shape[2]
        total = lax.dot_general(held[0], up_ref[:, :width], transposed, preferred_element_type=jnp.float32)
        for piece in range(1, down_steps):
            total += lax.dot_general(
                held[piece],
                up_ref[:, piece * width : (piece + 1) * width],
                transposed,
                preferred_element_type=jnp.float32,
            )
        part_ref[...] = total.astype(jnp.bfloat16)


def backward_layer(grad, proj, w_up, w_down):
    tokens, features = grad.shape
    units = w_up.shape[1]
    down_width, up_width = min(units, 256), 512
    down_steps, up_steps = units // down_width, features // up_width
    return pl.pallas_call(
        functools.partial(backward_kernel, down_steps),
        grid=(down_steps + up_steps,),
        in_specs=[
            pl.BlockSpec((tokens, features), lambda step: (0, 0)),
            pl.BlockSpec((tokens, down_width), lambda step: (0, jnp.minimum(step, down_steps - 1))),
            pl.BlockSpec((down_width, features), lambda step: (jnp.minimum(step, down_steps - 1), 0)),
            pl.BlockSpec((up_width, units), lambda step: (jnp.maximum(step - down_steps, 0), 0)),
        ],
        out_specs=[
            pl.BlockSpec((tokens, up_width), lambda step: (0, jnp.maximum(step - down_steps, 0))),
            pl.BlockSpec((tokens, down_width), lambda step: (0, jnp.minimum(step, down_steps - 1))),
            pl.BlockSpec((tokens, down_width), lambda step: (0, jnp.minimum(step, down_steps - 1))),
        ],
        out_shape=[
            jax.ShapeDtypeStruct((tokens, features), jnp.bfloat16),
            jax.ShapeDtypeStruct((tokens, units), jnp.bfloat16),
            jax.ShapeDtypeStruct((tokens, units), jnp.bfloat16),
        ],
        scratch_shapes=[pltpu.VMEM((down_steps, tokens, down_width), jnp.bfloat16)],
        compiler_params=pltpu.CompilerParams(
            dimension_semantics=("arbitrary",), vmem_limit_bytes=VMEM_BYTES
        ),
        name="backward_layer",
    )(grad, proj, w_down, w_up)


def from_behind(array, axis, by):
    count = lax.axis_size(axis)
    pairs = [(i, i + by) for i in range(count) if 0 <= i + by < count]
    return lax.ppermute(array, axis, pairs)


def all_rows(local_rows):
    return lax.all_gather(local_rows, "tp", axis=0, tiled=True)


def shards(
    inputs, cotangent, gains, up_blocks, up_index, up_count, down_blocks, down_index, down_count
):
    micro_count, tok_rows, features = inputs.shape
    section_index = lax.axis_index("section")
    section_count = lax.axis_size("section")
    tp_index = lax.axis_index("tp")
    group_width = FF // lax.axis_size("tp")
    local_count = micro_count * tok_rows
    total_rows = local_count * lax.axis_size("tp")
    row_blocks = features // BLOCK
    group_blocks = group_width // BLOCK
    activ = all_rows(inputs.reshape(local_count, features))
    w_up = densify(up_blocks[0], up_index[0], up_count[0], row_blocks, group_blocks)
    w_down = densify(down_blocks[0], down_index[0], down_count[0], group_blocks, row_blocks)
    gain = gains[0]

    def own_rows(rows):
        return lax.dynamic_slice_in_dim(rows, tp_index * local_count, local_count, 0)

    kept_rows = jnp.zeros((total_rows, features), jnp.bfloat16)
    kept_proj = jnp.zeros((total_rows, group_width), jnp.float32)
    layer_input = jnp.zeros((local_count, features), jnp.bfloat16)
    layer_output = jnp.zeros((local_count, features), jnp.bfloat16)
    for stage in range(section_count):
        active = section_index == stage

        def run_forward():
            return list(forward_layer(activ, gains, w_up, w_down))

        def skip_forward():
            return [jnp.zeros((total_rows, features), jnp.bfloat16), kept_rows, kept_proj]

        partial, kept_rows, kept_proj = lax.cond(active, run_forward, skip_forward)
        layer_input = jnp.where(active, own_rows(activ), layer_input)
        if stage == section_count - 1:
            mixed = lax.psum_scatter(partial, "tp", scatter_dimension=0, tiled=True)
            last = (layer_input.astype(jnp.float32) + mixed.astype(jnp.float32)).astype(jnp.bfloat16)
            layer_output = jnp.where(active, last, layer_output)
        else:
            mixed = lax.psum(partial, ("section", "tp"))
            activ = (activ.astype(jnp.float32) + mixed.astype(jnp.float32)).astype(jnp.bfloat16)
            layer_output = jnp.where(active, own_rows(activ), layer_output)

    values = layer_input.astype(jnp.float32)
    inv_rms = lax.rsqrt(jnp.mean(values * values, axis=-1, keepdims=True) + NORM_EPSILON)
    kept_grad = jnp.zeros((total_rows, features), jnp.bfloat16)
    kept_upgrad = jnp.zeros((total_rows, group_width), jnp.bfloat16)
    kept_hidden = jnp.zeros((total_rows, group_width), jnp.bfloat16)
    incoming = cotangent.reshape(local_count, features)
    input_grad = jnp.zeros((local_count, features), jnp.bfloat16)
    for stage in reversed(range(section_count)):
        active = section_index == stage
        grad_rows = all_rows(incoming)

        def run_backward():
            return list(backward_layer(grad_rows, kept_proj, w_up, w_down)) + [grad_rows]

        def skip_backward():
            return [jnp.zeros((total_rows, features), jnp.bfloat16), kept_upgrad, kept_hidden, kept_grad]

        partial, kept_upgrad, kept_hidden, kept_grad = lax.cond(active, run_backward, skip_backward)
        norm_grad = lax.psum_scatter(partial, "tp", scatter_dimension=0, tiled=True).astype(jnp.float32)
        scaled_grad = norm_grad * gain.astype(jnp.float32)
        norm_term = inv_rms * scaled_grad - values * (inv_rms * inv_rms * inv_rms) * jnp.mean(
            scaled_grad * values, axis=-1, keepdims=True
        )
        grad_in = (incoming.astype(jnp.float32) + norm_term).astype(jnp.bfloat16)
        input_grad = jnp.where(active, grad_in, input_grad)
        if stage:
            incoming = from_behind(grad_in, "section", -1)
    up_grads = block_grads(kept_rows, kept_upgrad, up_index[0], up_count[0])
    down_grads = block_grads(kept_hidden, kept_grad, down_index[0], down_count[0])
    shape = (1, micro_count, tok_rows, features)
    return (layer_output.reshape(shape), input_grad.reshape(shape), up_grads[None], down_grads[None])


def solution(mesh):
    return jax.shard_map(
        shards,
        mesh=mesh,
        in_specs=(
            P(None, "tp", None),
            P(None, "tp", None),
            P("section", None),
            P("section", "tp", None),
            P("section", "tp"),
            P("section", "tp"),
            P("section", "tp", None),
            P("section", "tp"),
            P("section", "tp"),
        ),
        out_specs=(
            P("section", None, "tp", None),
            P("section", None, "tp", None),
            P("section", "tp", None),
            P("section", "tp", None),
        ),
        check_vma=False,
    )
```

```python
import functools

import jax
import jax.numpy as jnp
from jax import lax
from jax.experimental import pallas as pl
from jax.experimental.pallas import tpu as pltpu
from jax.sharding import PartitionSpec as P

FF = 16384
BLOCK = 64
PAIR = 2 * BLOCK
HALF = BLOCK // 2
STRIP = 256
VMEM_BYTES = 58 * 2**20

NORM_EPSILON = 1e-05


def slot_step(slots):
    for size in (192, 128, 64, 32, 16):
        if slots % size == 0:
            return size
    return slots


def split_order(rows_split):
    first = lax.broadcasted_iota(jnp.int32, (STRIP, STRIP), 0)
    second = lax.broadcasted_iota(jnp.int32, (STRIP, STRIP), 1)
    split, natural = (first, second) if rows_split else (second, first)
    inner = split % BLOCK
    target = (split - inner) + 2 * (inner % HALF) + inner // HALF
    return (target == natural).astype(jnp.bfloat16)


def densify_kernel(slots, step_slots, index_ref, count_ref, block_ref, out_ref, held, packed, halves, order, place):
    step = pl.program_id(0)
    load_steps = slots // step_slots
    width = out_ref.shape[1]
    pairs = width // PAIR

    @pl.when(step == 0)
    def _():
        order[...] = split_order(False)
        held[slots] = jnp.zeros((HALF, PAIR), jnp.bfloat16)

        @pl.loop(0, place.shape[0] // 16)
        def _(group):
            for lane in range(16):
                place[group * 16 + lane] = slots

    @pl.when(step < load_steps)
    def _():
        first = step * step_slots
        for start in range(0, step_slots, 16):
            packed[start : start + 16] = block_ref[start : start + 16, :].reshape(16, HALF, PAIR)

        @pl.loop(0, step_slots // 16)
        def _(group):
            start = pl.multiple_of(group * 16, 16)
            for lane in range(16):
                slot = first + start + lane
                held[slot] = packed[start + lane]

                @pl.when(slot < count_ref[0])
                def _():
                    place[index_ref[slot]] = slot

    @pl.when(step >= load_steps)
    def _():
        strip = step - load_steps
        lane = lax.broadcasted_iota(jnp.int32, (HALF, PAIR), 1)
        low = lane < BLOCK
        for row in range(STRIP // BLOCK):
            for col in range(pairs):
                pair = (strip * (STRIP // BLOCK) + row) * pairs + col
                left = held[place[2 * pair]]
                right = held[place[2 * pair + 1]]
                top = row * BLOCK
                lanes = slice(col * PAIR, (col + 1) * PAIR)
                halves[top : top + HALF, lanes] = jnp.where(low, left, pltpu.roll(right, BLOCK, 1))
                halves[top + HALF : top + BLOCK, lanes] = jnp.where(low, pltpu.roll(left, BLOCK, 1), right)
        piece = min(width, 512)
        for start in range(0, width, piece):
            out_ref[:, start : start + piece] = jnp.dot(
                order[...], halves[:, start : start + piece], preferred_element_type=jnp.float32
            ).astype(jnp.bfloat16)


def densify(blocks, block_index, live_count, row_blocks, col_blocks):
    slots = blocks.shape[0]
    step_slots = slot_step(slots)
    load_steps = slots // step_slots
    width = min(col_blocks * BLOCK, 2048)
    across = col_blocks * BLOCK // width
    strips = row_blocks * BLOCK // STRIP
    if across > 1:
        piece_blocks = width // BLOCK
        row, col = block_index // col_blocks, block_index % col_blocks
        strip, row = row // 4, row % 4
        block_index = ((strip * across + col // piece_blocks) * 4 + row) * piece_blocks + col % piece_blocks

    def out_place(step, index, count):
        spot = jnp.maximum(step - load_steps, 0)
        return (spot // across, spot % across)

    return pl.pallas_call(
        functools.partial(densify_kernel, slots, step_slots),
        grid_spec=pltpu.PrefetchScalarGridSpec(
            num_scalar_prefetch=2,
            grid=(load_steps + strips * across,),
            in_specs=[
                pl.BlockSpec((step_slots, BLOCK * BLOCK), lambda step, index, count: (jnp.minimum(step, load_steps - 1), 0))
            ],
            out_specs=pl.BlockSpec((STRIP, width), out_place),
            scratch_shapes=[
                pltpu.VMEM((slots + 1, HALF, PAIR), jnp.bfloat16),
                pltpu.VMEM((step_slots, HALF, PAIR), jnp.bfloat16),
                pltpu.VMEM((STRIP, width), jnp.bfloat16),
                pltpu.VMEM((STRIP, STRIP), jnp.bfloat16),
                pltpu.SMEM((row_blocks * col_blocks,), jnp.int32),
            ],
        ),
        out_shape=jax.ShapeDtypeStruct((row_blocks * BLOCK, col_blocks * BLOCK), jnp.bfloat16),
        compiler_params=pltpu.CompilerParams(
            dimension_semantics=("arbitrary",), vmem_limit_bytes=VMEM_BYTES
        ),
        name="densify",
    )(block_index, live_count, blocks)


def block_grads_kernel(strips, step_slots, index_ref, count_ref, left_ref, right_ref, out_ref, dense, order, packed):
    step = pl.program_id(0)
    width = right_ref.shape[1]
    pairs = width // PAIR

    @pl.when(step == 0)
    def _():
        order[...] = split_order(False)

    @pl.when(step < strips)
    def _():
        left = jnp.dot(left_ref[...], order[...], preferred_element_type=jnp.float32).astype(jnp.bfloat16)
        left = left.T
        piece = min(width, 512)
        for start in range(0, width, piece):
            product = jnp.dot(
                left, right_ref[:, start : start + piece], preferred_element_type=jnp.float32
            ).astype(jnp.bfloat16)
            for row in range(STRIP // BLOCK):
                for col in range(piece // PAIR):
                    pair = (step * (STRIP // BLOCK) + row) * pairs + start // PAIR + col
                    dense[pair] = product[row * BLOCK : (row + 1) * BLOCK, col * PAIR : (col + 1) * PAIR]

    @pl.when(step >= strips)
    def _():
        first = (step - strips) * step_slots
        lane = lax.broadcasted_iota(jnp.int32, (HALF, PAIR), 1)
        low = lane < BLOCK

        @pl.loop(0, step_slots // 16)
        def _(group):
            start = pl.multiple_of(group * 16, 16)
            for one in range(16):
                slot = first + start + one
                spot = index_ref[slot]
                odd = spot % 2
                live = slot < count_ref[0]
                tile = dense[spot // 2]
                even_rows, odd_rows = tile[:HALF], tile[HALF:]
                even_swap = pltpu.roll(even_rows, BLOCK, 1)
                odd_swap = pltpu.roll(odd_rows, BLOCK, 1)
                from_left = jnp.where(low, even_rows, odd_swap)
                from_right = jnp.where(low, even_swap, odd_rows)
                picked = jnp.where(odd == 0, from_left, from_right)
                packed[one] = jnp.where(live, picked, jnp.zeros_like(picked))
            out_ref[pl.ds(start, 16), :] = packed[...].reshape(16, BLOCK * BLOCK)


def block_grads(left, right, block_index, live_count, tokens):
    rows = left.shape[1]
    cols = right.shape[1]
    slots = block_index.shape[0]
    step_slots = slot_step(slots)
    strips = rows // STRIP
    return pl.pallas_call(
        functools.partial(block_grads_kernel, strips, step_slots),
        grid_spec=pltpu.PrefetchScalarGridSpec(
            num_scalar_prefetch=2,
            grid=(strips + slots // step_slots,),
            in_specs=[
                pl.BlockSpec((tokens, STRIP), lambda step, index, count: (0, jnp.minimum(step, strips - 1))),
                pl.BlockSpec((tokens, cols), lambda step, index, count: (0, 0)),
            ],
            out_specs=pl.BlockSpec(
                (step_slots, BLOCK * BLOCK), lambda step, index, count: (jnp.maximum(step - strips, 0), 0)
            ),
            scratch_shapes=[
                pltpu.VMEM((rows * cols // (BLOCK * PAIR), BLOCK, PAIR), jnp.bfloat16),
                pltpu.VMEM((STRIP, STRIP), jnp.bfloat16),
                pltpu.VMEM((16, HALF, PAIR), jnp.bfloat16),
            ],
        ),
        out_shape=jax.ShapeDtypeStruct((slots, BLOCK * BLOCK), jnp.bfloat16),
        compiler_params=pltpu.CompilerParams(
            dimension_semantics=("arbitrary",), vmem_limit_bytes=VMEM_BYTES
        ),
        name="block_grads",
    )(block_index, live_count, left, right)


def normalize(activ_rows, gain):
    values = activ_rows.astype(jnp.float32)
    inv_rms = lax.rsqrt(jnp.mean(values * values, axis=-1, keepdims=True) + NORM_EPSILON)
    return (values, inv_rms, (values * inv_rms * gain.astype(jnp.float32)).astype(jnp.bfloat16))


def all_rows(local_rows):
    return lax.all_gather(local_rows, "tp", axis=0, tiled=True)


def row_sums(partial):
    return lax.psum_scatter(partial, "tp", scatter_dimension=0, tiled=True).astype(jnp.float32)


def forward_layer(rows, w_up, w_down):
    up_proj = jnp.dot(rows, w_up, preferred_element_type=jnp.float32)
    hidden = jax.nn.silu(up_proj).astype(jnp.bfloat16)
    partial = jnp.dot(hidden, w_down, preferred_element_type=jnp.float32).astype(jnp.bfloat16)
    return partial, up_proj, hidden


def backward_layer(grad_rows, up_proj, w_up, w_down):
    act_grad = jnp.dot(grad_rows, w_down.T, preferred_element_type=jnp.float32)
    gate = jax.nn.sigmoid(up_proj)
    up_grad = (act_grad * gate * (1.0 + up_proj * (1.0 - gate))).astype(jnp.bfloat16)
    partial = jnp.dot(up_grad, w_up.T, preferred_element_type=jnp.float32).astype(jnp.bfloat16)
    return partial, up_grad


def put(buffer, value, place):
    return lax.dynamic_update_slice_in_dim(buffer, value, place * value.shape[0], 0)


def take(buffer, place, count):
    return lax.dynamic_slice_in_dim(buffer, place * count, count, 0)


def shards(
    inputs, cotangent, gains, up_blocks, up_index, up_count, down_blocks, down_index, down_count
):
    micro_count, tok_rows, features = inputs.shape
    section_index = lax.axis_index("section")
    section_count = lax.axis_size("section")
    last = section_count - 1
    tp_count = lax.axis_size("tp")
    group_width = FF // tp_count
    total_rows = tok_rows * tp_count
    row_blocks = features // BLOCK
    group_blocks = group_width // BLOCK
    gain = gains[0]
    first_rows = all_rows(normalize(inputs[0], gain)[2])
    cot_rows = [all_rows(cotangent[micro]) for micro in range(micro_count)]
    w_up = densify(up_blocks[0], up_index[0], up_count[0], row_blocks, group_blocks)
    w_down = densify(down_blocks[0], down_index[0], down_count[0], group_blocks, row_blocks)

    places = micro_count + 1
    kept_rows = jnp.zeros((places * total_rows, features), jnp.bfloat16)
    kept_up = jnp.zeros((places * total_rows, group_width), jnp.float32)
    kept_hidden = jnp.zeros((places * total_rows, group_width), jnp.bfloat16)
    kept_grad = jnp.zeros((places * total_rows, features), jnp.bfloat16)
    kept_upgrad = jnp.zeros((places * total_rows, group_width), jnp.bfloat16)
    kept_input = jnp.zeros((places * tok_rows, features), jnp.bfloat16)
    kept_output = jnp.zeros((places * tok_rows, features), jnp.bfloat16)
    kept_ingrad = jnp.zeros((places * tok_rows, features), jnp.bfloat16)
    final_parts = []

    rounds = 2 * section_count - 1
    ticks = rounds + micro_count - 1
    current = inputs[0]
    gathered = first_rows
    for tick in range(ticks):
        micro_fwd = tick - section_index
        micro_bwd = tick - (2 * last - section_index)
        fwd_active = (micro_fwd >= 0) & (micro_fwd < micro_count)
        bwd_active = (micro_bwd >= 0) & (micro_bwd < micro_count)
        any_fwd = tick <= last + micro_count - 1
        any_bwd = tick >= last
        partial = None
        if any_fwd:
            place = jnp.where(fwd_active, micro_fwd, micro_count)
            partial, up_proj, hidden = lax.cond(
                fwd_active,
                lambda: forward_layer(gathered, w_up, w_down),
                lambda: (
                    jnp.zeros((total_rows, features), jnp.bfloat16),
                    jnp.zeros((total_rows, group_width), jnp.float32),
                    jnp.zeros((total_rows, group_width), jnp.bfloat16),
                ),
            )
            kept_rows = put(kept_rows, gathered, place)
            kept_up = put(kept_up, up_proj, place)
            kept_hidden = put(kept_hidden, hidden, place)
            kept_input = put(kept_input, current, place)
            if tick >= last:
                final_parts.append(partial)
        if any_bwd:
            place_bwd = jnp.where(bwd_active, micro_bwd, micro_count)
            grad_rows, incoming = gathered, current
            if tick - last < micro_count:
                is_last = section_index == last
                grad_rows = jnp.where(is_last, cot_rows[tick - last], gathered)
                incoming = jnp.where(is_last, cotangent[tick - last], current)
            up_proj = take(kept_up, place_bwd, total_rows)
            otherwise = jnp.zeros((total_rows, features), jnp.bfloat16) if partial is None else partial
            partial, up_grad = lax.cond(
                bwd_active,
                lambda: backward_layer(grad_rows, up_proj, w_up, w_down),
                lambda: (otherwise, jnp.zeros((total_rows, group_width), jnp.bfloat16)),
            )
            kept_grad = put(kept_grad, grad_rows, place_bwd)
            kept_upgrad = put(kept_upgrad, up_grad, place_bwd)
        sums = row_sums(partial)
        send = None
        if any_fwd and tick < last + micro_count - 1:
            layer_out = (current.astype(jnp.float32) + sums).astype(jnp.bfloat16)
            kept_output = put(kept_output, layer_out, place)
            send = layer_out
        if any_bwd:
            values, inv_rms, _ = normalize(take(kept_input, place_bwd, tok_rows), gain)
            scaled_grad = sums * gain.astype(jnp.float32)
            norm_term = inv_rms * scaled_grad - values * (inv_rms * inv_rms * inv_rms) * jnp.mean(
                scaled_grad * values, axis=-1, keepdims=True
            )
            grad_in = (incoming.astype(jnp.float32) + norm_term).astype(jnp.bfloat16)
            kept_ingrad = put(kept_ingrad, grad_in, place_bwd)
            send = grad_in if send is None else jnp.where(bwd_active, grad_in, send)
        if tick + 1 == ticks:
            break
        pairs = []
        for micro in range(micro_count):
            done = tick - micro
            if 0 <= done < rounds - 1:
                pairs.append((last - abs(last - done), last - abs(last - done - 1)))
        current = lax.ppermute(send, "section", pairs)
        if tick + 1 < micro_count:
            current = jnp.where(section_index == 0, inputs[tick + 1], current)
        next_fwd = tick + 1 <= last + micro_count - 1
        next_bwd = tick + 1 > last
        source = current
        if next_fwd:
            source = normalize(current, gain)[2]
            if next_bwd:
                source = jnp.where(section_index + micro_count > tick + 1, source, current)
        gathered = all_rows(source)

    final = jnp.concatenate([part.reshape(tp_count, 1, tok_rows, features) for part in final_parts], axis=1)
    final, _ = lax.optimization_barrier((final, grad_in))
    final_sums = row_sums(final.reshape(micro_count * total_rows, features))
    kept_input = kept_input[: micro_count * tok_rows]
    final_out = (kept_input.astype(jnp.float32) + final_sums).astype(jnp.bfloat16)
    outputs = jnp.where(section_index == last, final_out, kept_output[: micro_count * tok_rows])
    up_grads = block_grads(kept_rows, kept_upgrad, up_index[0], up_count[0], micro_count * total_rows)
    down_grads = block_grads(kept_hidden, kept_grad, down_index[0], down_count[0], micro_count * total_rows)
    shape = (1, micro_count, tok_rows, features)
    return (
        outputs.reshape(shape),
        kept_ingrad[: micro_count * tok_rows].reshape(shape),
        up_grads[None],
        down_grads[None],
    )


def solution(mesh):
    return jax.shard_map(
        shards,
        mesh=mesh,
        in_specs=(
            P(None, "tp", None),
            P(None, "tp", None),
            P("section", None),
            P("section", "tp", None),
            P("section", "tp"),
            P("section", "tp"),
            P("section", "tp", None),
            P("section", "tp"),
            P("section", "tp"),
        ),
        out_specs=(
            P("section", None, "tp", None),
            P("section", None, "tp", None),
            P("section", "tp", None),
            P("section", "tp", None),
        ),
        check_vma=False,
    )
```

```python
import functools

import jax
import jax.numpy as jnp
from jax import lax
from jax.experimental import pallas as pl
from jax.experimental.pallas import tpu as pltpu
from jax.sharding import PartitionSpec as P

FF = 16384
BLOCK = 64
MICRO = 2
PAIR = 2 * BLOCK
HALF = BLOCK // 2
STRIP = 256
VMEM_BYTES = 58 * 2**20

NORM_EPSILON = 1e-05


def slot_step(slots):
    for size in (192, 128, 64, 32, 16):
        if slots % size == 0:
            return size
    return slots


def split_order(rows_split):
    first = lax.broadcasted_iota(jnp.int32, (STRIP, STRIP), 0)
    second = lax.broadcasted_iota(jnp.int32, (STRIP, STRIP), 1)
    split, natural = (first, second) if rows_split else (second, first)
    inner = split % BLOCK
    target = (split - inner) + 2 * (inner % HALF) + inner // HALF
    return (target == natural).astype(jnp.bfloat16)


def densify_kernel(slots, step_slots, index_ref, count_ref, block_ref, out_ref, held, packed, halves, order, place):
    step = pl.program_id(0)
    load_steps = slots // step_slots
    width = out_ref.shape[1]
    pairs = width // PAIR

    @pl.when(step == 0)
    def _():
        order[...] = split_order(False)
        held[slots] = jnp.zeros((HALF, PAIR), jnp.bfloat16)

        @pl.loop(0, place.shape[0] // 16)
        def _(group):
            for lane in range(16):
                place[group * 16 + lane] = slots

    @pl.when(step < load_steps)
    def _():
        first = step * step_slots
        for start in range(0, step_slots, 16):
            packed[start : start + 16] = block_ref[start : start + 16, :].reshape(16, HALF, PAIR)

        @pl.loop(0, step_slots // 16)
        def _(group):
            start = pl.multiple_of(group * 16, 16)
            for lane in range(16):
                slot = first + start + lane
                held[slot] = packed[start + lane]

                @pl.when(slot < count_ref[0])
                def _():
                    place[index_ref[slot]] = slot

    @pl.when(step >= load_steps)
    def _():
        strip = step - load_steps
        lane = lax.broadcasted_iota(jnp.int32, (HALF, PAIR), 1)
        low = lane < BLOCK
        for row in range(STRIP // BLOCK):
            for col in range(pairs):
                pair = (strip * (STRIP // BLOCK) + row) * pairs + col
                left = held[place[2 * pair]]
                right = held[place[2 * pair + 1]]
                top = row * BLOCK
                lanes = slice(col * PAIR, (col + 1) * PAIR)
                crossed = pltpu.roll(jnp.where(low, right, left), BLOCK, 1)
                halves[top : top + HALF, lanes] = jnp.where(low, left, crossed)
                halves[top + HALF : top + BLOCK, lanes] = jnp.where(low, crossed, right)
        piece = min(width, 512)
        for start in range(0, width, piece):
            out_ref[:, start : start + piece] = jnp.dot(
                order[...], halves[:, start : start + piece], preferred_element_type=jnp.float32
            ).astype(jnp.bfloat16)


def densify(blocks, block_index, live_count, row_blocks, col_blocks):
    slots = blocks.shape[0]
    step_slots = slot_step(slots)
    load_steps = slots // step_slots
    width = min(col_blocks * BLOCK, 2048)
    across = col_blocks * BLOCK // width
    strips = row_blocks * BLOCK // STRIP
    if across > 1:
        piece_blocks = width // BLOCK
        row, col = block_index // col_blocks, block_index % col_blocks
        strip, row = row // 4, row % 4
        block_index = ((strip * across + col // piece_blocks) * 4 + row) * piece_blocks + col % piece_blocks

    def out_place(step, index, count):
        spot = jnp.maximum(step - load_steps, 0)
        return (spot // across, spot % across)

    return pl.pallas_call(
        functools.partial(densify_kernel, slots, step_slots),
        grid_spec=pltpu.PrefetchScalarGridSpec(
            num_scalar_prefetch=2,
            grid=(load_steps + strips * across,),
            in_specs=[
                pl.BlockSpec((step_slots, BLOCK * BLOCK), lambda step, index, count: (jnp.minimum(step, load_steps - 1), 0))
            ],
            out_specs=pl.BlockSpec((STRIP, width), out_place),
            scratch_shapes=[
                pltpu.VMEM((slots + 1, HALF, PAIR), jnp.bfloat16),
                pltpu.VMEM((step_slots, HALF, PAIR), jnp.bfloat16),
                pltpu.VMEM((STRIP, width), jnp.bfloat16),
                pltpu.VMEM((STRIP, STRIP), jnp.bfloat16),
                pltpu.SMEM((row_blocks * col_blocks,), jnp.int32),
            ],
        ),
        out_shape=jax.ShapeDtypeStruct((row_blocks * BLOCK, col_blocks * BLOCK), jnp.bfloat16),
        compiler_params=pltpu.CompilerParams(
            dimension_semantics=("arbitrary",), vmem_limit_bytes=VMEM_BYTES
        ),
        name="densify",
    )(block_index, live_count, blocks)


def block_grads_kernel(strips, step_slots, index_ref, count_ref, left_ref, right_ref, out_ref, dense, order, packed):
    step = pl.program_id(0)
    width = right_ref.shape[1]
    pairs = width // PAIR

    @pl.when(step == 0)
    def _():
        order[...] = split_order(False)

    @pl.when(step < strips)
    def _():
        left = jnp.dot(left_ref[...], order[...], preferred_element_type=jnp.float32).astype(jnp.bfloat16)
        left = left.T
        piece = min(width, 512)
        for start in range(0, width, piece):
            product = jnp.dot(
                left, right_ref[:, start : start + piece], preferred_element_type=jnp.float32
            ).astype(jnp.bfloat16)
            for row in range(STRIP // BLOCK):
                for col in range(piece // PAIR):
                    pair = (step * (STRIP // BLOCK) + row) * pairs + start // PAIR + col
                    lanes = slice(col * PAIR, (col + 1) * PAIR)
                    dense[2 * pair] = product[row * BLOCK : row * BLOCK + HALF, lanes]
                    dense[2 * pair + 1] = product[row * BLOCK + HALF : (row + 1) * BLOCK, lanes]

    @pl.when(step >= strips)
    def _():
        first = (step - strips) * step_slots
        lane = lax.broadcasted_iota(jnp.int32, (HALF, PAIR), 1)
        low = lane < BLOCK

        @pl.loop(0, step_slots // 16)
        def _(group):
            start = pl.multiple_of(group * 16, 16)
            for one in range(16):
                slot = first + start + one
                spot = index_ref[slot]
                keep = dense[spot]
                other = pltpu.roll(dense[spot ^ 1], BLOCK, 1)
                picked = jnp.where(low == (spot % 2 == 0), keep, other)
                packed[one] = jnp.where(slot < count_ref[0], picked, jnp.zeros_like(picked))
            out_ref[pl.ds(start, 16), :] = packed[...].reshape(16, BLOCK * BLOCK)


def block_grads(left, right, block_index, live_count, tokens):
    rows = left.shape[1]
    cols = right.shape[1]
    slots = block_index.shape[0]
    step_slots = slot_step(slots)
    strips = rows // STRIP
    return pl.pallas_call(
        functools.partial(block_grads_kernel, strips, step_slots),
        grid_spec=pltpu.PrefetchScalarGridSpec(
            num_scalar_prefetch=2,
            grid=(strips + slots // step_slots,),
            in_specs=[
                pl.BlockSpec((tokens, STRIP), lambda step, index, count: (0, jnp.minimum(step, strips - 1))),
                pl.BlockSpec((tokens, cols), lambda step, index, count: (0, 0)),
            ],
            out_specs=pl.BlockSpec(
                (step_slots, BLOCK * BLOCK), lambda step, index, count: (jnp.maximum(step - strips, 0), 0)
            ),
            scratch_shapes=[
                pltpu.VMEM((rows * cols // (HALF * PAIR), HALF, PAIR), jnp.bfloat16),
                pltpu.VMEM((STRIP, STRIP), jnp.bfloat16),
                pltpu.VMEM((16, HALF, PAIR), jnp.bfloat16),
            ],
        ),
        out_shape=jax.ShapeDtypeStruct((slots, BLOCK * BLOCK), jnp.bfloat16),
        compiler_params=pltpu.CompilerParams(
            dimension_semantics=("arbitrary",), vmem_limit_bytes=VMEM_BYTES
        ),
        cost_estimate=pl.CostEstimate(
            flops=6 * tokens * rows * cols, bytes_accessed=6 * rows * cols, transcendentals=0
        ),
        name="block_grads",
    )(block_index, live_count, left, right)


def normalize(activ_rows, gain):
    values = activ_rows.astype(jnp.float32)
    inv_rms = lax.rsqrt(jnp.mean(values * values, axis=-1, keepdims=True) + NORM_EPSILON)
    return (values, inv_rms, (values * inv_rms * gain.astype(jnp.float32)).astype(jnp.bfloat16))


def all_rows(local_rows):
    return lax.all_gather(local_rows, "tp", axis=0, tiled=True)


def row_sums(partial):
    return lax.psum_scatter(partial, "tp", scatter_dimension=0, tiled=True).astype(jnp.float32)


def layer_params():
    return pltpu.CompilerParams(dimension_semantics=("arbitrary",), vmem_limit_bytes=VMEM_BYTES)


def forward_kernel(up_steps, flags, rows_ref, up_ref, down_ref, *rest):
    part_ref, kept_rows_ref, kept_up_ref, kept_hidden_ref, total = rest[-5:]
    step = pl.program_id(0)
    depth = up_ref.shape[0]
    up_active, down_active = flags[0] > 0, flags[1] > 0

    @pl.when(up_active & (step < up_steps))
    def _():
        @pl.when(step == 0)
        def _():
            kept_rows_ref[...] = rows_ref[...]
            total[...] = jnp.zeros_like(total)

        rows = rows_ref[:, pl.ds(pl.multiple_of(step * depth, depth), depth)]
        total[...] += jnp.dot(rows, up_ref[...], preferred_element_type=jnp.float32)

        @pl.when(step == up_steps - 1)
        def _():
            proj = total[...]
            kept_up_ref[...] = proj
            kept_hidden_ref[...] = (proj * (1.0 / (1.0 + jnp.exp(-proj)))).astype(jnp.bfloat16)

    @pl.when(step >= up_steps)
    def _():
        @pl.when(down_active)
        def _():
            part_ref[...] = jnp.dot(
                kept_hidden_ref[...], down_ref[...], preferred_element_type=jnp.float32
            ).astype(jnp.bfloat16)

        @pl.when(jnp.logical_not(down_active))
        def _():
            part_ref[...] = jnp.zeros_like(part_ref)


def forward_layer(flags, rows, w_up, w_down, kept):
    tokens, features = rows.shape
    units = w_up.shape[1]
    depth = 1024
    up_steps = down_steps = features // depth
    last_up = up_steps - 1
    any_space = [pl.BlockSpec(memory_space=pl.ANY)] * len(kept)
    places = (MICRO + 1) * tokens
    return pl.pallas_call(
        functools.partial(forward_kernel, up_steps),
        grid_spec=pltpu.PrefetchScalarGridSpec(
            num_scalar_prefetch=1,
            grid=(up_steps + down_steps,),
            in_specs=[
                pl.BlockSpec((tokens, features), lambda step, flags: (0, 0)),
                pl.BlockSpec((depth, units), lambda step, flags: (flags[0] * jnp.minimum(step, last_up), 0)),
                pl.BlockSpec((units, depth), lambda step, flags: (0, flags[1] * jnp.maximum(step - up_steps, 0))),
            ]
            + any_space,
            out_specs=[
                pl.BlockSpec((tokens, depth), lambda step, flags: (0, jnp.maximum(step - up_steps, 0))),
                pl.BlockSpec((tokens, features), lambda step, flags: (flags[2], 0)),
                pl.BlockSpec((tokens, units), lambda step, flags: (flags[2], 0)),
                pl.BlockSpec((tokens, units), lambda step, flags: (flags[2], 0)),
            ],
            scratch_shapes=[pltpu.VMEM((tokens, units), jnp.float32)],
        ),
        out_shape=[
            jax.ShapeDtypeStruct((tokens, features), jnp.bfloat16),
            jax.ShapeDtypeStruct((places, features), jnp.bfloat16),
            jax.ShapeDtypeStruct((places, units), jnp.float32),
            jax.ShapeDtypeStruct((places, units), jnp.bfloat16),
        ],
        input_output_aliases={4 + number: 1 + number for number in range(len(kept))},
        compiler_params=layer_params(),
        cost_estimate=pl.CostEstimate(
            flops=4 * tokens * features * units, bytes_accessed=4 * features * units, transcendentals=0
        ),
        name="forward_layer",
    )(flags, rows, w_up, w_down, *kept)


def backward_kernel(down_steps, flags, grad_ref, proj_ref, down_ref, up_ref, *rest):
    part_ref, kept_grad_ref, kept_upgrad_ref = rest[-3:]
    step = pl.program_id(0)
    transposed = (((1,), (1,)), ((), ()))
    width = down_ref.shape[0]
    active = flags[0] > 0

    @pl.when(active & (step < down_steps))
    def _():
        @pl.when(step == 0)
        def _():
            kept_grad_ref[...] = grad_ref[...]

        act_grad = lax.dot_general(grad_ref[...], down_ref[...], transposed, preferred_element_type=jnp.float32)
        lanes = pl.ds(pl.multiple_of(step * width, width), width)
        proj = proj_ref[:, lanes]
        gate = 1.0 / (1.0 + jnp.exp(-proj))
        kept_upgrad_ref[:, lanes] = (act_grad * gate * (1.0 + proj * (1.0 - gate))).astype(jnp.bfloat16)

    @pl.when(step >= down_steps)
    def _():
        @pl.when(active)
        def _():
            part_ref[...] = lax.dot_general(
                kept_upgrad_ref[...], up_ref[...], transposed, preferred_element_type=jnp.float32
            ).astype(jnp.bfloat16)

        @pl.when(jnp.logical_not(active))
        def _():
            part_ref[...] = jnp.zeros_like(part_ref)


def backward_layer(flags, grad, kept_up, w_up, w_down, kept):
    tokens, features = grad.shape
    units = w_up.shape[1]
    width, depth = min(units, 256), 1024
    down_steps, up_steps = units // width, features // depth
    last_down = down_steps - 1
    any_space = [pl.BlockSpec(memory_space=pl.ANY)] * len(kept)
    places = (MICRO + 1) * tokens
    return pl.pallas_call(
        functools.partial(backward_kernel, down_steps),
        grid_spec=pltpu.PrefetchScalarGridSpec(
            num_scalar_prefetch=1,
            grid=(down_steps + up_steps,),
            in_specs=[
                pl.BlockSpec((tokens, features), lambda step, flags: (0, 0)),
                pl.BlockSpec((tokens, units), lambda step, flags: (flags[1], 0)),
                pl.BlockSpec((width, features), lambda step, flags: (flags[0] * jnp.minimum(step, last_down), 0)),
                pl.BlockSpec((depth, units), lambda step, flags: (flags[0] * jnp.maximum(step - down_steps, 0), 0)),
            ]
            + any_space,
            out_specs=[
                pl.BlockSpec((tokens, depth), lambda step, flags: (0, jnp.maximum(step - down_steps, 0))),
                pl.BlockSpec((tokens, features), lambda step, flags: (flags[1], 0)),
                pl.BlockSpec((tokens, units), lambda step, flags: (flags[1], 0)),
            ],
        ),
        out_shape=[
            jax.ShapeDtypeStruct((tokens, features), jnp.bfloat16),
            jax.ShapeDtypeStruct((places, features), jnp.bfloat16),
            jax.ShapeDtypeStruct((places, units), jnp.bfloat16),
        ],
        input_output_aliases={5 + number: 1 + number for number in range(len(kept))},
        compiler_params=layer_params(),
        cost_estimate=pl.CostEstimate(
            flops=4 * tokens * features * units, bytes_accessed=4 * features * units, transcendentals=0
        ),
        name="backward_layer",
    )(flags, grad, kept_up, w_down, w_up, *kept)


def put(buffer, value, place):
    return lax.dynamic_update_slice_in_dim(buffer, value, place * value.shape[0], 0)


def take(buffer, place, count):
    return lax.dynamic_slice_in_dim(buffer, place * count, count, 0)


def shards(
    inputs, cotangent, gains, up_blocks, up_index, up_count, down_blocks, down_index, down_count
):
    micro_count, tok_rows, features = inputs.shape
    section_index = lax.axis_index("section")
    section_count = lax.axis_size("section")
    last = section_count - 1
    tp_count = lax.axis_size("tp")
    group_width = FF // tp_count
    total_rows = tok_rows * tp_count
    row_blocks = features // BLOCK
    group_blocks = group_width // BLOCK
    gain = gains[0]
    first_rows = all_rows(normalize(inputs[0], gain)[2])
    cot_rows = [all_rows(cotangent[micro]) for micro in range(micro_count)]
    w_up = densify(up_blocks[0], up_index[0], up_count[0], row_blocks, group_blocks)
    w_down = densify(down_blocks[0], down_index[0], down_count[0], group_blocks, row_blocks)

    places = micro_count + 1
    kept_fwd, kept_bwd = [], []
    kept_input = jnp.zeros((places * tok_rows, features), jnp.bfloat16)
    kept_output = jnp.zeros((places * tok_rows, features), jnp.bfloat16)
    kept_ingrad = jnp.zeros((places * tok_rows, features), jnp.bfloat16)
    is_last = section_index == last

    rounds = 2 * section_count - 1
    ticks = rounds + micro_count - 1
    current = inputs[0]
    gathered = first_rows
    for tick in range(ticks):
        micro_fwd = tick - section_index
        micro_bwd = tick - (2 * last - section_index)
        fwd_active = (micro_fwd >= 0) & (micro_fwd < micro_count)
        bwd_active = (micro_bwd >= 0) & (micro_bwd < micro_count)
        any_fwd = tick <= last + micro_count - 1
        any_bwd = tick >= last
        partial = None
        if any_fwd:
            place = jnp.where(fwd_active, micro_fwd, micro_count)
            down_active = fwd_active & jnp.logical_not(is_last)
            flags = jnp.stack([fwd_active.astype(jnp.int32), down_active.astype(jnp.int32), place])
            partial, *kept_fwd = forward_layer(flags, gathered, w_up, w_down, kept_fwd)
            kept_input = put(kept_input, current, place)
        if any_bwd:
            place_bwd = jnp.where(bwd_active, micro_bwd, micro_count)
            grad_rows, incoming = gathered, current
            if tick == last:
                grad_rows, incoming = cot_rows[0], cotangent[0]
            elif tick - last < micro_count:
                grad_rows = jnp.where(is_last, cot_rows[tick - last], gathered)
                incoming = jnp.where(is_last, cotangent[tick - last], current)
            flags = jnp.stack([bwd_active.astype(jnp.int32), place_bwd])
            back, *kept_bwd = backward_layer(flags, grad_rows, kept_fwd[1], w_up, w_down, kept_bwd)
            partial = jnp.where(bwd_active, back, partial) if tick < last + micro_count - 1 else back
        if tick == last + micro_count:
            hidden, partial = lax.optimization_barrier((kept_fwd[2], partial))
            final = lax.cond(
                is_last,
                lambda: jnp.dot(
                    hidden[: micro_count * total_rows], w_down, preferred_element_type=jnp.float32
                ).astype(jnp.bfloat16),
                lambda: jnp.zeros((micro_count * total_rows, features), jnp.bfloat16),
            )
            final = final.reshape(micro_count, tp_count, tok_rows, features).swapaxes(0, 1)
        sums = row_sums(partial)
        if tick + 1 == ticks:
            live_rows = micro_count * total_rows
            up_grads = block_grads(kept_fwd[0], kept_bwd[1], up_index[0], up_count[0], live_rows)
            sums, up_grads = lax.optimization_barrier((sums, up_grads))
        send = None
        if any_fwd and tick < last + micro_count - 1:
            layer_out = (current.astype(jnp.float32) + sums).astype(jnp.bfloat16)
            kept_output = put(kept_output, layer_out, place)
            send = layer_out
        if any_bwd:
            values, inv_rms, _ = normalize(take(kept_input, place_bwd, tok_rows), gain)
            scaled_grad = sums * gain.astype(jnp.float32)
            norm_term = inv_rms * scaled_grad - values * (inv_rms * inv_rms * inv_rms) * jnp.mean(
                scaled_grad * values, axis=-1, keepdims=True
            )
            grad_in = (incoming.astype(jnp.float32) + norm_term).astype(jnp.bfloat16)
            kept_ingrad = put(kept_ingrad, grad_in, place_bwd)
            send = grad_in if send is None else jnp.where(bwd_active, grad_in, send)
        if tick + 1 == ticks:
            break
        pairs = []
        for micro in range(micro_count):
            done = tick - micro
            if 0 <= done < rounds - 1:
                pairs.append((last - abs(last - done), last - abs(last - done - 1)))
        current = lax.ppermute(send, "section", pairs)
        if tick + 1 < micro_count:
            current = jnp.where(section_index == 0, inputs[tick + 1], current)
        next_fwd = tick + 1 <= last + micro_count - 1
        next_bwd = tick + 1 > last
        source = current
        if next_fwd:
            source = normalize(current, gain)[2]
            if next_bwd:
                source = jnp.where(section_index + micro_count > tick + 1, source, current)
        gathered = all_rows(source)

    down_grads = block_grads(kept_fwd[2], kept_bwd[0], down_index[0], down_count[0], live_rows)
    final, _ = lax.optimization_barrier((final, sums))
    final_sums = row_sums(final.reshape(live_rows, features))
    final_out = (kept_input[: micro_count * tok_rows].astype(jnp.float32) + final_sums).astype(jnp.bfloat16)
    outputs = jnp.where(is_last, final_out, kept_output[: micro_count * tok_rows])
    shape = (1, micro_count, tok_rows, features)
    return (
        outputs.reshape(shape),
        kept_ingrad[: micro_count * tok_rows].reshape(shape),
        up_grads[None],
        down_grads[None],
    )


def solution(mesh):
    return jax.shard_map(
        shards,
        mesh=mesh,
        in_specs=(
            P(None, "tp", None),
            P(None, "tp", None),
            P("section", None),
            P("section", "tp", None),
            P("section", "tp"),
            P("section", "tp"),
            P("section", "tp", None),
            P("section", "tp"),
            P("section", "tp"),
        ),
        out_specs=(
            P("section", None, "tp", None),
            P("section", None, "tp", None),
            P("section", "tp", None),
            P("section", "tp", None),
        ),
        check_vma=False,
    )
```

```python
import functools

import jax
import jax.numpy as jnp
from jax import lax
from jax.experimental import pallas as pl
from jax.experimental.pallas import tpu as pltpu
from jax.sharding import PartitionSpec as P

FF = 16384
BLOCK = 64
MICRO = 2
PAIR = 2 * BLOCK
HALF = BLOCK // 2
STRIP = 256
VMEM_BYTES = 58 * 2**20

NORM_EPSILON = 1e-05


def slot_step(slots):
    for size in (192, 128, 64, 32, 16):
        if slots % size == 0:
            return size
    return slots


def split_order(rows_split):
    first = lax.broadcasted_iota(jnp.int32, (STRIP, STRIP), 0)
    second = lax.broadcasted_iota(jnp.int32, (STRIP, STRIP), 1)
    split, natural = (first, second) if rows_split else (second, first)
    inner = split % BLOCK
    target = (split - inner) + 2 * (inner % HALF) + inner // HALF
    return (target == natural).astype(jnp.bfloat16)


def densify_kernel(slots, step_slots, index_ref, count_ref, block_ref, out_ref, held, packed, halves, order, place):
    step = pl.program_id(0)
    load_steps = slots // step_slots
    width = out_ref.shape[1]
    pairs = width // PAIR
    spare = place.shape[0] - 1

    @pl.when(step == 0)
    def _():
        order[...] = split_order(False)
        held[slots] = jnp.zeros((HALF, PAIR), jnp.bfloat16)

        @pl.loop(0, spare // 16)
        def _(group):
            for lane in range(16):
                place[group * 16 + lane] = slots

    @pl.when(step < load_steps)
    def _():
        first = step * step_slots
        for start in range(0, step_slots, 16):
            packed[start : start + 16] = block_ref[start : start + 16, :].reshape(16, HALF, PAIR)

        @pl.loop(0, step_slots // 16)
        def _(group):
            start = pl.multiple_of(group * 16, 16)
            for lane in range(16):
                slot = first + start + lane
                held[slot] = packed[start + lane]
                place[jnp.where(slot < count_ref[0], index_ref[slot], spare)] = slot

    @pl.when(step >= load_steps)
    def _():
        strip = step - load_steps
        lane = lax.broadcasted_iota(jnp.int32, (HALF, PAIR), 1)
        low = lane < BLOCK
        for row in range(STRIP // BLOCK):
            for col in range(pairs):
                pair = (strip * (STRIP // BLOCK) + row) * pairs + col
                left = held[place[2 * pair]]
                right = held[place[2 * pair + 1]]
                top = row * BLOCK
                lanes = slice(col * PAIR, (col + 1) * PAIR)
                crossed = pltpu.roll(jnp.where(low, right, left), BLOCK, 1)
                halves[top : top + HALF, lanes] = jnp.where(low, left, crossed)
                halves[top + HALF : top + BLOCK, lanes] = jnp.where(low, crossed, right)
        piece = min(width, 512)
        for start in range(0, width, piece):
            out_ref[:, start : start + piece] = jnp.dot(
                order[...], halves[:, start : start + piece], preferred_element_type=jnp.float32
            ).astype(jnp.bfloat16)


def densify(blocks, block_index, live_count, row_blocks, col_blocks):
    slots = blocks.shape[0]
    step_slots = slot_step(slots)
    load_steps = slots // step_slots
    width = min(col_blocks * BLOCK, 2048)
    across = col_blocks * BLOCK // width
    strips = row_blocks * BLOCK // STRIP
    if across > 1:
        piece_blocks = width // BLOCK
        row, col = block_index // col_blocks, block_index % col_blocks
        strip, row = row // 4, row % 4
        block_index = ((strip * across + col // piece_blocks) * 4 + row) * piece_blocks + col % piece_blocks

    def out_place(step, index, count):
        spot = jnp.maximum(step - load_steps, 0)
        return (spot // across, spot % across)

    return pl.pallas_call(
        functools.partial(densify_kernel, slots, step_slots),
        grid_spec=pltpu.PrefetchScalarGridSpec(
            num_scalar_prefetch=2,
            grid=(load_steps + strips * across,),
            in_specs=[
                pl.BlockSpec((step_slots, BLOCK * BLOCK), lambda step, index, count: (jnp.minimum(step, load_steps - 1), 0))
            ],
            out_specs=pl.BlockSpec((STRIP, width), out_place),
            scratch_shapes=[
                pltpu.VMEM((slots + 1, HALF, PAIR), jnp.bfloat16),
                pltpu.VMEM((step_slots, HALF, PAIR), jnp.bfloat16),
                pltpu.VMEM((STRIP, width), jnp.bfloat16),
                pltpu.VMEM((STRIP, STRIP), jnp.bfloat16),
                pltpu.SMEM((row_blocks * col_blocks + 1,), jnp.int32),
            ],
        ),
        out_shape=jax.ShapeDtypeStruct((row_blocks * BLOCK, col_blocks * BLOCK), jnp.bfloat16),
        compiler_params=pltpu.CompilerParams(
            dimension_semantics=("arbitrary",), vmem_limit_bytes=VMEM_BYTES
        ),
        name="densify",
    )(block_index, live_count, blocks)


def block_grads_kernel(strips, step_slots, index_ref, count_ref, left_ref, right_ref, out_ref, dense, order, packed):
    step = pl.program_id(0)
    width = right_ref.shape[1]
    pairs = width // PAIR

    @pl.when(step == 0)
    def _():
        order[...] = split_order(False)

    @pl.when(step < strips)
    def _():
        left = jnp.dot(left_ref[...], order[...], preferred_element_type=jnp.float32).astype(jnp.bfloat16)
        left = left.T
        piece = min(width, 512)
        for start in range(0, width, piece):
            product = jnp.dot(
                left, right_ref[:, start : start + piece], preferred_element_type=jnp.float32
            ).astype(jnp.bfloat16)
            for row in range(STRIP // BLOCK):
                for col in range(piece // PAIR):
                    pair = (step * (STRIP // BLOCK) + row) * pairs + start // PAIR + col
                    lanes = slice(col * PAIR, (col + 1) * PAIR)
                    dense[2 * pair] = product[row * BLOCK : row * BLOCK + HALF, lanes]
                    dense[2 * pair + 1] = product[row * BLOCK + HALF : (row + 1) * BLOCK, lanes]

    @pl.when(step >= strips)
    def _():
        first = (step - strips) * step_slots
        lane = lax.broadcasted_iota(jnp.int32, (HALF, PAIR), 1)
        low = lane < BLOCK

        @pl.loop(0, step_slots // 16)
        def _(group):
            start = pl.multiple_of(group * 16, 16)
            for one in range(16):
                slot = first + start + one
                spot = index_ref[slot]
                keep = dense[spot]
                other = pltpu.roll(dense[spot ^ 1], BLOCK, 1)
                picked = jnp.where(low == (spot % 2 == 0), keep, other)
                packed[one] = jnp.where(slot < count_ref[0], picked, jnp.zeros_like(picked))
            out_ref[pl.ds(start, 16), :] = packed[...].reshape(16, BLOCK * BLOCK)


def block_grads(left, right, block_index, live_count, tokens):
    rows = left.shape[1]
    cols = right.shape[1]
    slots = block_index.shape[0]
    step_slots = slot_step(slots)
    strips = rows // STRIP
    return pl.pallas_call(
        functools.partial(block_grads_kernel, strips, step_slots),
        grid_spec=pltpu.PrefetchScalarGridSpec(
            num_scalar_prefetch=2,
            grid=(strips + slots // step_slots,),
            in_specs=[
                pl.BlockSpec((tokens, STRIP), lambda step, index, count: (0, jnp.minimum(step, strips - 1))),
                pl.BlockSpec((tokens, cols), lambda step, index, count: (0, 0)),
            ],
            out_specs=pl.BlockSpec(
                (step_slots, BLOCK * BLOCK), lambda step, index, count: (jnp.maximum(step - strips, 0), 0)
            ),
            scratch_shapes=[
                pltpu.VMEM((rows * cols // (HALF * PAIR), HALF, PAIR), jnp.bfloat16),
                pltpu.VMEM((STRIP, STRIP), jnp.bfloat16),
                pltpu.VMEM((16, HALF, PAIR), jnp.bfloat16),
            ],
        ),
        out_shape=jax.ShapeDtypeStruct((slots, BLOCK * BLOCK), jnp.bfloat16),
        compiler_params=pltpu.CompilerParams(
            dimension_semantics=("arbitrary",), vmem_limit_bytes=VMEM_BYTES
        ),
        cost_estimate=pl.CostEstimate(
            flops=6 * tokens * rows * cols, bytes_accessed=6 * rows * cols, transcendentals=0
        ),
        name="block_grads",
    )(block_index, live_count, left, right)


def normalize(activ_rows, gain):
    values = activ_rows.astype(jnp.float32)
    inv_rms = lax.rsqrt(jnp.mean(values * values, axis=-1, keepdims=True) + NORM_EPSILON)
    return (values, inv_rms, (values * inv_rms * gain.astype(jnp.float32)).astype(jnp.bfloat16))


def all_rows(local_rows):
    return lax.all_gather(local_rows, "tp", axis=0, tiled=True)


def row_sums(partial):
    return lax.psum_scatter(partial, "tp", scatter_dimension=0, tiled=True).astype(jnp.float32)


def layer_params():
    return pltpu.CompilerParams(dimension_semantics=("arbitrary",), vmem_limit_bytes=VMEM_BYTES)


def forward_kernel(up_steps, flags, rows_ref, up_ref, down_ref, *rest):
    part_ref, kept_rows_ref, kept_up_ref, kept_hidden_ref, total, turned = rest[-6:]
    step = pl.program_id(0)
    depth = up_ref.shape[0]
    up_active, down_active = flags[0] > 0, flags[1] > 0
    first_axes = (((0,), (0,)), ((), ()))

    @pl.when(up_active & (step < up_steps))
    def _():
        @pl.when(step == 0)
        def _():
            kept_rows_ref[...] = rows_ref[...]
            total[...] = jnp.zeros_like(total)

        rows = rows_ref[:, pl.ds(pl.multiple_of(step * depth, depth), depth)]
        total[...] += lax.dot_general(up_ref[...], rows.T, first_axes, preferred_element_type=jnp.float32)

        @pl.when(step == up_steps - 1)
        def _():
            proj = total[...]
            kept_up_ref[...] = proj
            hidden = (proj * (1.0 / (1.0 + jnp.exp(-proj)))).astype(jnp.bfloat16)
            turned[...] = hidden
            kept_hidden_ref[...] = hidden.T

    @pl.when(step >= up_steps)
    def _():
        @pl.when(down_active)
        def _():
            part = lax.dot_general(down_ref[...], turned[...], first_axes, preferred_element_type=jnp.float32)
            part_ref[...] = part.astype(jnp.bfloat16).T

        @pl.when(jnp.logical_not(down_active))
        def _():
            part_ref[...] = jnp.zeros_like(part_ref)


def forward_layer(flags, rows, w_up, w_down, kept):
    tokens, features = rows.shape
    units = w_up.shape[1]
    depth = 1024
    up_steps = down_steps = features // depth
    last_up = up_steps - 1
    any_space = [pl.BlockSpec(memory_space=pl.ANY)] * len(kept)
    places = (MICRO + 1) * tokens
    return pl.pallas_call(
        functools.partial(forward_kernel, up_steps),
        grid_spec=pltpu.PrefetchScalarGridSpec(
            num_scalar_prefetch=1,
            grid=(up_steps + down_steps,),
            in_specs=[
                pl.BlockSpec((tokens, features), lambda step, flags: (0, 0)),
                pl.BlockSpec((depth, units), lambda step, flags: (flags[0] * jnp.minimum(step, last_up), 0)),
                pl.BlockSpec((units, depth), lambda step, flags: (0, flags[1] * jnp.maximum(step - up_steps, 0))),
            ]
            + any_space,
            out_specs=[
                pl.BlockSpec((tokens, depth), lambda step, flags: (0, jnp.maximum(step - up_steps, 0))),
                pl.BlockSpec((tokens, features), lambda step, flags: (flags[2], 0)),
                pl.BlockSpec((units, tokens), lambda step, flags: (flags[2], 0)),
                pl.BlockSpec((tokens, units), lambda step, flags: (flags[2], 0)),
            ],
            scratch_shapes=[pltpu.VMEM((units, tokens), jnp.float32), pltpu.VMEM((units, tokens), jnp.bfloat16)],
        ),
        out_shape=[
            jax.ShapeDtypeStruct((tokens, features), jnp.bfloat16),
            jax.ShapeDtypeStruct((places, features), jnp.bfloat16),
            jax.ShapeDtypeStruct(((MICRO + 1) * units, tokens), jnp.float32),
            jax.ShapeDtypeStruct((places, units), jnp.bfloat16),
        ],
        input_output_aliases={4 + number: 1 + number for number in range(len(kept))},
        compiler_params=layer_params(),
        cost_estimate=pl.CostEstimate(
            flops=4 * tokens * features * units, bytes_accessed=4 * features * units, transcendentals=0
        ),
        name="forward_layer",
    )(flags, rows, w_up, w_down, *kept)


def backward_kernel(down_steps, flags, grad_ref, proj_ref, down_ref, up_ref, *rest):
    part_ref, kept_grad_ref, kept_upgrad_ref, total, turned = rest[-5:]
    step = pl.program_id(0)
    depth = down_ref.shape[1]
    active = flags[0] > 0

    @pl.when(active & (step < down_steps))
    def _():
        @pl.when(step == 0)
        def _():
            kept_grad_ref[...] = grad_ref[...]
            total[...] = jnp.zeros_like(total)

        grad = grad_ref[:, pl.ds(pl.multiple_of(step * depth, depth), depth)]
        total[...] += jnp.dot(down_ref[...], grad.T, preferred_element_type=jnp.float32)

        @pl.when(step == down_steps - 1)
        def _():
            proj = proj_ref[...]
            gate = 1.0 / (1.0 + jnp.exp(-proj))
            up_grad = (total[...] * gate * (1.0 + proj * (1.0 - gate))).astype(jnp.bfloat16)
            turned[...] = up_grad
            kept_upgrad_ref[...] = up_grad.T

    @pl.when(step >= down_steps)
    def _():
        @pl.when(active)
        def _():
            part = jnp.dot(up_ref[...], turned[...], preferred_element_type=jnp.float32)
            part_ref[...] = part.astype(jnp.bfloat16).T

        @pl.when(jnp.logical_not(active))
        def _():
            part_ref[...] = jnp.zeros_like(part_ref)


def backward_layer(flags, grad, kept_up, w_up, w_down, kept):
    tokens, features = grad.shape
    units = w_up.shape[1]
    depth = 1024
    down_steps = up_steps = features // depth
    last_down = down_steps - 1
    any_space = [pl.BlockSpec(memory_space=pl.ANY)] * len(kept)
    places = (MICRO + 1) * tokens
    return pl.pallas_call(
        functools.partial(backward_kernel, down_steps),
        grid_spec=pltpu.PrefetchScalarGridSpec(
            num_scalar_prefetch=1,
            grid=(down_steps + up_steps,),
            in_specs=[
                pl.BlockSpec((tokens, features), lambda step, flags: (0, 0)),
                pl.BlockSpec((units, tokens), lambda step, flags: (flags[1], 0)),
                pl.BlockSpec((units, depth), lambda step, flags: (0, flags[0] * jnp.minimum(step, last_down))),
                pl.BlockSpec((depth, units), lambda step, flags: (flags[0] * jnp.maximum(step - down_steps, 0), 0)),
            ]
            + any_space,
            out_specs=[
                pl.BlockSpec((tokens, depth), lambda step, flags: (0, jnp.maximum(step - down_steps, 0))),
                pl.BlockSpec((tokens, features), lambda step, flags: (flags[1], 0)),
                pl.BlockSpec((tokens, units), lambda step, flags: (flags[1], 0)),
            ],
            scratch_shapes=[pltpu.VMEM((units, tokens), jnp.float32), pltpu.VMEM((units, tokens), jnp.bfloat16)],
        ),
        out_shape=[
            jax.ShapeDtypeStruct((tokens, features), jnp.bfloat16),
            jax.ShapeDtypeStruct((places, features), jnp.bfloat16),
            jax.ShapeDtypeStruct((places, units), jnp.bfloat16),
        ],
        input_output_aliases={5 + number: 1 + number for number in range(len(kept))},
        compiler_params=layer_params(),
        cost_estimate=pl.CostEstimate(
            flops=4 * tokens * features * units, bytes_accessed=4 * features * units, transcendentals=0
        ),
        name="backward_layer",
    )(flags, grad, kept_up, w_down, w_up, *kept)


def put(buffer, value, place):
    return lax.dynamic_update_slice_in_dim(buffer, value, place * value.shape[0], 0)


def take(buffer, place, count):
    return lax.dynamic_slice_in_dim(buffer, place * count, count, 0)


def shards(
    inputs, cotangent, gains, up_blocks, up_index, up_count, down_blocks, down_index, down_count
):
    micro_count, tok_rows, features = inputs.shape
    section_index = lax.axis_index("section")
    section_count = lax.axis_size("section")
    last = section_count - 1
    tp_count = lax.axis_size("tp")
    group_width = FF // tp_count
    total_rows = tok_rows * tp_count
    row_blocks = features // BLOCK
    group_blocks = group_width // BLOCK
    gain = gains[0]
    first_rows = all_rows(normalize(inputs[0], gain)[2])
    cot_rows = [all_rows(cotangent[micro]) for micro in range(micro_count)]
    first_rows, cot_rows = lax.optimization_barrier((first_rows, cot_rows))
    w_up = densify(up_blocks[0], up_index[0], up_count[0], row_blocks, group_blocks)
    w_down = densify(down_blocks[0], down_index[0], down_count[0], group_blocks, row_blocks)

    places = micro_count + 1
    kept_fwd, kept_bwd = [], []
    kept_input = jnp.zeros((places * tok_rows, features), jnp.bfloat16)
    kept_output = jnp.zeros((places * tok_rows, features), jnp.bfloat16)
    kept_ingrad = jnp.zeros((places * tok_rows, features), jnp.bfloat16)
    is_last = section_index == last

    rounds = 2 * section_count - 1
    ticks = rounds + micro_count - 1
    current = inputs[0]
    gathered = first_rows
    for tick in range(ticks):
        micro_fwd = tick - section_index
        micro_bwd = tick - (2 * last - section_index)
        fwd_active = (micro_fwd >= 0) & (micro_fwd < micro_count)
        bwd_active = (micro_bwd >= 0) & (micro_bwd < micro_count)
        any_fwd = tick <= last + micro_count - 1
        any_bwd = tick >= last
        partial = None
        if any_fwd:
            place = jnp.where(fwd_active, micro_fwd, micro_count)
            down_active = fwd_active & jnp.logical_not(is_last)
            flags = jnp.stack([fwd_active.astype(jnp.int32), down_active.astype(jnp.int32), place])
            partial, *kept_fwd = forward_layer(flags, gathered, w_up, w_down, kept_fwd)
            kept_input = put(kept_input, current, place)
        if any_bwd:
            place_bwd = jnp.where(bwd_active, micro_bwd, micro_count)
            grad_rows, incoming = gathered, current
            if tick == last:
                grad_rows, incoming = cot_rows[0], cotangent[0]
            elif tick - last < micro_count:
                grad_rows = jnp.where(is_last, cot_rows[tick - last], gathered)
                incoming = jnp.where(is_last, cotangent[tick - last], current)
            flags = jnp.stack([bwd_active.astype(jnp.int32), place_bwd])
            back, *kept_bwd = backward_layer(flags, grad_rows, kept_fwd[1], w_up, w_down, kept_bwd)
            partial = jnp.where(bwd_active, back, partial) if tick < last + micro_count - 1 else back
        if tick == last + micro_count:
            hidden, partial = lax.optimization_barrier((kept_fwd[2], partial))
            final = lax.cond(
                is_last,
                lambda: jnp.dot(
                    hidden[: micro_count * total_rows], w_down, preferred_element_type=jnp.float32
                ).astype(jnp.bfloat16),
                lambda: jnp.zeros((micro_count * total_rows, features), jnp.bfloat16),
            )
            final = final.reshape(micro_count, tp_count, tok_rows, features).swapaxes(0, 1)
        if tick > last + micro_count:
            final, partial = lax.optimization_barrier((final, partial))
        sums = row_sums(partial)
        if tick + 1 == ticks:
            live_rows = micro_count * total_rows
            up_grads = block_grads(kept_fwd[0], kept_bwd[1], up_index[0], up_count[0], live_rows)
            final, last_sums = lax.optimization_barrier((final, sums))
            sums, up_grads = lax.optimization_barrier((last_sums, up_grads))
        send = None
        if any_fwd and tick < last + micro_count - 1:
            layer_out = (current.astype(jnp.float32) + sums).astype(jnp.bfloat16)
            kept_output = put(kept_output, layer_out, place)
            send = layer_out
        if any_bwd:
            values, inv_rms, _ = normalize(take(kept_input, place_bwd, tok_rows), gain)
            scaled_grad = sums * gain.astype(jnp.float32)
            norm_term = inv_rms * scaled_grad - values * (inv_rms * inv_rms * inv_rms) * jnp.mean(
                scaled_grad * values, axis=-1, keepdims=True
            )
            grad_in = (incoming.astype(jnp.float32) + norm_term).astype(jnp.bfloat16)
            kept_ingrad = put(kept_ingrad, grad_in, place_bwd)
            send = grad_in if send is None else jnp.where(bwd_active, grad_in, send)
        if tick + 1 == ticks:
            break
        pairs = []
        for micro in range(micro_count):
            done = tick - micro
            if 0 <= done < rounds - 1:
                pairs.append((last - abs(last - done), last - abs(last - done - 1)))
        current = lax.ppermute(send, "section", pairs)
        if tick + 1 < micro_count:
            current = jnp.where(section_index == 0, inputs[tick + 1], current)
        next_fwd = tick + 1 <= last + micro_count - 1
        next_bwd = tick + 1 > last
        source = current
        if next_fwd:
            source = normalize(current, gain)[2]
            if next_bwd:
                source = jnp.where(section_index + micro_count > tick + 1, source, current)
        gathered = all_rows(source)

    down_grads = block_grads(kept_fwd[2], kept_bwd[0], down_index[0], down_count[0], live_rows)
    final_sums = row_sums(final.reshape(live_rows, features))
    final_out = (kept_input[: micro_count * tok_rows].astype(jnp.float32) + final_sums).astype(jnp.bfloat16)
    outputs = jnp.where(is_last, final_out, kept_output[: micro_count * tok_rows])
    shape = (1, micro_count, tok_rows, features)
    return (
        outputs.reshape(shape),
        kept_ingrad[: micro_count * tok_rows].reshape(shape),
        up_grads[None],
        down_grads[None],
    )


def solution(mesh):
    return jax.shard_map(
        shards,
        mesh=mesh,
        in_specs=(
            P(None, "tp", None),
            P(None, "tp", None),
            P("section", None),
            P("section", "tp", None),
            P("section", "tp"),
            P("section", "tp"),
            P("section", "tp", None),
            P("section", "tp"),
            P("section", "tp"),
        ),
        out_specs=(
            P("section", None, "tp", None),
            P("section", None, "tp", None),
            P("section", "tp", None),
            P("section", "tp", None),
        ),
        check_vma=False,
    )
```

```python
import functools

import jax
import jax.numpy as jnp
from jax import lax
from jax.experimental import pallas as pl
from jax.experimental.pallas import tpu as pltpu
from jax.sharding import PartitionSpec as P

FF = 16384
BLOCK = 64
MICRO = 2
STREAMS = 4
PAIR = 2 * BLOCK
HALF = BLOCK // 2
STRIP = 256
VMEM_BYTES = 58 * 2**20

NORM_EPSILON = 1e-05


def slot_step(slots):
    for size in (192, 128, 64, 32, 16):
        if slots % size == 0:
            return size
    return slots


def split_order(rows_split):
    first = lax.broadcasted_iota(jnp.int32, (STRIP, STRIP), 0)
    second = lax.broadcasted_iota(jnp.int32, (STRIP, STRIP), 1)
    split, natural = (first, second) if rows_split else (second, first)
    inner = split % BLOCK
    target = (split - inner) + 2 * (inner % HALF) + inner // HALF
    return (target == natural).astype(jnp.bfloat16)


def densify_kernel(slots, step_slots, index_ref, count_ref, block_ref, out_ref, held, packed, place):
    step = pl.program_id(0)
    load_steps = slots // step_slots
    width = out_ref.shape[1]
    pairs = width // PAIR
    spare = place.shape[0] - 1

    @pl.when(step == 0)
    def _():
        held[slots] = jnp.zeros((HALF, PAIR), jnp.bfloat16)

        @pl.loop(0, spare // 16)
        def _(group):
            for lane in range(16):
                place[group * 16 + lane] = slots

    @pl.when(step < load_steps)
    def _():
        first = step * step_slots
        for start in range(0, step_slots, 16):
            packed[start : start + 16] = block_ref[start : start + 16, :].reshape(16, HALF, PAIR)

        @pl.loop(0, step_slots // 16)
        def _(group):
            start = pl.multiple_of(group * 16, 16)
            for lane in range(16):
                slot = first + start + lane
                held[slot] = packed[start + lane]
                place[jnp.where(slot < count_ref[0], index_ref[slot], spare)] = slot

    @pl.when(step >= load_steps)
    def _():
        strip = step - load_steps
        lane = lax.broadcasted_iota(jnp.int32, (HALF, PAIR), 1)
        low = lane < BLOCK
        for row in range(STRIP // BLOCK):
            for col in range(pairs):
                pair = (strip * (STRIP // BLOCK) + row) * pairs + col
                left = held[place[2 * pair]]
                right = held[place[2 * pair + 1]]
                top = row * BLOCK
                lanes = slice(col * PAIR, (col + 1) * PAIR)
                crossed = pltpu.roll(jnp.where(low, right, left), BLOCK, 1)
                out_ref[top : top + HALF, lanes] = jnp.where(low, left, crossed)
                out_ref[top + HALF : top + BLOCK, lanes] = jnp.where(low, crossed, right)


def densify(blocks, block_index, live_count, row_blocks, col_blocks):
    slots = blocks.shape[0]
    step_slots = slot_step(slots)
    load_steps = slots // step_slots
    width = min(col_blocks * BLOCK, 2048)
    across = col_blocks * BLOCK // width
    strips = row_blocks * BLOCK // STRIP
    if across > 1:
        piece_blocks = width // BLOCK
        row, col = block_index // col_blocks, block_index % col_blocks
        strip, row = row // 4, row % 4
        block_index = ((strip * across + col // piece_blocks) * 4 + row) * piece_blocks + col % piece_blocks

    def out_place(step, index, count):
        spot = jnp.maximum(step - load_steps, 0)
        return (spot // across, spot % across)

    return pl.pallas_call(
        functools.partial(densify_kernel, slots, step_slots),
        grid_spec=pltpu.PrefetchScalarGridSpec(
            num_scalar_prefetch=2,
            grid=(load_steps + strips * across,),
            in_specs=[
                pl.BlockSpec((step_slots, BLOCK * BLOCK), lambda step, index, count: (jnp.minimum(step, load_steps - 1), 0))
            ],
            out_specs=pl.BlockSpec((STRIP, width), out_place),
            scratch_shapes=[
                pltpu.VMEM((slots + 1, HALF, PAIR), jnp.bfloat16),
                pltpu.VMEM((step_slots, HALF, PAIR), jnp.bfloat16),
                pltpu.SMEM((row_blocks * col_blocks + 1,), jnp.int32),
            ],
        ),
        out_shape=jax.ShapeDtypeStruct((row_blocks * BLOCK, col_blocks * BLOCK), jnp.bfloat16),
        compiler_params=pltpu.CompilerParams(
            dimension_semantics=("arbitrary",), vmem_limit_bytes=VMEM_BYTES
        ),
        name="densify",
    )(block_index, live_count, blocks)


def block_grads_kernel(strips, step_slots, reorder, index_ref, count_ref, left_ref, right_ref, out_ref, dense, order, packed):
    step = pl.program_id(0)
    width = right_ref.shape[1]
    pairs = width // PAIR

    @pl.when(step == 0)
    def _():
        order[...] = split_order(False)

    @pl.when(step < strips)
    def _():
        left = left_ref[...]
        if reorder:
            left = jnp.dot(left, order[...], preferred_element_type=jnp.float32).astype(jnp.bfloat16)
        left = left.T
        piece = min(width, 512)
        for start in range(0, width, piece):
            product = jnp.dot(
                left, right_ref[:, start : start + piece], preferred_element_type=jnp.float32
            ).astype(jnp.bfloat16)
            for row in range(STRIP // BLOCK):
                for col in range(piece // PAIR):
                    pair = (step * (STRIP // BLOCK) + row) * pairs + start // PAIR + col
                    lanes = slice(col * PAIR, (col + 1) * PAIR)
                    dense[2 * pair] = product[row * BLOCK : row * BLOCK + HALF, lanes]
                    dense[2 * pair + 1] = product[row * BLOCK + HALF : (row + 1) * BLOCK, lanes]

    @pl.when(step >= strips)
    def _():
        first = (step - strips) * step_slots
        lane = lax.broadcasted_iota(jnp.int32, (HALF, PAIR), 1)
        low = lane < BLOCK

        @pl.loop(0, step_slots // 16)
        def _(group):
            start = pl.multiple_of(group * 16, 16)
            for one in range(16):
                slot = first + start + one
                spot = index_ref[slot]
                keep = dense[spot]
                other = pltpu.roll(dense[spot ^ 1], BLOCK, 1)
                picked = jnp.where(low == (spot % 2 == 0), keep, other)
                packed[one] = jnp.where(slot < count_ref[0], picked, jnp.zeros_like(picked))
            out_ref[pl.ds(start, 16), :] = packed[...].reshape(16, BLOCK * BLOCK)


def block_grads(left, right, block_index, live_count, tokens, reorder):
    rows = left.shape[1]
    cols = right.shape[1]
    slots = block_index.shape[0]
    step_slots = slot_step(slots)
    strips = rows // STRIP
    return pl.pallas_call(
        functools.partial(block_grads_kernel, strips, step_slots, reorder),
        grid_spec=pltpu.PrefetchScalarGridSpec(
            num_scalar_prefetch=2,
            grid=(strips + slots // step_slots,),
            in_specs=[
                pl.BlockSpec((tokens, STRIP), lambda step, index, count: (0, jnp.minimum(step, strips - 1))),
                pl.BlockSpec((tokens, cols), lambda step, index, count: (0, 0)),
            ],
            out_specs=pl.BlockSpec(
                (step_slots, BLOCK * BLOCK), lambda step, index, count: (jnp.maximum(step - strips, 0), 0)
            ),
            scratch_shapes=[
                pltpu.VMEM((rows * cols // (HALF * PAIR), HALF, PAIR), jnp.bfloat16),
                pltpu.VMEM((STRIP, STRIP), jnp.bfloat16),
                pltpu.VMEM((16, HALF, PAIR), jnp.bfloat16),
            ],
        ),
        out_shape=jax.ShapeDtypeStruct((slots, BLOCK * BLOCK), jnp.bfloat16),
        compiler_params=pltpu.CompilerParams(
            dimension_semantics=("arbitrary",), vmem_limit_bytes=VMEM_BYTES
        ),
        cost_estimate=pl.CostEstimate(
            flops=6 * tokens * rows * cols, bytes_accessed=6 * rows * cols, transcendentals=0
        ),
        name="block_grads",
    )(block_index, live_count, left, right)


def normalize(activ_rows, gain):
    values = activ_rows.astype(jnp.float32)
    inv_rms = lax.rsqrt(jnp.mean(values * values, axis=-1, keepdims=True) + NORM_EPSILON)
    return (values, inv_rms, (values * inv_rms * gain.astype(jnp.float32)).astype(jnp.bfloat16))


def same_core():
    count = lax.axis_size("tp")
    return [list(range(core, count, 2)) for core in range(2)]


def other_core(array):
    return lax.ppermute(array, "tp", [(index, index ^ 1) for index in range(lax.axis_size("tp"))])


def own_rows(local_rows):
    return lax.all_gather(local_rows, "tp", axis=0, tiled=True, axis_index_groups=same_core())


def all_rows(local_rows):
    own = own_rows(local_rows)
    return own, other_core(own)


def row_sums(part_own, part_other):
    chip = (part_own.astype(jnp.float32) + other_core(part_other).astype(jnp.float32)).astype(jnp.bfloat16)
    return lax.psum_scatter(
        chip, "tp", scatter_dimension=0, tiled=True, axis_index_groups=same_core()
    ).astype(jnp.float32)


def reordered(values, order, dtype=jnp.bfloat16, precision=None):
    groups = [
        jnp.dot(
            values[:, start : start + STRIP], order, preferred_element_type=jnp.float32, precision=precision
        ).astype(dtype)
        for start in range(0, values.shape[1], STRIP)
    ]
    return groups[0] if len(groups) == 1 else jnp.concatenate(groups, axis=1)


def times_turned(left, refs):
    transposed = (((1,), (1,)), ((), ()))
    width = refs[0].shape[1]
    total = None
    for number, ref in enumerate(refs):
        part = lax.dot_general(
            left[:, number * width : (number + 1) * width], ref[...], transposed, preferred_element_type=jnp.float32
        )
        total = part if total is None else total + part
    return total


def forward_kernel(up_steps, turn, flags, own_ref, other_ref, *rest):
    ups, downs, rest = rest[:STREAMS], rest[STREAMS : 2 * STREAMS], rest[2 * STREAMS :]
    outs = rest[len(rest) - 8 - turn :]
    part_own, part_other, kept_rows, kept_up, kept_hidden = outs[:5]
    total, order, back = outs[-3:]
    step = pl.program_id(0)
    depth = ups[0].shape[0]
    half = own_ref.shape[0]
    up_active, down_active, turn_active = flags[0] > 0, flags[1] > 0, flags[3] > 0

    @pl.when(up_active & (step < up_steps))
    def _():
        @pl.when(step == 0)
        def _():
            kept_rows[:half, :] = own_ref[...]
            kept_rows[half:, :] = other_ref[...]
            total[...] = jnp.zeros_like(total)
            order[...] = split_order(False)
            back[...] = split_order(True)

        rows = reordered(kept_rows[:, pl.ds(pl.multiple_of(step * depth, depth), depth)], order[...])
        width = ups[0].shape[1]
        for number, ref in enumerate(ups):
            lanes = slice(number * width, (number + 1) * width)
            total[:, lanes] += jnp.dot(rows, ref[...], preferred_element_type=jnp.float32)

        @pl.when(step == up_steps - 1)
        def _():
            proj = total[...]
            kept_up[...] = proj
            gate = 1.0 / (1.0 + jnp.exp(-proj))
            kept_hidden[...] = reordered((proj * gate).astype(jnp.bfloat16), order[...])
            if turn:
                pre_ref, kept_upgrad = rest[0], outs[5]
                kept_upgrad[...] = (pre_ref[...] * gate * (1.0 + proj * (1.0 - gate))).astype(jnp.bfloat16)

    @pl.when(step >= up_steps)
    def _():
        @pl.when(down_active)
        def _():
            width = downs[0].shape[1]
            hidden = kept_hidden[...]
            for number, ref in enumerate(downs):
                part = jnp.dot(hidden, ref[...], preferred_element_type=jnp.float32).astype(jnp.bfloat16)
                lanes = slice(number * width, (number + 1) * width)
                part_own[:, lanes] = part[:half]
                part_other[:, lanes] = part[half:]

        if turn:

            @pl.when(turn_active)
            def _():
                part = reordered(times_turned(outs[5][...], ups).astype(jnp.bfloat16), back[...])
                part_own[...] = part[:half]
                part_other[...] = part[half:]

        @pl.when(jnp.logical_not(down_active | turn_active))
        def _():
            part_own[...] = jnp.zeros_like(part_own)
            part_other[...] = jnp.zeros_like(part_other)


def layer_cost(tokens, features, units):
    return pl.CostEstimate(flops=4 * tokens * features * units, bytes_accessed=4 * features * units, transcendentals=0)


def forward_layer(flags, rows, w_up, w_down, kept, pre=None):
    turn = pre is not None
    half, features = rows[0].shape
    tokens = 2 * half
    units = w_up.shape[1]
    depth = 1024
    up_steps = down_steps = features // depth
    last_up = up_steps - 1
    up_width, down_width = units // STREAMS, depth // STREAMS
    any_space = [pl.BlockSpec(memory_space=pl.ANY)] * len(kept)

    def up_place(number):
        def place(step, flags):
            plain = flags[0] * jnp.minimum(step, last_up)
            return (jnp.where(flags[3] > 0, step % up_steps, plain) if turn else plain, number)

        return place

    def down_place(number):
        return lambda step, flags: (0, STREAMS * flags[1] * jnp.maximum(step - up_steps, 0) + number)

    def part_place(step, flags):
        return (0, jnp.maximum(step - up_steps, 0))

    def kept_place(step, flags):
        return (flags[2], 0)

    pre_spec = [pl.BlockSpec((tokens, units), lambda step, flags: (jnp.minimum(flags[2], MICRO - 1), 0))] * turn
    inputs = [flags, *rows, *[w_up] * STREAMS, *[w_down] * STREAMS, *[pre] * turn]
    places = (MICRO + 1) * tokens
    return pl.pallas_call(
        functools.partial(forward_kernel, up_steps, turn),
        grid_spec=pltpu.PrefetchScalarGridSpec(
            num_scalar_prefetch=1,
            grid=(up_steps + down_steps,),
            in_specs=[pl.BlockSpec((half, features), lambda step, flags: (0, 0))] * 2
            + [pl.BlockSpec((depth, up_width), up_place(number)) for number in range(STREAMS)]
            + [pl.BlockSpec((units, down_width), down_place(number)) for number in range(STREAMS)]
            + pre_spec
            + any_space,
            out_specs=[pl.BlockSpec((half, depth), part_place)] * 2
            + [
                pl.BlockSpec((tokens, features), kept_place),
                pl.BlockSpec((tokens, units), kept_place),
                pl.BlockSpec((tokens, units), kept_place),
            ]
            + [pl.BlockSpec((tokens, units), kept_place)] * turn,
            scratch_shapes=[
                pltpu.VMEM((tokens, units), jnp.float32),
                pltpu.VMEM((STRIP, STRIP), jnp.bfloat16),
                pltpu.VMEM((STRIP, STRIP), jnp.bfloat16),
            ],
        ),
        out_shape=[jax.ShapeDtypeStruct((half, features), jnp.bfloat16)] * 2
        + [
            jax.ShapeDtypeStruct((places, features), jnp.bfloat16),
            jax.ShapeDtypeStruct((places, units), jnp.float32),
            jax.ShapeDtypeStruct((places, units), jnp.bfloat16),
        ]
        + [jax.ShapeDtypeStruct((places, units), jnp.bfloat16)] * turn,
        input_output_aliases={len(inputs) + number: 2 + number for number in range(len(kept))},
        compiler_params=pltpu.CompilerParams(dimension_semantics=("arbitrary",), vmem_limit_bytes=VMEM_BYTES),
        cost_estimate=layer_cost(tokens, features, units),
        name="forward_layer",
    )(*inputs, *kept)


def backward_kernel(down_steps, flags, own_ref, other_ref, proj_ref, *rest):
    downs, ups = rest[:STREAMS], rest[STREAMS : 2 * STREAMS]
    part_own, part_other, kept_grad, kept_upgrad, back = rest[-5:]
    step = pl.program_id(0)
    width = downs[0].shape[0]
    half = own_ref.shape[0]
    active = flags[0] > 0

    @pl.when(active & (step < down_steps))
    def _():
        @pl.when(step == 0)
        def _():
            kept_grad[:half, :] = own_ref[...]
            kept_grad[half:, :] = other_ref[...]
            back[...] = split_order(True)

        act_grad = reordered(
            times_turned(kept_grad, downs), back[...].astype(jnp.float32), jnp.float32, lax.Precision.HIGHEST
        )
        lanes = pl.ds(pl.multiple_of(step * width, width), width)
        proj = proj_ref[:, lanes]
        gate = 1.0 / (1.0 + jnp.exp(-proj))
        kept_upgrad[:, lanes] = (act_grad * gate * (1.0 + proj * (1.0 - gate))).astype(jnp.bfloat16)

    @pl.when(step >= down_steps)
    def _():
        @pl.when(active)
        def _():
            part = reordered(times_turned(kept_upgrad[...], ups).astype(jnp.bfloat16), back[...])
            part_own[...] = part[:half]
            part_other[...] = part[half:]

        @pl.when(jnp.logical_not(active))
        def _():
            part_own[...] = jnp.zeros_like(part_own)
            part_other[...] = jnp.zeros_like(part_other)


def backward_layer(flags, grad, kept_up, w_up, w_down, kept):
    half, features = grad[0].shape
    tokens = 2 * half
    units = w_up.shape[1]
    width, depth = min(units, STRIP), 1024
    down_steps, up_steps = units // width, features // depth
    last_down = down_steps - 1
    any_space = [pl.BlockSpec(memory_space=pl.ANY)] * len(kept)

    def down_place(number):
        return lambda step, flags: (flags[0] * jnp.minimum(step, last_down), number)

    def up_place(number):
        return lambda step, flags: (flags[0] * jnp.maximum(step - down_steps, 0), number)

    def part_place(step, flags):
        return (0, jnp.maximum(step - down_steps, 0))

    def kept_place(step, flags):
        return (flags[1], 0)

    inputs = [flags, *grad, kept_up, *[w_down] * STREAMS, *[w_up] * STREAMS]
    places = (MICRO + 1) * tokens
    return pl.pallas_call(
        functools.partial(backward_kernel, down_steps),
        grid_spec=pltpu.PrefetchScalarGridSpec(
            num_scalar_prefetch=1,
            grid=(down_steps + up_steps,),
            in_specs=[pl.BlockSpec((half, features), lambda step, flags: (0, 0))] * 2
            + [pl.BlockSpec((tokens, units), kept_place)]
            + [pl.BlockSpec((width, features // STREAMS), down_place(number)) for number in range(STREAMS)]
            + [pl.BlockSpec((depth, units // STREAMS), up_place(number)) for number in range(STREAMS)]
            + any_space,
            out_specs=[pl.BlockSpec((half, depth), part_place)] * 2
            + [pl.BlockSpec((tokens, features), kept_place), pl.BlockSpec((tokens, units), kept_place)],
            scratch_shapes=[pltpu.VMEM((STRIP, STRIP), jnp.bfloat16)],
        ),
        out_shape=[jax.ShapeDtypeStruct((half, features), jnp.bfloat16)] * 2
        + [
            jax.ShapeDtypeStruct((places, features), jnp.bfloat16),
            jax.ShapeDtypeStruct((places, units), jnp.bfloat16),
        ],
        input_output_aliases={len(inputs) + number: 2 + number for number in range(len(kept))},
        compiler_params=pltpu.CompilerParams(dimension_semantics=("arbitrary",), vmem_limit_bytes=VMEM_BYTES),
        cost_estimate=layer_cost(tokens, features, units),
        name="backward_layer",
    )(*inputs, *kept)


def natural_columns(values):
    rows, cols = values.shape
    return values.reshape(rows, cols // BLOCK, 2, HALF).swapaxes(2, 3).reshape(rows, cols)


def put(buffer, value, place):
    return lax.dynamic_update_slice_in_dim(buffer, value, place * value.shape[0], 0)


def take(buffer, place, count):
    return lax.dynamic_slice_in_dim(buffer, place * count, count, 0)


def shards(
    inputs, cotangent, gains, up_blocks, up_index, up_count, down_blocks, down_index, down_count
):
    micro_count, tok_rows, features = inputs.shape
    section_index = lax.axis_index("section")
    section_count = lax.axis_size("section")
    last = section_count - 1
    tp_count = lax.axis_size("tp")
    group_width = FF // tp_count
    total_rows = tok_rows * tp_count
    row_blocks = features // BLOCK
    group_blocks = group_width // BLOCK
    gain = gains[0]
    first_own = own_rows(normalize(inputs[0], gain)[2])
    cot_own = [own_rows(cotangent[micro]) for micro in range(micro_count)]
    w_down = densify(down_blocks[0], down_index[0], down_count[0], group_blocks, row_blocks)
    first_own, cot_own, up_later, _ = lax.optimization_barrier((first_own, cot_own, up_blocks[0], w_down))
    gathered = (first_own, other_core(first_own))
    w_up = densify(up_later, up_index[0], up_count[0], row_blocks, group_blocks)
    live_rows = micro_count * total_rows

    places = micro_count + 1
    kept_fwd = []
    kept_input = jnp.zeros((places * tok_rows, features), jnp.bfloat16)
    kept_output = jnp.zeros((places * tok_rows, features), jnp.bfloat16)
    kept_ingrad = jnp.zeros((places * tok_rows, features), jnp.bfloat16)
    is_last = section_index == last

    rounds = 2 * section_count - 1
    ticks = rounds + micro_count - 1
    current = inputs[0]
    for tick in range(ticks):
        micro_fwd = tick - section_index
        micro_bwd = tick - (2 * last - section_index)
        fwd_active = (micro_fwd >= 0) & (micro_fwd < micro_count)
        bwd_active = (micro_bwd >= 0) & (micro_bwd < micro_count)
        any_fwd = tick <= last + micro_count - 1
        any_bwd = tick >= last
        partial = None
        if any_fwd:
            place = jnp.where(fwd_active, micro_fwd, micro_count)
            flags = jnp.stack([fwd_active, fwd_active & jnp.logical_not(is_last), place, fwd_active & is_last])
            flags = flags.astype(jnp.int32)
            if tick < last:
                *partial, kept_rows, kept_up, kept_hidden = forward_layer(flags, gathered, w_up, w_down, kept_fwd)
                kept_fwd = [kept_rows, kept_up, kept_hidden]
            else:
                *partial, kept_rows, kept_up, kept_hidden, kept_upgrad = forward_layer(
                    flags, gathered, w_up, w_down, kept_fwd, pre_grad
                )
                kept_fwd = [kept_rows, kept_up, kept_hidden, kept_upgrad]
            kept_input = put(kept_input, current, place)
        if tick == 0:
            cot_own, partial = lax.optimization_barrier((cot_own, partial))
            kept_grad = jnp.concatenate(
                [half for own in cot_own for half in (own, other_core(own))]
                + [jnp.zeros((total_rows, features), jnp.bfloat16)]
            )
        if tick == 1:
            cot_all, partial = lax.optimization_barrier((kept_grad, partial))
            pre_grad = lax.cond(
                is_last,
                lambda: natural_columns(
                    jnp.dot(cot_all[:live_rows], w_down.T, preferred_element_type=jnp.float32)
                ),
                lambda: jnp.zeros((live_rows, group_width), jnp.float32),
            )
        if tick == 2:
            pre_grad, partial = lax.optimization_barrier((pre_grad, partial))
        if any_bwd:
            place_bwd = jnp.where(bwd_active, micro_bwd, micro_count)
            incoming = current
            if tick - last < micro_count:
                incoming = jnp.where(is_last, cotangent[tick - last], current)
        if tick > last:
            flags = jnp.stack([bwd_active & jnp.logical_not(is_last), place_bwd]).astype(jnp.int32)
            flags = flags.at[1].set(jnp.where(is_last, micro_count, place_bwd))
            *back, kept_grad, kept_upgrad = backward_layer(
                flags, gathered, kept_up, w_up, w_down, [kept_grad, kept_upgrad]
            )
            if any_fwd:
                back = [jnp.where(is_last, turned, one) for turned, one in zip(partial, back)]
            partial = back
        if tick == last + micro_count:
            hidden, partial = lax.optimization_barrier((kept_hidden, partial))
            final = lax.cond(
                is_last,
                lambda: jnp.dot(hidden[:live_rows], w_down, preferred_element_type=jnp.float32).astype(jnp.bfloat16),
                lambda: jnp.zeros((live_rows, features), jnp.bfloat16),
            )
            final = final.reshape(micro_count, 2, tp_count // 2, tok_rows, features)
            final = jnp.where(lax.axis_index("tp") % 2 == 0, final, final[:, ::-1])
            final = final.transpose(2, 1, 0, 3, 4).reshape(live_rows, features)
        if tick > last + micro_count:
            final, partial = lax.optimization_barrier((final, partial))
        sums = row_sums(*partial)
        if tick + 1 == ticks:
            up_grads = block_grads(kept_rows, kept_upgrad, up_index[0], up_count[0], live_rows, True)
            sums, up_grads = lax.optimization_barrier((sums, up_grads))
            final, _ = lax.optimization_barrier((final, sums))
        send = None
        if any_fwd and tick < last + micro_count - 1:
            layer_out = (current.astype(jnp.float32) + sums).astype(jnp.bfloat16)
            kept_output = put(kept_output, layer_out, place)
            send = layer_out
        if any_bwd:
            values, inv_rms, _ = normalize(take(kept_input, place_bwd, tok_rows), gain)
            scaled_grad = sums * gain.astype(jnp.float32)
            norm_term = inv_rms * scaled_grad - values * (inv_rms * inv_rms * inv_rms) * jnp.mean(
                scaled_grad * values, axis=-1, keepdims=True
            )
            grad_in = (incoming.astype(jnp.float32) + norm_term).astype(jnp.bfloat16)
            kept_ingrad = put(kept_ingrad, grad_in, place_bwd)
            send = grad_in if send is None else jnp.where(bwd_active, grad_in, send)
        if tick + 1 == ticks:
            break
        pairs = []
        for micro in range(micro_count):
            done = tick - micro
            if 0 <= done < rounds - 1:
                pairs.append((last - abs(last - done), last - abs(last - done - 1)))
        current = lax.ppermute(send, "section", pairs)
        if tick + 1 < micro_count:
            current = jnp.where(section_index == 0, inputs[tick + 1], current)
        next_fwd = tick + 1 <= last + micro_count - 1
        next_bwd = tick + 1 > last
        source = current
        if next_fwd:
            source = normalize(current, gain)[2]
            if next_bwd:
                source = jnp.where(section_index + micro_count > tick + 1, source, current)
        gathered = all_rows(source)

    down_grads = block_grads(kept_hidden, kept_grad, down_index[0], down_count[0], live_rows, False)
    final_sums = lax.psum_scatter(final, "tp", scatter_dimension=0, tiled=True).astype(jnp.float32)
    final_out = (kept_input[: micro_count * tok_rows].astype(jnp.float32) + final_sums).astype(jnp.bfloat16)
    outputs = jnp.where(is_last, final_out, kept_output[: micro_count * tok_rows])
    shape = (1, micro_count, tok_rows, features)
    return (
        outputs.reshape(shape),
        kept_ingrad[: micro_count * tok_rows].reshape(shape),
        up_grads[None],
        down_grads[None],
    )


def solution(mesh):
    return jax.shard_map(
        shards,
        mesh=mesh,
        in_specs=(
            P(None, "tp", None),
            P(None, "tp", None),
            P("section", None),
            P("section", "tp", None),
            P("section", "tp"),
            P("section", "tp"),
            P("section", "tp", None),
            P("section", "tp"),
            P("section", "tp"),
        ),
        out_specs=(
            P("section", None, "tp", None),
            P("section", None, "tp", None),
            P("section", "tp", None),
            P("section", "tp", None),
        ),
        check_vma=False,
    )
```

```python
import functools

import jax
import jax.numpy as jnp
from jax import lax
from jax.experimental import pallas as pl
from jax.experimental.pallas import tpu as pltpu
from jax.sharding import PartitionSpec as P

FF = 16384
BLOCK = 64
MICRO = 2
STREAMS = 4
PAIR = 2 * BLOCK
HALF = BLOCK // 2
STRIP = 256
VMEM_BYTES = 58 * 2**20

NORM_EPSILON = 1e-05


def slot_step(slots):
    for size in (192, 128, 64, 32, 16):
        if slots % size == 0:
            return size
    return slots


def split_order(rows_split):
    first = lax.broadcasted_iota(jnp.int32, (STRIP, STRIP), 0)
    second = lax.broadcasted_iota(jnp.int32, (STRIP, STRIP), 1)
    split, natural = (first, second) if rows_split else (second, first)
    inner = split % BLOCK
    target = (split - inner) + 2 * (inner % HALF) + inner // HALF
    return (target == natural).astype(jnp.bfloat16)


def densify_kernel(slots, step_slots, index_ref, count_ref, block_ref, out_ref, held, packed, place):
    step = pl.program_id(0)
    load_steps = slots // step_slots
    width = out_ref.shape[1]
    pairs = width // PAIR
    spare = place.shape[0] - 1

    @pl.when(step == 0)
    def _():
        held[slots] = jnp.zeros((HALF, PAIR), jnp.bfloat16)

        @pl.loop(0, spare // 16)
        def _(group):
            for lane in range(16):
                place[group * 16 + lane] = slots

    @pl.when(step < load_steps)
    def _():
        first = step * step_slots
        for start in range(0, step_slots, 16):
            packed[start : start + 16] = block_ref[start : start + 16, :].reshape(16, HALF, PAIR)

        @pl.loop(0, step_slots // 16)
        def _(group):
            start = pl.multiple_of(group * 16, 16)
            for lane in range(16):
                slot = first + start + lane
                held[slot] = packed[start + lane]
                place[jnp.where(slot < count_ref[0], index_ref[slot], spare)] = slot

    @pl.when(step >= load_steps)
    def _():
        strip = step - load_steps
        lane = lax.broadcasted_iota(jnp.int32, (HALF, PAIR), 1)
        low = lane < BLOCK
        for row in range(STRIP // BLOCK):
            for col in range(pairs):
                pair = (strip * (STRIP // BLOCK) + row) * pairs + col
                left = held[place[2 * pair]]
                right = held[place[2 * pair + 1]]
                top = row * BLOCK
                lanes = slice(col * PAIR, (col + 1) * PAIR)
                crossed = pltpu.roll(jnp.where(low, right, left), BLOCK, 1)
                out_ref[top : top + HALF, lanes] = jnp.where(low, left, crossed)
                out_ref[top + HALF : top + BLOCK, lanes] = jnp.where(low, crossed, right)


def densify(blocks, block_index, live_count, row_blocks, col_blocks):
    slots = blocks.shape[0]
    step_slots = slot_step(slots)
    load_steps = slots // step_slots
    width = min(col_blocks * BLOCK, 2048)
    across = col_blocks * BLOCK // width
    strips = row_blocks * BLOCK // STRIP
    if across > 1:
        piece_blocks = width // BLOCK
        row, col = block_index // col_blocks, block_index % col_blocks
        strip, row = row // 4, row % 4
        block_index = ((strip * across + col // piece_blocks) * 4 + row) * piece_blocks + col % piece_blocks

    def out_place(step, index, count):
        spot = jnp.maximum(step - load_steps, 0)
        return (spot // across, spot % across)

    return pl.pallas_call(
        functools.partial(densify_kernel, slots, step_slots),
        grid_spec=pltpu.PrefetchScalarGridSpec(
            num_scalar_prefetch=2,
            grid=(load_steps + strips * across,),
            in_specs=[
                pl.BlockSpec((step_slots, BLOCK * BLOCK), lambda step, index, count: (jnp.minimum(step, load_steps - 1), 0))
            ],
            out_specs=pl.BlockSpec((STRIP, width), out_place),
            scratch_shapes=[
                pltpu.VMEM((slots + 1, HALF, PAIR), jnp.bfloat16),
                pltpu.VMEM((step_slots, HALF, PAIR), jnp.bfloat16),
                pltpu.SMEM((row_blocks * col_blocks + 1,), jnp.int32),
            ],
        ),
        out_shape=jax.ShapeDtypeStruct((row_blocks * BLOCK, col_blocks * BLOCK), jnp.bfloat16),
        compiler_params=pltpu.CompilerParams(
            dimension_semantics=("arbitrary",), vmem_limit_bytes=VMEM_BYTES
        ),
        name="densify",
    )(block_index, live_count, blocks)


def block_grads_kernel(strips, step_slots, index_ref, count_ref, left_ref, right_ref, out_ref, dense, packed):
    step = pl.program_id(0)
    width = right_ref.shape[1]
    pairs = width // PAIR

    @pl.when(step < strips)
    def _():
        left = left_ref[...].T
        piece = min(width, 512)
        for start in range(0, width, piece):
            product = jnp.dot(
                left, right_ref[:, start : start + piece], preferred_element_type=jnp.float32
            ).astype(jnp.bfloat16)
            for row in range(STRIP // BLOCK):
                for col in range(piece // PAIR):
                    pair = (step * (STRIP // BLOCK) + row) * pairs + start // PAIR + col
                    lanes = slice(col * PAIR, (col + 1) * PAIR)
                    dense[2 * pair] = product[row * BLOCK : row * BLOCK + HALF, lanes]
                    dense[2 * pair + 1] = product[row * BLOCK + HALF : (row + 1) * BLOCK, lanes]

    @pl.when(step >= strips)
    def _():
        first = (step - strips) * step_slots
        lane = lax.broadcasted_iota(jnp.int32, (HALF, PAIR), 1)
        low = lane < BLOCK

        @pl.loop(0, step_slots // 16)
        def _(group):
            start = pl.multiple_of(group * 16, 16)
            for one in range(16):
                slot = first + start + one
                spot = index_ref[slot]
                keep = dense[spot]
                other = pltpu.roll(dense[spot ^ 1], BLOCK, 1)
                picked = jnp.where(low == (spot % 2 == 0), keep, other)
                packed[one] = jnp.where(slot < count_ref[0], picked, jnp.zeros_like(picked))
            out_ref[pl.ds(start, 16), :] = packed[...].reshape(16, BLOCK * BLOCK)


def block_grads(left, right, block_index, live_count, tokens):
    rows = left.shape[1]
    cols = right.shape[1]
    slots = block_index.shape[0]
    step_slots = slot_step(slots)
    strips = rows // STRIP
    return pl.pallas_call(
        functools.partial(block_grads_kernel, strips, step_slots),
        grid_spec=pltpu.PrefetchScalarGridSpec(
            num_scalar_prefetch=2,
            grid=(strips + slots // step_slots,),
            in_specs=[
                pl.BlockSpec((tokens, STRIP), lambda step, index, count: (0, jnp.minimum(step, strips - 1))),
                pl.BlockSpec((tokens, cols), lambda step, index, count: (0, 0)),
            ],
            out_specs=pl.BlockSpec(
                (step_slots, BLOCK * BLOCK), lambda step, index, count: (jnp.maximum(step - strips, 0), 0)
            ),
            scratch_shapes=[
                pltpu.VMEM((rows * cols // (HALF * PAIR), HALF, PAIR), jnp.bfloat16),
                pltpu.VMEM((16, HALF, PAIR), jnp.bfloat16),
            ],
        ),
        out_shape=jax.ShapeDtypeStruct((slots, BLOCK * BLOCK), jnp.bfloat16),
        compiler_params=pltpu.CompilerParams(
            dimension_semantics=("arbitrary",), vmem_limit_bytes=VMEM_BYTES
        ),
        cost_estimate=pl.CostEstimate(
            flops=6 * tokens * rows * cols, bytes_accessed=6 * rows * cols, transcendentals=0
        ),
        name="block_grads",
    )(block_index, live_count, left, right)


def normalize(activ_rows, gain):
    values = activ_rows.astype(jnp.float32)
    inv_rms = lax.rsqrt(jnp.mean(values * values, axis=-1, keepdims=True) + NORM_EPSILON)
    return (values, inv_rms, (values * inv_rms * gain.astype(jnp.float32)).astype(jnp.bfloat16))


def same_core():
    count = lax.axis_size("tp")
    return [list(range(core, count, 2)) for core in range(2)]


def other_core(array):
    return lax.ppermute(array, "tp", [(index, index ^ 1) for index in range(lax.axis_size("tp"))])


def own_rows(local_rows):
    return lax.all_gather(local_rows, "tp", axis=0, tiled=True, axis_index_groups=same_core())


def all_rows(local_rows):
    own = own_rows(local_rows)
    return own, other_core(own)


def row_sums(part_own, part_other):
    chip = (part_own.astype(jnp.float32) + other_core(part_other).astype(jnp.float32)).astype(jnp.bfloat16)
    return lax.psum_scatter(
        chip, "tp", scatter_dimension=0, tiled=True, axis_index_groups=same_core()
    ).astype(jnp.float32)


def reordered(values, order, dtype=jnp.bfloat16):
    groups = [
        jnp.dot(values[:, start : start + STRIP], order, preferred_element_type=jnp.float32).astype(dtype)
        for start in range(0, values.shape[1], STRIP)
    ]
    return groups[0] if len(groups) == 1 else jnp.concatenate(groups, axis=1)


def reordered_wide(values, order):
    high = values.astype(jnp.bfloat16)
    low = (values - high.astype(jnp.float32)).astype(jnp.bfloat16)
    return reordered(high, order, jnp.float32) + reordered(low, order, jnp.float32)


def times_turned(left, refs):
    transposed = (((1,), (1,)), ((), ()))
    width = refs[0].shape[1]
    total = None
    for number, ref in enumerate(refs):
        part = lax.dot_general(
            left[:, number * width : (number + 1) * width], ref[...], transposed, preferred_element_type=jnp.float32
        )
        total = part if total is None else total + part
    return total


def forward_kernel(up_steps, turn, flags, own_ref, other_ref, *rest):
    ups, downs, rest = rest[:STREAMS], rest[STREAMS : 2 * STREAMS], rest[2 * STREAMS :]
    outs = rest[len(rest) - 8 - turn :]
    part_own, part_other, kept_rows, kept_up, kept_hidden = outs[:5]
    total, order, back = outs[-3:]
    step = pl.program_id(0)
    depth = ups[0].shape[0]
    half = own_ref.shape[0]
    up_active, down_active, turn_active = flags[0] > 0, flags[1] > 0, flags[3] > 0

    @pl.when(up_active & (step < up_steps))
    def _():
        @pl.when(step == 0)
        def _():
            total[...] = jnp.zeros_like(total)
            order[...] = split_order(False)
            back[...] = split_order(True)

        features = pl.ds(pl.multiple_of(step * depth, depth), depth)
        rows = jnp.concatenate([own_ref[:, features], other_ref[:, features]], axis=0)
        rows = reordered(rows, order[...])
        kept_rows[:, features] = rows
        width = ups[0].shape[1]
        for number, ref in enumerate(ups):
            lanes = slice(number * width, (number + 1) * width)
            total[:, lanes] += jnp.dot(rows, ref[...], preferred_element_type=jnp.float32)

        @pl.when(step == up_steps - 1)
        def _():
            proj = total[...]
            kept_up[...] = proj
            gate = 1.0 / (1.0 + jnp.exp(-proj))
            kept_hidden[...] = reordered((proj * gate).astype(jnp.bfloat16), order[...])
            if turn:
                pre_ref, kept_upgrad = rest[0], outs[5]
                act_grad = reordered_wide(pre_ref[...], back[...])
                kept_upgrad[...] = (act_grad * gate * (1.0 + proj * (1.0 - gate))).astype(jnp.bfloat16)

    @pl.when(step >= up_steps)
    def _():
        @pl.when(down_active)
        def _():
            width = downs[0].shape[1]
            hidden = kept_hidden[...]
            for number, ref in enumerate(downs):
                part = jnp.dot(hidden, ref[...], preferred_element_type=jnp.float32).astype(jnp.bfloat16)
                lanes = slice(number * width, (number + 1) * width)
                part_own[:, lanes] = part[:half]
                part_other[:, lanes] = part[half:]

        if turn:

            @pl.when(turn_active)
            def _():
                part = reordered(times_turned(outs[5][...], ups).astype(jnp.bfloat16), back[...])
                part_own[...] = part[:half]
                part_other[...] = part[half:]

        @pl.when(jnp.logical_not(down_active | turn_active))
        def _():
            part_own[...] = jnp.zeros_like(part_own)
            part_other[...] = jnp.zeros_like(part_other)


def layer_cost(tokens, features, units):
    return pl.CostEstimate(flops=4 * tokens * features * units, bytes_accessed=4 * features * units, transcendentals=0)


def forward_layer(flags, rows, w_up, w_down, kept, pre=None):
    turn = pre is not None
    half, features = rows[0].shape
    tokens = 2 * half
    units = w_up.shape[1]
    depth = 1024
    up_steps = down_steps = features // depth
    last_up = up_steps - 1
    up_width, down_width = units // STREAMS, depth // STREAMS
    any_space = [pl.BlockSpec(memory_space=pl.ANY)] * len(kept)

    def up_place(number):
        def place(step, flags):
            plain = flags[0] * jnp.minimum(step, last_up)
            return (jnp.where(flags[3] > 0, step % up_steps, plain) if turn else plain, number)

        return place

    def down_place(number):
        return lambda step, flags: (0, STREAMS * flags[1] * jnp.maximum(step - up_steps, 0) + number)

    def part_place(step, flags):
        return (0, jnp.maximum(step - up_steps, 0))

    def kept_place(step, flags):
        return (flags[2], 0)

    pre_spec = [pl.BlockSpec((tokens, units), lambda step, flags: (jnp.minimum(flags[2], MICRO - 1), 0))] * turn
    inputs = [flags, *rows, *[w_up] * STREAMS, *[w_down] * STREAMS, *[pre] * turn]
    places = (MICRO + 1) * tokens
    return pl.pallas_call(
        functools.partial(forward_kernel, up_steps, turn),
        grid_spec=pltpu.PrefetchScalarGridSpec(
            num_scalar_prefetch=1,
            grid=(up_steps + down_steps,),
            in_specs=[pl.BlockSpec((half, features), lambda step, flags: (0, 0))] * 2
            + [pl.BlockSpec((depth, up_width), up_place(number)) for number in range(STREAMS)]
            + [pl.BlockSpec((units, down_width), down_place(number)) for number in range(STREAMS)]
            + pre_spec
            + any_space,
            out_specs=[pl.BlockSpec((half, depth), part_place)] * 2
            + [
                pl.BlockSpec((tokens, features), kept_place),
                pl.BlockSpec((tokens, units), kept_place),
                pl.BlockSpec((tokens, units), kept_place),
            ]
            + [pl.BlockSpec((tokens, units), kept_place)] * turn,
            scratch_shapes=[
                pltpu.VMEM((tokens, units), jnp.float32),
                pltpu.VMEM((STRIP, STRIP), jnp.bfloat16),
                pltpu.VMEM((STRIP, STRIP), jnp.bfloat16),
            ],
        ),
        out_shape=[jax.ShapeDtypeStruct((half, features), jnp.bfloat16)] * 2
        + [
            jax.ShapeDtypeStruct((places, features), jnp.bfloat16),
            jax.ShapeDtypeStruct((places, units), jnp.float32),
            jax.ShapeDtypeStruct((places, units), jnp.bfloat16),
        ]
        + [jax.ShapeDtypeStruct((places, units), jnp.bfloat16)] * turn,
        input_output_aliases={len(inputs) + number: 2 + number for number in range(len(kept))},
        compiler_params=pltpu.CompilerParams(dimension_semantics=("arbitrary",), vmem_limit_bytes=VMEM_BYTES),
        cost_estimate=layer_cost(tokens, features, units),
        name="forward_layer",
    )(*inputs, *kept)


def backward_kernel(down_steps, flags, own_ref, other_ref, proj_ref, *rest):
    downs, ups = rest[:STREAMS], rest[STREAMS : 2 * STREAMS]
    part_own, part_other, kept_grad, kept_upgrad, back = rest[-5:]
    step = pl.program_id(0)
    width = downs[0].shape[0]
    half = own_ref.shape[0]
    active = flags[0] > 0

    @pl.when(active & (step < down_steps))
    def _():
        @pl.when(step == 0)
        def _():
            kept_grad[:half, :] = own_ref[...]
            kept_grad[half:, :] = other_ref[...]
            back[...] = split_order(True)

        act_grad = reordered_wide(times_turned(kept_grad, downs), back[...])
        lanes = pl.ds(pl.multiple_of(step * width, width), width)
        proj = proj_ref[:, lanes]
        gate = 1.0 / (1.0 + jnp.exp(-proj))
        kept_upgrad[:, lanes] = (act_grad * gate * (1.0 + proj * (1.0 - gate))).astype(jnp.bfloat16)

    @pl.when(step >= down_steps)
    def _():
        @pl.when(active)
        def _():
            part = reordered(times_turned(kept_upgrad[...], ups).astype(jnp.bfloat16), back[...])
            part_own[...] = part[:half]
            part_other[...] = part[half:]

        @pl.when(jnp.logical_not(active))
        def _():
            part_own[...] = jnp.zeros_like(part_own)
            part_other[...] = jnp.zeros_like(part_other)


def backward_layer(flags, grad, kept_up, w_up, w_down, kept):
    half, features = grad[0].shape
    tokens = 2 * half
    units = w_up.shape[1]
    width, depth = min(units, STRIP), 1024
    down_steps, up_steps = units // width, features // depth
    last_down = down_steps - 1
    any_space = [pl.BlockSpec(memory_space=pl.ANY)] * len(kept)

    def down_place(number):
        return lambda step, flags: (flags[0] * jnp.minimum(step, last_down), number)

    def up_place(number):
        return lambda step, flags: (flags[0] * jnp.maximum(step - down_steps, 0), number)

    def part_place(step, flags):
        return (0, jnp.maximum(step - down_steps, 0))

    def kept_place(step, flags):
        return (flags[1], 0)

    inputs = [flags, *grad, kept_up, *[w_down] * STREAMS, *[w_up] * STREAMS]
    places = (MICRO + 1) * tokens
    return pl.pallas_call(
        functools.partial(backward_kernel, down_steps),
        grid_spec=pltpu.PrefetchScalarGridSpec(
            num_scalar_prefetch=1,
            grid=(down_steps + up_steps,),
            in_specs=[pl.BlockSpec((half, features), lambda step, flags: (0, 0))] * 2
            + [pl.BlockSpec((tokens, units), kept_place)]
            + [pl.BlockSpec((width, features // STREAMS), down_place(number)) for number in range(STREAMS)]
            + [pl.BlockSpec((depth, units // STREAMS), up_place(number)) for number in range(STREAMS)]
            + any_space,
            out_specs=[pl.BlockSpec((half, depth), part_place)] * 2
            + [pl.BlockSpec((tokens, features), kept_place), pl.BlockSpec((tokens, units), kept_place)],
            scratch_shapes=[pltpu.VMEM((STRIP, STRIP), jnp.bfloat16)],
        ),
        out_shape=[jax.ShapeDtypeStruct((half, features), jnp.bfloat16)] * 2
        + [
            jax.ShapeDtypeStruct((places, features), jnp.bfloat16),
            jax.ShapeDtypeStruct((places, units), jnp.bfloat16),
        ],
        input_output_aliases={len(inputs) + number: 2 + number for number in range(len(kept))},
        compiler_params=pltpu.CompilerParams(dimension_semantics=("arbitrary",), vmem_limit_bytes=VMEM_BYTES),
        cost_estimate=layer_cost(tokens, features, units),
        name="backward_layer",
    )(*inputs, *kept)


def put(buffer, value, place):
    return lax.dynamic_update_slice_in_dim(buffer, value, place * value.shape[0], 0)


def take(buffer, place, count):
    return lax.dynamic_slice_in_dim(buffer, place * count, count, 0)


def shards(
    inputs, cotangent, gains, up_blocks, up_index, up_count, down_blocks, down_index, down_count
):
    micro_count, tok_rows, features = inputs.shape
    section_index = lax.axis_index("section")
    section_count = lax.axis_size("section")
    last = section_count - 1
    tp_count = lax.axis_size("tp")
    group_width = FF // tp_count
    total_rows = tok_rows * tp_count
    row_blocks = features // BLOCK
    group_blocks = group_width // BLOCK
    gain = gains[0]
    first_own = own_rows(normalize(inputs[0], gain)[2])
    cot_own = [own_rows(cotangent[micro]) for micro in range(micro_count)]
    w_up = densify(up_blocks[0], up_index[0], up_count[0], row_blocks, group_blocks)
    w_down = densify(down_blocks[0], down_index[0], down_count[0], group_blocks, row_blocks)
    first_own, cot_own, w_up, w_down = lax.optimization_barrier((first_own, cot_own, w_up, w_down))
    gathered = (first_own, other_core(first_own))
    live_rows = micro_count * total_rows

    places = micro_count + 1
    kept_fwd = []
    kept_input = jnp.zeros((places * tok_rows, features), jnp.bfloat16)
    kept_output = jnp.zeros((places * tok_rows, features), jnp.bfloat16)
    kept_ingrad = jnp.zeros((places * tok_rows, features), jnp.bfloat16)
    is_last = section_index == last

    rounds = 2 * section_count - 1
    ticks = rounds + micro_count - 1
    current = inputs[0]
    for tick in range(ticks):
        micro_fwd = tick - section_index
        micro_bwd = tick - (2 * last - section_index)
        fwd_active = (micro_fwd >= 0) & (micro_fwd < micro_count)
        bwd_active = (micro_bwd >= 0) & (micro_bwd < micro_count)
        any_fwd = tick <= last + micro_count - 1
        any_bwd = tick >= last
        partial = None
        if tick + 1 == ticks:
            final, gathered = lax.optimization_barrier((final, gathered))
            final_sums = lax.psum_scatter(final, "tp", scatter_dimension=0, tiled=True).astype(jnp.float32)
        if any_fwd:
            place = jnp.where(fwd_active, micro_fwd, micro_count)
            flags = jnp.stack([fwd_active, fwd_active & jnp.logical_not(is_last), place, fwd_active & is_last])
            flags = flags.astype(jnp.int32)
            if tick < last:
                *partial, kept_rows, kept_up, kept_hidden = forward_layer(flags, gathered, w_up, w_down, kept_fwd)
                kept_fwd = [kept_rows, kept_up, kept_hidden]
            else:
                *partial, kept_rows, kept_up, kept_hidden, kept_upgrad = forward_layer(
                    flags, gathered, w_up, w_down, kept_fwd, pre_grad
                )
                kept_fwd = [kept_rows, kept_up, kept_hidden, kept_upgrad]
            kept_input = put(kept_input, current, place)
        if tick == 0:
            cot_own, partial = lax.optimization_barrier((cot_own, partial))
            kept_grad = jnp.concatenate(
                [half for own in cot_own for half in (own, other_core(own))]
                + [jnp.zeros((total_rows, features), jnp.bfloat16)]
            )
        if tick == 1:
            cot_all, partial = lax.optimization_barrier((kept_grad, partial))
            pre_grad = lax.cond(
                is_last,
                lambda: jnp.dot(cot_all[:live_rows], w_down.T, preferred_element_type=jnp.float32),
                lambda: jnp.zeros((live_rows, group_width), jnp.float32),
            )
        if tick == 2:
            pre_grad, partial = lax.optimization_barrier((pre_grad, partial))
        if any_bwd:
            place_bwd = jnp.where(bwd_active, micro_bwd, micro_count)
            incoming = current
            if tick - last < micro_count:
                incoming = jnp.where(is_last, cotangent[tick - last], current)
        if tick > last:
            flags = jnp.stack([bwd_active & jnp.logical_not(is_last), place_bwd]).astype(jnp.int32)
            flags = flags.at[1].set(jnp.where(is_last, micro_count, place_bwd))
            *back, kept_grad, kept_upgrad = backward_layer(
                flags, gathered, kept_up, w_up, w_down, [kept_grad, kept_upgrad]
            )
            if any_fwd:
                back = [jnp.where(is_last, turned, one) for turned, one in zip(partial, back)]
            partial = back
        if tick == last + micro_count:
            hidden, partial = lax.optimization_barrier((kept_hidden, partial))

            def last_sums():
                parts = jnp.dot(hidden[:live_rows], w_down, preferred_element_type=jnp.float32).astype(jnp.bfloat16)
                parts = parts.reshape(micro_count, 2, tp_count // 2, tok_rows, features)
                parts = jnp.where(lax.axis_index("tp") % 2 == 0, parts, parts[:, ::-1])
                return parts.transpose(2, 1, 0, 3, 4).reshape(live_rows, features)

            final = lax.cond(is_last, last_sums, lambda: jnp.zeros((live_rows, features), jnp.bfloat16))
        if tick == last + micro_count + 1 and tick + 1 < ticks:
            final, partial = lax.optimization_barrier((final, partial))
        sums = row_sums(*partial)
        if tick + 1 == ticks:
            up_grads = block_grads(kept_rows, kept_upgrad, up_index[0], up_count[0], live_rows)
            sums, up_grads = lax.optimization_barrier((sums, up_grads))
        send = None
        if any_fwd and tick < last + micro_count - 1:
            layer_out = (current.astype(jnp.float32) + sums).astype(jnp.bfloat16)
            kept_output = put(kept_output, layer_out, place)
            send = layer_out
        if any_bwd:
            values, inv_rms, _ = normalize(take(kept_input, place_bwd, tok_rows), gain)
            scaled_grad = sums * gain.astype(jnp.float32)
            norm_term = inv_rms * scaled_grad - values * (inv_rms * inv_rms * inv_rms) * jnp.mean(
                scaled_grad * values, axis=-1, keepdims=True
            )
            grad_in = (incoming.astype(jnp.float32) + norm_term).astype(jnp.bfloat16)
            kept_ingrad = put(kept_ingrad, grad_in, place_bwd)
            send = grad_in if send is None else jnp.where(bwd_active, grad_in, send)
        if tick + 1 == ticks:
            break
        pairs = []
        for micro in range(micro_count):
            done = tick - micro
            if 0 <= done < rounds - 1:
                pairs.append((last - abs(last - done), last - abs(last - done - 1)))
        current = lax.ppermute(send, "section", pairs)
        if tick + 1 < micro_count:
            current = jnp.where(section_index == 0, inputs[tick + 1], current)
        next_fwd = tick + 1 <= last + micro_count - 1
        next_bwd = tick + 1 > last
        source = current
        if next_fwd:
            source = normalize(current, gain)[2]
            if next_bwd:
                source = jnp.where(section_index + micro_count > tick + 1, source, current)
        gathered = all_rows(source)

    down_grads = block_grads(kept_hidden, kept_grad, down_index[0], down_count[0], live_rows)
    final_out = (kept_input[: micro_count * tok_rows].astype(jnp.float32) + final_sums).astype(jnp.bfloat16)
    outputs = jnp.where(is_last, final_out, kept_output[: micro_count * tok_rows])
    shape = (1, micro_count, tok_rows, features)
    return (
        outputs.reshape(shape),
        kept_ingrad[: micro_count * tok_rows].reshape(shape),
        up_grads[None],
        down_grads[None],
    )


def solution(mesh):
    return jax.shard_map(
        shards,
        mesh=mesh,
        in_specs=(
            P(None, "tp", None),
            P(None, "tp", None),
            P("section", None),
            P("section", "tp", None),
            P("section", "tp"),
            P("section", "tp"),
            P("section", "tp", None),
            P("section", "tp"),
            P("section", "tp"),
        ),
        out_specs=(
            P("section", None, "tp", None),
            P("section", None, "tp", None),
            P("section", "tp", None),
            P("section", "tp", None),
        ),
        check_vma=False,
    )
```

```python
import functools

import jax
import jax.numpy as jnp
from jax import lax
from jax.experimental import pallas as pl
from jax.experimental.pallas import tpu as pltpu
from jax.sharding import PartitionSpec as P

FF = 16384
BLOCK = 64
MICRO = 2
STREAMS = 4
PAIR = 2 * BLOCK
HALF = BLOCK // 2
STRIP = 256
VMEM_BYTES = 58 * 2**20

NORM_EPSILON = 1e-05


def slot_step(slots):
    for size in (192, 128, 64, 32, 16):
        if slots % size == 0:
            return size
    return slots


def split_order(rows_split):
    first = lax.broadcasted_iota(jnp.int32, (STRIP, STRIP), 0)
    second = lax.broadcasted_iota(jnp.int32, (STRIP, STRIP), 1)
    split, natural = (first, second) if rows_split else (second, first)
    inner = split % BLOCK
    target = (split - inner) + 2 * (inner % HALF) + inner // HALF
    return (target == natural).astype(jnp.bfloat16)


def densify_kernel(slots, step_slots, index_ref, count_ref, block_ref, out_ref, held, packed, place):
    step = pl.program_id(0)
    load_steps = slots // step_slots
    width = out_ref.shape[1]
    pairs = width // PAIR
    spare = place.shape[0] - 1

    @pl.when(step == 0)
    def _():
        held[slots] = jnp.zeros((HALF, PAIR), jnp.bfloat16)

        @pl.loop(0, spare // 16)
        def _(group):
            for lane in range(16):
                place[group * 16 + lane] = slots

    @pl.when(step < load_steps)
    def _():
        first = step * step_slots
        for start in range(0, step_slots, 16):
            packed[start : start + 16] = block_ref[start : start + 16, :].reshape(16, HALF, PAIR)

        @pl.loop(0, step_slots // 16)
        def _(group):
            start = pl.multiple_of(group * 16, 16)
            for lane in range(16):
                slot = first + start + lane
                held[slot] = packed[start + lane]
                place[jnp.where(slot < count_ref[0], index_ref[slot], spare)] = slot

    @pl.when(step >= load_steps)
    def _():
        strip = step - load_steps
        lane = lax.broadcasted_iota(jnp.int32, (HALF, PAIR), 1)
        low = lane < BLOCK
        for row in range(STRIP // BLOCK):
            for col in range(pairs):
                pair = (strip * (STRIP // BLOCK) + row) * pairs + col
                left = held[place[2 * pair]]
                right = held[place[2 * pair + 1]]
                top = row * BLOCK
                lanes = slice(col * PAIR, (col + 1) * PAIR)
                crossed = pltpu.roll(jnp.where(low, right, left), BLOCK, 1)
                out_ref[top : top + HALF, lanes] = jnp.where(low, left, crossed)
                out_ref[top + HALF : top + BLOCK, lanes] = jnp.where(low, crossed, right)


def densify(blocks, block_index, live_count, row_blocks, col_blocks):
    slots = blocks.shape[0]
    step_slots = slot_step(slots)
    load_steps = slots // step_slots
    width = min(col_blocks * BLOCK, 2048)
    across = col_blocks * BLOCK // width
    strips = row_blocks * BLOCK // STRIP
    if across > 1:
        piece_blocks = width // BLOCK
        row, col = block_index // col_blocks, block_index % col_blocks
        strip, row = row // 4, row % 4
        block_index = ((strip * across + col // piece_blocks) * 4 + row) * piece_blocks + col % piece_blocks

    def out_place(step, index, count):
        spot = jnp.maximum(step - load_steps, 0)
        return (spot // across, spot % across)

    return pl.pallas_call(
        functools.partial(densify_kernel, slots, step_slots),
        grid_spec=pltpu.PrefetchScalarGridSpec(
            num_scalar_prefetch=2,
            grid=(load_steps + strips * across,),
            in_specs=[
                pl.BlockSpec((step_slots, BLOCK * BLOCK), lambda step, index, count: (jnp.minimum(step, load_steps - 1), 0))
            ],
            out_specs=pl.BlockSpec((STRIP, width), out_place),
            scratch_shapes=[
                pltpu.VMEM((slots + 1, HALF, PAIR), jnp.bfloat16),
                pltpu.VMEM((step_slots, HALF, PAIR), jnp.bfloat16),
                pltpu.SMEM((row_blocks * col_blocks + 1,), jnp.int32),
            ],
        ),
        out_shape=jax.ShapeDtypeStruct((row_blocks * BLOCK, col_blocks * BLOCK), jnp.bfloat16),
        compiler_params=pltpu.CompilerParams(
            dimension_semantics=("arbitrary",), vmem_limit_bytes=VMEM_BYTES
        ),
        name="densify",
    )(block_index, live_count, blocks)


def block_grads_kernel(strips, step_slots, index_ref, count_ref, left_ref, right_ref, out_ref, dense, packed):
    step = pl.program_id(0)
    width = right_ref.shape[1]
    pairs = width // PAIR

    @pl.when(step < strips)
    def _():
        left = left_ref[...].T
        piece = min(width, 512)
        for start in range(0, width, piece):
            product = jnp.dot(
                left, right_ref[:, start : start + piece], preferred_element_type=jnp.float32
            ).astype(jnp.bfloat16)
            for row in range(STRIP // BLOCK):
                for col in range(piece // PAIR):
                    pair = (step * (STRIP // BLOCK) + row) * pairs + start // PAIR + col
                    lanes = slice(col * PAIR, (col + 1) * PAIR)
                    dense[2 * pair] = product[row * BLOCK : row * BLOCK + HALF, lanes]
                    dense[2 * pair + 1] = product[row * BLOCK + HALF : (row + 1) * BLOCK, lanes]

    @pl.when(step >= strips)
    def _():
        first = (step - strips) * step_slots
        lane = lax.broadcasted_iota(jnp.int32, (HALF, PAIR), 1)
        low = lane < BLOCK

        @pl.loop(0, step_slots // 16)
        def _(group):
            start = pl.multiple_of(group * 16, 16)
            for one in range(16):
                slot = first + start + one
                spot = index_ref[slot]
                keep = dense[spot]
                other = pltpu.roll(dense[spot ^ 1], BLOCK, 1)
                picked = jnp.where(low == (spot % 2 == 0), keep, other)
                packed[one] = jnp.where(slot < count_ref[0], picked, jnp.zeros_like(picked))
            out_ref[pl.ds(start, 16), :] = packed[...].reshape(16, BLOCK * BLOCK)


def block_grads(left, right, block_index, live_count, tokens):
    rows = left.shape[1]
    cols = right.shape[1]
    slots = block_index.shape[0]
    step_slots = slot_step(slots)
    strips = rows // STRIP
    return pl.pallas_call(
        functools.partial(block_grads_kernel, strips, step_slots),
        grid_spec=pltpu.PrefetchScalarGridSpec(
            num_scalar_prefetch=2,
            grid=(strips + slots // step_slots,),
            in_specs=[
                pl.BlockSpec((tokens, STRIP), lambda step, index, count: (0, jnp.minimum(step, strips - 1))),
                pl.BlockSpec((tokens, cols), lambda step, index, count: (0, 0)),
            ],
            out_specs=pl.BlockSpec(
                (step_slots, BLOCK * BLOCK), lambda step, index, count: (jnp.maximum(step - strips, 0), 0)
            ),
            scratch_shapes=[
                pltpu.VMEM((rows * cols // (HALF * PAIR), HALF, PAIR), jnp.bfloat16),
                pltpu.VMEM((16, HALF, PAIR), jnp.bfloat16),
            ],
        ),
        out_shape=jax.ShapeDtypeStruct((slots, BLOCK * BLOCK), jnp.bfloat16),
        compiler_params=pltpu.CompilerParams(
            dimension_semantics=("arbitrary",), vmem_limit_bytes=VMEM_BYTES
        ),
        cost_estimate=pl.CostEstimate(
            flops=6 * tokens * rows * cols, bytes_accessed=6 * rows * cols, transcendentals=0
        ),
        name="block_grads",
    )(block_index, live_count, left, right)


def normalize(activ_rows, gain):
    values = activ_rows.astype(jnp.float32)
    inv_rms = lax.rsqrt(jnp.mean(values * values, axis=-1, keepdims=True) + NORM_EPSILON)
    return (values, inv_rms, (values * inv_rms * gain.astype(jnp.float32)).astype(jnp.bfloat16))


def same_core():
    count = lax.axis_size("tp")
    return [list(range(core, count, 2)) for core in range(2)]


def other_core(array):
    return lax.ppermute(array, "tp", [(index, index ^ 1) for index in range(lax.axis_size("tp"))])


def all_rows(local_rows):
    return lax.all_gather(local_rows, "tp", axis=0, tiled=True)


def row_sums(part_own, part_other):
    chip = (part_own.astype(jnp.float32) + other_core(part_other).astype(jnp.float32)).astype(jnp.bfloat16)
    return lax.psum_scatter(
        chip, "tp", scatter_dimension=0, tiled=True, axis_index_groups=same_core()
    ).astype(jnp.float32)


def reordered(values, order, dtype=jnp.bfloat16):
    groups = [
        jnp.dot(values[:, start : start + STRIP], order, preferred_element_type=jnp.float32).astype(dtype)
        for start in range(0, values.shape[1], STRIP)
    ]
    return groups[0] if len(groups) == 1 else jnp.concatenate(groups, axis=1)


def reordered_wide(values, order):
    high = values.astype(jnp.bfloat16)
    low = (values - high.astype(jnp.float32)).astype(jnp.bfloat16)
    return reordered(high, order, jnp.float32) + reordered(low, order, jnp.float32)


def times_turned(left, refs):
    transposed = (((1,), (1,)), ((), ()))
    width = refs[0].shape[1]
    total = None
    for number, ref in enumerate(refs):
        part = lax.dot_general(
            left[:, number * width : (number + 1) * width], ref[...], transposed, preferred_element_type=jnp.float32
        )
        total = part if total is None else total + part
    return total


def core_halves(part, local_count, core):
    pieces = [part[start : start + local_count] for start in range(0, part.shape[0], local_count)]
    even = jnp.concatenate(pieces[0::2], axis=0)
    odd = jnp.concatenate(pieces[1::2], axis=0)
    return jnp.where(core == 0, even, odd), jnp.where(core == 0, odd, even)


def forward_kernel(up_steps, turn, base, local_count, flags, rows_ref, *rest):
    ups, downs, rest = rest[:STREAMS], rest[STREAMS : 2 * STREAMS], rest[2 * STREAMS :]
    outs = rest[len(rest) - 8 - turn :]
    part_own, part_other, kept_rows, kept_up, kept_hidden = outs[:5]
    total, order, back = outs[-3:]
    step = pl.program_id(0)
    depth = ups[0].shape[0]
    up_active, down_active, turn_active = flags[base + 0] > 0, flags[base + 1] > 0, flags[base + 3] > 0

    @pl.when(up_active & (step < up_steps))
    def _():
        @pl.when(step == 0)
        def _():
            total[...] = jnp.zeros_like(total)
            order[...] = split_order(False)
            back[...] = split_order(True)

        features = pl.ds(pl.multiple_of(step * depth, depth), depth)
        rows = reordered(rows_ref[:, features], order[...])
        kept_rows[:, features] = rows
        width = ups[0].shape[1]
        for number, ref in enumerate(ups):
            lanes = slice(number * width, (number + 1) * width)
            total[:, lanes] += jnp.dot(rows, ref[...], preferred_element_type=jnp.float32)

        @pl.when(step == up_steps - 1)
        def _():
            proj = total[...]
            kept_up[...] = proj
            gate = 1.0 / (1.0 + jnp.exp(-proj))
            kept_hidden[...] = reordered((proj * gate).astype(jnp.bfloat16), order[...])
            if turn:
                pre_ref, kept_upgrad = rest[0], outs[5]
                act_grad = reordered_wide(pre_ref[...], back[...])
                kept_upgrad[...] = (act_grad * gate * (1.0 + proj * (1.0 - gate))).astype(jnp.bfloat16)

    @pl.when(step >= up_steps)
    def _():
        @pl.when(down_active)
        def _():
            width = downs[0].shape[1]
            hidden = kept_hidden[...]
            for number, ref in enumerate(downs):
                part = jnp.dot(hidden, ref[...], preferred_element_type=jnp.float32).astype(jnp.bfloat16)
                lanes = slice(number * width, (number + 1) * width)
                part_own[:, lanes], part_other[:, lanes] = core_halves(part, local_count, flags[base + 6])

        if turn:

            @pl.when(turn_active)
            def _():
                part = reordered(times_turned(outs[5][...], ups).astype(jnp.bfloat16), back[...])
                part_own[...], part_other[...] = core_halves(part, local_count, flags[base + 6])

        @pl.when(jnp.logical_not(down_active | turn_active))
        def _():
            part_own[...] = jnp.zeros_like(part_own)
            part_other[...] = jnp.zeros_like(part_other)


def layer_cost(tokens, features, units):
    return pl.CostEstimate(flops=4 * tokens * features * units, bytes_accessed=4 * features * units, transcendentals=0)


def forward_layer(flags, base, local_count, rows, w_up, w_down, kept, pre=None):
    turn = pre is not None
    tokens, features = rows.shape
    half = tokens // 2
    units = w_up.shape[1]
    depth = 1024
    up_steps = down_steps = features // depth
    last_up = up_steps - 1
    up_width, down_width = units // STREAMS, depth // STREAMS
    any_space = [pl.BlockSpec(memory_space=pl.ANY)] * len(kept)

    def up_place(number):
        def place(step, flags):
            plain = flags[base + 0] * jnp.minimum(step, last_up)
            return (jnp.where(flags[base + 3] > 0, step % up_steps, plain) if turn else plain, number)

        return place

    def down_place(number):
        return lambda step, flags: (0, STREAMS * flags[base + 1] * jnp.maximum(step - up_steps, 0) + number)

    def part_place(step, flags):
        return (0, jnp.maximum(step - up_steps, 0))

    def kept_place(step, flags):
        return (flags[base + 2], 0)

    pre_spec = [pl.BlockSpec((tokens, units), lambda step, flags: (jnp.minimum(flags[base + 2], MICRO - 1), 0))] * turn
    inputs = [flags, rows, *[w_up] * STREAMS, *[w_down] * STREAMS, *[pre] * turn]
    places = (MICRO + 1) * tokens
    return pl.pallas_call(
        functools.partial(forward_kernel, up_steps, turn, base, local_count),
        grid_spec=pltpu.PrefetchScalarGridSpec(
            num_scalar_prefetch=1,
            grid=(up_steps + down_steps,),
            in_specs=[pl.BlockSpec((tokens, features), lambda step, flags: (0, 0))]
            + [pl.BlockSpec((depth, up_width), up_place(number)) for number in range(STREAMS)]
            + [pl.BlockSpec((units, down_width), down_place(number)) for number in range(STREAMS)]
            + pre_spec
            + any_space,
            out_specs=[pl.BlockSpec((half, depth), part_place)] * 2
            + [
                pl.BlockSpec((tokens, features), kept_place),
                pl.BlockSpec((tokens, units), kept_place),
                pl.BlockSpec((tokens, units), kept_place),
            ]
            + [pl.BlockSpec((tokens, units), kept_place)] * turn,
            scratch_shapes=[
                pltpu.VMEM((tokens, units), jnp.float32),
                pltpu.VMEM((STRIP, STRIP), jnp.bfloat16),
                pltpu.VMEM((STRIP, STRIP), jnp.bfloat16),
            ],
        ),
        out_shape=[jax.ShapeDtypeStruct((half, features), jnp.bfloat16)] * 2
        + [
            jax.ShapeDtypeStruct((places, features), jnp.bfloat16),
            jax.ShapeDtypeStruct((places, units), jnp.float32),
            jax.ShapeDtypeStruct((places, units), jnp.bfloat16),
        ]
        + [jax.ShapeDtypeStruct((places, units), jnp.bfloat16)] * turn,
        input_output_aliases={len(inputs) + number: 2 + number for number in range(len(kept))},
        compiler_params=pltpu.CompilerParams(dimension_semantics=("arbitrary",), vmem_limit_bytes=VMEM_BYTES),
        cost_estimate=layer_cost(tokens, features, units),
        name="forward_layer",
    )(*inputs, *kept)


def backward_kernel(down_steps, base, local_count, flags, grad_ref, proj_ref, *rest):
    downs, ups = rest[:STREAMS], rest[STREAMS : 2 * STREAMS]
    part_own, part_other, kept_grad, kept_upgrad, back = rest[-5:]
    step = pl.program_id(0)
    width = downs[0].shape[0]
    active = flags[base + 4] > 0

    @pl.when(active & (step < down_steps))
    def _():
        @pl.when(step == 0)
        def _():
            kept_grad[...] = grad_ref[...]
            back[...] = split_order(True)

        act_grad = reordered_wide(times_turned(grad_ref, downs), back[...])
        lanes = pl.ds(pl.multiple_of(step * width, width), width)
        proj = proj_ref[:, lanes]
        gate = 1.0 / (1.0 + jnp.exp(-proj))
        kept_upgrad[:, lanes] = (act_grad * gate * (1.0 + proj * (1.0 - gate))).astype(jnp.bfloat16)

    @pl.when(step >= down_steps)
    def _():
        @pl.when(active)
        def _():
            part = reordered(times_turned(kept_upgrad[...], ups).astype(jnp.bfloat16), back[...])
            part_own[...], part_other[...] = core_halves(part, local_count, flags[base + 6])

        @pl.when(jnp.logical_not(active))
        def _():
            part_own[...] = jnp.zeros_like(part_own)
            part_other[...] = jnp.zeros_like(part_other)


def backward_layer(flags, base, local_count, grad, kept_up, w_up, w_down, kept):
    tokens, features = grad.shape
    half = tokens // 2
    units = w_up.shape[1]
    width, depth = min(units, STRIP), 1024
    down_steps, up_steps = units // width, features // depth
    last_down = down_steps - 1
    any_space = [pl.BlockSpec(memory_space=pl.ANY)] * len(kept)

    def down_place(number):
        return lambda step, flags: (flags[base + 4] * jnp.minimum(step, last_down), number)

    def up_place(number):
        return lambda step, flags: (flags[base + 4] * jnp.maximum(step - down_steps, 0), number)

    def part_place(step, flags):
        return (0, jnp.maximum(step - down_steps, 0))

    def kept_place(step, flags):
        return (flags[base + 5], 0)

    inputs = [flags, grad, kept_up, *[w_down] * STREAMS, *[w_up] * STREAMS]
    places = (MICRO + 1) * tokens
    return pl.pallas_call(
        functools.partial(backward_kernel, down_steps, base, local_count),
        grid_spec=pltpu.PrefetchScalarGridSpec(
            num_scalar_prefetch=1,
            grid=(down_steps + up_steps,),
            in_specs=[pl.BlockSpec((tokens, features), lambda step, flags: (0, 0))]
            + [pl.BlockSpec((tokens, units), kept_place)]
            + [pl.BlockSpec((width, features // STREAMS), down_place(number)) for number in range(STREAMS)]
            + [pl.BlockSpec((depth, units // STREAMS), up_place(number)) for number in range(STREAMS)]
            + any_space,
            out_specs=[pl.BlockSpec((half, depth), part_place)] * 2
            + [pl.BlockSpec((tokens, features), kept_place), pl.BlockSpec((tokens, units), kept_place)],
            scratch_shapes=[pltpu.VMEM((STRIP, STRIP), jnp.bfloat16)],
        ),
        out_shape=[jax.ShapeDtypeStruct((half, features), jnp.bfloat16)] * 2
        + [
            jax.ShapeDtypeStruct((places, features), jnp.bfloat16),
            jax.ShapeDtypeStruct((places, units), jnp.bfloat16),
        ],
        input_output_aliases={len(inputs) + number: 2 + number for number in range(len(kept))},
        compiler_params=pltpu.CompilerParams(dimension_semantics=("arbitrary",), vmem_limit_bytes=VMEM_BYTES),
        cost_estimate=layer_cost(tokens, features, units),
        name="backward_layer",
    )(*inputs, *kept)


def put(buffer, value, place):
    return lax.dynamic_update_slice_in_dim(buffer, value, place * value.shape[0], 0)


def take(buffer, place, count):
    return lax.dynamic_slice_in_dim(buffer, place * count, count, 0)


def shards(
    inputs, cotangent, gains, up_blocks, up_index, up_count, down_blocks, down_index, down_count
):
    micro_count, tok_rows, features = inputs.shape
    section_index = lax.axis_index("section")
    section_count = lax.axis_size("section")
    last = section_count - 1
    tp_count = lax.axis_size("tp")
    group_width = FF // tp_count
    total_rows = tok_rows * tp_count
    row_blocks = features // BLOCK
    group_blocks = group_width // BLOCK
    gain = gains[0]
    gathered = all_rows(normalize(inputs[0], gain)[2])
    cot_rows = [all_rows(cotangent[micro]) for micro in range(micro_count)]
    w_up = densify(up_blocks[0], up_index[0], up_count[0], row_blocks, group_blocks)
    w_down = densify(down_blocks[0], down_index[0], down_count[0], group_blocks, row_blocks)
    gathered, cot_rows, w_up, w_down = lax.optimization_barrier((gathered, cot_rows, w_up, w_down))
    live_rows = micro_count * total_rows

    places = micro_count + 1
    kept_fwd = []
    kept_input = jnp.zeros((places * tok_rows, features), jnp.bfloat16)
    kept_output = jnp.zeros((places * tok_rows, features), jnp.bfloat16)
    kept_ingrad = jnp.zeros((places * tok_rows, features), jnp.bfloat16)
    is_last = section_index == last

    rounds = 2 * section_count - 1
    ticks = rounds + micro_count - 1
    current = inputs[0]
    table = []
    for tick in range(ticks):
        micro_fwd = tick - section_index
        micro_bwd = tick - (2 * last - section_index)
        fwd_active = (micro_fwd >= 0) & (micro_fwd < micro_count)
        bwd_active = (micro_bwd >= 0) & (micro_bwd < micro_count) & jnp.logical_not(is_last)
        table += [
            fwd_active,
            fwd_active & jnp.logical_not(is_last),
            jnp.where(fwd_active, micro_fwd, micro_count),
            fwd_active & is_last,
            bwd_active,
            jnp.where(bwd_active, micro_bwd, micro_count),
            lax.axis_index("tp") % 2,
        ]
    flags = jnp.stack([jnp.asarray(entry, jnp.int32) for entry in table])
    flags, gathered = lax.optimization_barrier((flags, gathered))
    for tick in range(ticks):
        base = 7 * tick
        micro_fwd = tick - section_index
        micro_bwd = tick - (2 * last - section_index)
        fwd_active = (micro_fwd >= 0) & (micro_fwd < micro_count)
        bwd_active = (micro_bwd >= 0) & (micro_bwd < micro_count)
        any_fwd = tick <= last + micro_count - 1
        any_bwd = tick >= last
        partial = None
        if tick + 1 == ticks:
            final, gathered = lax.optimization_barrier((final, gathered))
            final_sums = lax.psum_scatter(final, "tp", scatter_dimension=0, tiled=True).astype(jnp.float32)
        if any_fwd:
            place = jnp.where(fwd_active, micro_fwd, micro_count)
            if tick < last:
                *partial, kept_rows, kept_up, kept_hidden = forward_layer(
                    flags, base, tok_rows, gathered, w_up, w_down, kept_fwd
                )
                kept_fwd = [kept_rows, kept_up, kept_hidden]
            else:
                *partial, kept_rows, kept_up, kept_hidden, kept_upgrad = forward_layer(
                    flags, base, tok_rows, gathered, w_up, w_down, kept_fwd, pre_grad
                )
                kept_fwd = [kept_rows, kept_up, kept_hidden, kept_upgrad]
            kept_input = put(kept_input, current, place)
        if tick == 0:
            cot_rows, partial = lax.optimization_barrier((cot_rows, partial))
            kept_grad = jnp.concatenate(cot_rows + [jnp.zeros((total_rows, features), jnp.bfloat16)])
        if tick == 1:
            cot_all, partial = lax.optimization_barrier((kept_grad, partial))
            pre_grad = lax.cond(
                is_last,
                lambda: jnp.dot(cot_all[:live_rows], w_down.T, preferred_element_type=jnp.float32),
                lambda: jnp.zeros((live_rows, group_width), jnp.float32),
            )
        if any_bwd:
            place_bwd = jnp.where(bwd_active, micro_bwd, micro_count)
            incoming = current
            if tick - last < micro_count:
                incoming = jnp.where(is_last, cotangent[tick - last], current)
        if tick > last:
            *back, kept_grad, kept_upgrad = backward_layer(
                flags, base, tok_rows, gathered, kept_up, w_up, w_down, [kept_grad, kept_upgrad]
            )
            if any_fwd:
                back = [jnp.where(is_last, turned, one) for turned, one in zip(partial, back)]
            partial = back
        if tick == last + micro_count:
            hidden, partial = lax.optimization_barrier((kept_hidden, partial))

            def last_sums():
                parts = jnp.dot(hidden[:live_rows], w_down, preferred_element_type=jnp.float32).astype(jnp.bfloat16)
                parts = parts.reshape(micro_count, tp_count, tok_rows, features)
                return parts.swapaxes(0, 1).reshape(live_rows, features)

            final = lax.cond(is_last, last_sums, lambda: jnp.zeros((live_rows, features), jnp.bfloat16))
        sums = row_sums(*partial)
        if tick == 1:
            pre_grad, sums = lax.optimization_barrier((pre_grad, sums))
        if tick == last + micro_count:
            final, sums = lax.optimization_barrier((final, sums))
        if tick + 1 == ticks:
            up_grads = block_grads(kept_rows, kept_upgrad, up_index[0], up_count[0], live_rows)
            sums, up_grads = lax.optimization_barrier((sums, up_grads))
        send = None
        if any_fwd and tick < last + micro_count - 1:
            layer_out = (current.astype(jnp.float32) + sums).astype(jnp.bfloat16)
            kept_output = put(kept_output, layer_out, place)
            send = layer_out
        if any_bwd:
            values, inv_rms, _ = normalize(take(kept_input, place_bwd, tok_rows), gain)
            scaled_grad = sums * gain.astype(jnp.float32)
            norm_term = inv_rms * scaled_grad - values * (inv_rms * inv_rms * inv_rms) * jnp.mean(
                scaled_grad * values, axis=-1, keepdims=True
            )
            grad_in = (incoming.astype(jnp.float32) + norm_term).astype(jnp.bfloat16)
            kept_ingrad = put(kept_ingrad, grad_in, place_bwd)
            send = grad_in if send is None else jnp.where(bwd_active, grad_in, send)
        if tick + 1 == ticks:
            break
        pairs = []
        for micro in range(micro_count):
            done = tick - micro
            if 0 <= done < rounds - 1:
                pairs.append((last - abs(last - done), last - abs(last - done - 1)))
        current = lax.ppermute(send, "section", pairs)
        if tick + 1 < micro_count:
            current = jnp.where(section_index == 0, inputs[tick + 1], current)
        next_fwd = tick + 1 <= last + micro_count - 1
        next_bwd = tick + 1 > last
        source = current
        if next_fwd:
            source = normalize(current, gain)[2]
            if next_bwd:
                source = jnp.where(section_index + micro_count > tick + 1, source, current)
        gathered = all_rows(source)

    down_grads = block_grads(kept_hidden, kept_grad, down_index[0], down_count[0], live_rows)
    final_out = (kept_input[: micro_count * tok_rows].astype(jnp.float32) + final_sums).astype(jnp.bfloat16)
    outputs = jnp.where(is_last, final_out, kept_output[: micro_count * tok_rows])
    shape = (1, micro_count, tok_rows, features)
    return (
        outputs.reshape(shape),
        kept_ingrad[: micro_count * tok_rows].reshape(shape),
        up_grads[None],
        down_grads[None],
    )


def solution(mesh):
    return jax.shard_map(
        shards,
        mesh=mesh,
        in_specs=(
            P(None, "tp", None),
            P(None, "tp", None),
            P("section", None),
            P("section", "tp", None),
            P("section", "tp"),
            P("section", "tp"),
            P("section", "tp", None),
            P("section", "tp"),
            P("section", "tp"),
        ),
        out_specs=(
            P("section", None, "tp", None),
            P("section", None, "tp", None),
            P("section", "tp", None),
            P("section", "tp", None),
        ),
        check_vma=False,
    )
```

```python
import functools

import jax
import jax.numpy as jnp
from jax import lax
from jax.experimental import pallas as pl
from jax.experimental.pallas import tpu as pltpu
from jax.sharding import PartitionSpec as P

FF = 16384
BLOCK = 64
MICRO = 2
STREAMS = 4
PAIR = 2 * BLOCK
HALF = BLOCK // 2
STRIP = 256
VMEM_BYTES = 58 * 2**20

NORM_EPSILON = 1e-05


def slot_step(slots):
    for size in (192, 128, 64, 32, 16):
        if slots % size == 0:
            return size
    return slots


def split_order(rows_split):
    first = lax.broadcasted_iota(jnp.int32, (STRIP, STRIP), 0)
    second = lax.broadcasted_iota(jnp.int32, (STRIP, STRIP), 1)
    split, natural = (first, second) if rows_split else (second, first)
    inner = split % BLOCK
    target = (split - inner) + 2 * (inner % HALF) + inner // HALF
    return (target == natural).astype(jnp.bfloat16)


def densify_kernel(slots, step_slots, index_ref, count_ref, block_ref, out_ref, held, packed, place):
    step = pl.program_id(0)
    load_steps = slots // step_slots
    width = out_ref.shape[1]
    pairs = width // PAIR
    spare = place.shape[0] - 1

    @pl.when(step == 0)
    def _():
        held[slots] = jnp.zeros((HALF, PAIR), jnp.bfloat16)

        @pl.loop(0, spare // 16)
        def _(group):
            for lane in range(16):
                place[group * 16 + lane] = slots

    @pl.when(step < load_steps)
    def _():
        first = step * step_slots
        for start in range(0, step_slots, 16):
            packed[start : start + 16] = block_ref[start : start + 16, :].reshape(16, HALF, PAIR)
        held[pl.ds(first, step_slots)] = packed[...]

        @pl.loop(0, step_slots // 16)
        def _(group):
            start = pl.multiple_of(group * 16, 16)
            for lane in range(16):
                slot = first + start + lane
                place[jnp.where(slot < count_ref[0], index_ref[slot], spare)] = slot

    @pl.when(step >= load_steps)
    def _():
        strip = step - load_steps
        lane = lax.broadcasted_iota(jnp.int32, (HALF, PAIR), 1)
        low = lane < BLOCK
        for row in range(STRIP // BLOCK):
            for col in range(pairs):
                pair = (strip * (STRIP // BLOCK) + row) * pairs + col
                left = held[place[2 * pair]]
                right = held[place[2 * pair + 1]]
                top = row * BLOCK
                lanes = slice(col * PAIR, (col + 1) * PAIR)
                crossed = pltpu.roll(jnp.where(low, right, left), BLOCK, 1)
                out_ref[top : top + HALF, lanes] = jnp.where(low, left, crossed)
                out_ref[top + HALF : top + BLOCK, lanes] = jnp.where(low, crossed, right)


def densify(blocks, block_index, live_count, row_blocks, col_blocks):
    slots = blocks.shape[0]
    step_slots = slot_step(slots)
    load_steps = slots // step_slots
    width = min(col_blocks * BLOCK, 2048)
    across = col_blocks * BLOCK // width
    strips = row_blocks * BLOCK // STRIP
    if across > 1:
        piece_blocks = width // BLOCK
        row, col = block_index // col_blocks, block_index % col_blocks
        strip, row = row // 4, row % 4
        block_index = ((strip * across + col // piece_blocks) * 4 + row) * piece_blocks + col % piece_blocks

    def out_place(step, index, count):
        spot = jnp.maximum(step - load_steps, 0)
        return (spot // across, spot % across)

    return pl.pallas_call(
        functools.partial(densify_kernel, slots, step_slots),
        grid_spec=pltpu.PrefetchScalarGridSpec(
            num_scalar_prefetch=2,
            grid=(load_steps + strips * across,),
            in_specs=[
                pl.BlockSpec((step_slots, BLOCK * BLOCK), lambda step, index, count: (jnp.minimum(step, load_steps - 1), 0))
            ],
            out_specs=pl.BlockSpec((STRIP, width), out_place),
            scratch_shapes=[
                pltpu.VMEM((slots + 1, HALF, PAIR), jnp.bfloat16),
                pltpu.VMEM((step_slots, HALF, PAIR), jnp.bfloat16),
                pltpu.SMEM((row_blocks * col_blocks + 1,), jnp.int32),
            ],
        ),
        out_shape=jax.ShapeDtypeStruct((row_blocks * BLOCK, col_blocks * BLOCK), jnp.bfloat16),
        compiler_params=pltpu.CompilerParams(
            dimension_semantics=("arbitrary",), vmem_limit_bytes=VMEM_BYTES
        ),
        name="densify",
    )(block_index, live_count, blocks)


def block_grads_kernel(strips, step_slots, index_ref, count_ref, left_ref, right_ref, out_ref, dense, packed):
    step = pl.program_id(0)
    width = right_ref.shape[1]
    pairs = width // PAIR

    @pl.when(step < strips)
    def _():
        left = left_ref[...].T
        high = left.shape[0] // BLOCK
        piece = min(width, 512)

        @pl.loop(0, width // piece)
        def _(number):
            lanes = pl.ds(pl.multiple_of(number * piece, piece), piece)
            product = jnp.dot(left, right_ref[:, lanes], preferred_element_type=jnp.float32).astype(jnp.bfloat16)
            for row in range(high):
                for col in range(piece // PAIR):
                    pair = (step * high + row) * pairs + number * (piece // PAIR) + col
                    cut = slice(col * PAIR, (col + 1) * PAIR)
                    dense[2 * pair] = product[row * BLOCK : row * BLOCK + HALF, cut]
                    dense[2 * pair + 1] = product[row * BLOCK + HALF : (row + 1) * BLOCK, cut]

    @pl.when(step >= strips)
    def _():
        first = (step - strips) * step_slots
        lane = lax.broadcasted_iota(jnp.int32, (HALF, PAIR), 1)
        low = lane < BLOCK

        @pl.loop(0, step_slots // 16)
        def _(group):
            start = pl.multiple_of(group * 16, 16)
            for one in range(16):
                slot = first + start + one
                spot = index_ref[slot]
                keep = dense[spot]
                other = pltpu.roll(dense[spot ^ 1], BLOCK, 1)
                picked = jnp.where(low == (spot % 2 == 0), keep, other)
                packed[one] = jnp.where(slot < count_ref[0], picked, jnp.zeros_like(picked))
            out_ref[pl.ds(start, 16), :] = packed[...].reshape(16, BLOCK * BLOCK)


def block_grads(left, right, block_index, live_count, tokens):
    rows = left.shape[1]
    cols = right.shape[1]
    slots = block_index.shape[0]
    step_slots = slot_step(slots)
    strip = min(rows, 1024)
    strips = rows // strip
    return pl.pallas_call(
        functools.partial(block_grads_kernel, strips, step_slots),
        grid_spec=pltpu.PrefetchScalarGridSpec(
            num_scalar_prefetch=2,
            grid=(strips + slots // step_slots,),
            in_specs=[
                pl.BlockSpec((tokens, strip), lambda step, index, count: (0, jnp.minimum(step, strips - 1))),
                pl.BlockSpec((tokens, cols), lambda step, index, count: (0, 0)),
            ],
            out_specs=pl.BlockSpec(
                (step_slots, BLOCK * BLOCK), lambda step, index, count: (jnp.maximum(step - strips, 0), 0)
            ),
            scratch_shapes=[
                pltpu.VMEM((rows * cols // (HALF * PAIR), HALF, PAIR), jnp.bfloat16),
                pltpu.VMEM((16, HALF, PAIR), jnp.bfloat16),
            ],
        ),
        out_shape=jax.ShapeDtypeStruct((slots, BLOCK * BLOCK), jnp.bfloat16),
        compiler_params=pltpu.CompilerParams(
            dimension_semantics=("arbitrary",), vmem_limit_bytes=VMEM_BYTES
        ),
        cost_estimate=pl.CostEstimate(
            flops=6 * tokens * rows * cols, bytes_accessed=6 * rows * cols, transcendentals=0
        ),
        name="block_grads",
    )(block_index, live_count, left, right)


def normalize(activ_rows, gain):
    values = activ_rows.astype(jnp.float32)
    inv_rms = lax.rsqrt(jnp.mean(values * values, axis=-1, keepdims=True) + NORM_EPSILON)
    return (values, inv_rms, (values * inv_rms * gain.astype(jnp.float32)).astype(jnp.bfloat16))


def same_core():
    count = lax.axis_size("tp")
    return [list(range(core, count, 2)) for core in range(2)]


def other_core(array):
    return lax.ppermute(array, "tp", [(index, index ^ 1) for index in range(lax.axis_size("tp"))])


def all_rows(local_rows):
    return lax.all_gather(local_rows, "tp", axis=0, tiled=True)


def row_sums(part_own, part_other):
    chip = (part_own.astype(jnp.float32) + other_core(part_other).astype(jnp.float32)).astype(jnp.bfloat16)
    return lax.psum_scatter(
        chip, "tp", scatter_dimension=0, tiled=True, axis_index_groups=same_core()
    ).astype(jnp.float32)


def reordered(values, order, dtype=jnp.bfloat16):
    groups = [
        jnp.dot(values[:, start : start + STRIP], order, preferred_element_type=jnp.float32).astype(dtype)
        for start in range(0, values.shape[1], STRIP)
    ]
    return groups[0] if len(groups) == 1 else jnp.concatenate(groups, axis=1)


def reordered_wide(values, order):
    high = values.astype(jnp.bfloat16)
    low = (values - high.astype(jnp.float32)).astype(jnp.bfloat16)
    return reordered(high, order, jnp.float32) + reordered(low, order, jnp.float32)


def times_turned(left, refs):
    transposed = (((1,), (1,)), ((), ()))
    width = refs[0].shape[1]
    total = None
    for number, ref in enumerate(refs):
        part = lax.dot_general(
            left[:, number * width : (number + 1) * width], ref[...], transposed, preferred_element_type=jnp.float32
        )
        total = part if total is None else total + part
    return total


def core_halves(part, local_count, core):
    pieces = [part[start : start + local_count] for start in range(0, part.shape[0], local_count)]
    even = jnp.concatenate(pieces[0::2], axis=0)
    odd = jnp.concatenate(pieces[1::2], axis=0)
    return jnp.where(core == 0, even, odd), jnp.where(core == 0, odd, even)


def forward_kernel(up_steps, turn, base, local_count, flags, rows_ref, *rest):
    ups, downs, rest = rest[:STREAMS], rest[STREAMS : 2 * STREAMS], rest[2 * STREAMS :]
    outs = rest[len(rest) - 8 - turn :]
    part_own, part_other, kept_rows, kept_up, kept_hidden = outs[:5]
    total, order, back = outs[-3:]
    step = pl.program_id(0)
    depth = ups[0].shape[0]
    up_active, down_active, turn_active = flags[base + 0] > 0, flags[base + 1] > 0, flags[base + 3] > 0

    @pl.when(up_active & (step < up_steps))
    def _():
        @pl.when(step == 0)
        def _():
            total[...] = jnp.zeros_like(total)
            order[...] = split_order(False)
            back[...] = split_order(True)

        features = pl.ds(pl.multiple_of(step * depth, depth), depth)
        rows = reordered(rows_ref[:, features], order[...])
        kept_rows[:, features] = rows
        width = ups[0].shape[1]
        for number, ref in enumerate(ups):
            lanes = slice(number * width, (number + 1) * width)
            total[:, lanes] += jnp.dot(rows, ref[...], preferred_element_type=jnp.float32)

        @pl.when(step == up_steps - 1)
        def _():
            proj = total[...]
            kept_up[...] = proj
            gate = 1.0 / (1.0 + jnp.exp(-proj))
            kept_hidden[...] = reordered((proj * gate).astype(jnp.bfloat16), order[...])
            if turn:
                pre_ref, kept_upgrad = rest[0], outs[5]
                act_grad = reordered_wide(pre_ref[...], back[...])
                kept_upgrad[...] = (act_grad * gate * (1.0 + proj * (1.0 - gate))).astype(jnp.bfloat16)

    @pl.when(step >= up_steps)
    def _():
        @pl.when(down_active)
        def _():
            width = downs[0].shape[1]
            hidden = kept_hidden[...]
            for number, ref in enumerate(downs):
                part = jnp.dot(hidden, ref[...], preferred_element_type=jnp.float32).astype(jnp.bfloat16)
                lanes = slice(number * width, (number + 1) * width)
                part_own[:, lanes], part_other[:, lanes] = core_halves(part, local_count, flags[base + 6])

        if turn:

            @pl.when(turn_active)
            def _():
                part = reordered(times_turned(outs[5][...], ups).astype(jnp.bfloat16), back[...])
                part_own[...], part_other[...] = core_halves(part, local_count, flags[base + 6])

        @pl.when(jnp.logical_not(down_active | turn_active))
        def _():
            part_own[...] = jnp.zeros_like(part_own)
            part_other[...] = jnp.zeros_like(part_other)


def layer_cost(tokens, features, units):
    return pl.CostEstimate(flops=4 * tokens * features * units, bytes_accessed=4 * features * units, transcendentals=0)


def forward_layer(flags, base, local_count, rows, w_up, w_down, kept, pre=None):
    turn = pre is not None
    tokens, features = rows.shape
    half = tokens // 2
    units = w_up.shape[1]
    depth = 1024
    up_steps = down_steps = features // depth
    last_up = up_steps - 1
    up_width, down_width = units // STREAMS, depth // STREAMS
    any_space = [pl.BlockSpec(memory_space=pl.ANY)] * len(kept)

    def up_place(number):
        def place(step, flags):
            plain = flags[base + 0] * jnp.minimum(step, last_up)
            return (jnp.where(flags[base + 3] > 0, step % up_steps, plain) if turn else plain, number)

        return place

    def down_place(number):
        return lambda step, flags: (0, STREAMS * flags[base + 1] * jnp.maximum(step - up_steps, 0) + number)

    def part_place(step, flags):
        return (0, jnp.maximum(step - up_steps, 0))

    def kept_place(step, flags):
        return (flags[base + 2], 0)

    pre_spec = [pl.BlockSpec((tokens, units), lambda step, flags: (jnp.minimum(flags[base + 2], MICRO - 1), 0))] * turn
    inputs = [flags, rows, *[w_up] * STREAMS, *[w_down] * STREAMS, *[pre] * turn]
    places = (MICRO + 1) * tokens
    return pl.pallas_call(
        functools.partial(forward_kernel, up_steps, turn, base, local_count),
        grid_spec=pltpu.PrefetchScalarGridSpec(
            num_scalar_prefetch=1,
            grid=(up_steps + down_steps,),
            in_specs=[pl.BlockSpec((tokens, features), lambda step, flags: (0, 0))]
            + [pl.BlockSpec((depth, up_width), up_place(number)) for number in range(STREAMS)]
            + [pl.BlockSpec((units, down_width), down_place(number)) for number in range(STREAMS)]
            + pre_spec
            + any_space,
            out_specs=[pl.BlockSpec((half, depth), part_place)] * 2
            + [
                pl.BlockSpec((tokens, features), kept_place),
                pl.BlockSpec((tokens, units), kept_place),
                pl.BlockSpec((tokens, units), kept_place),
            ]
            + [pl.BlockSpec((tokens, units), kept_place)] * turn,
            scratch_shapes=[
                pltpu.VMEM((tokens, units), jnp.float32),
                pltpu.VMEM((STRIP, STRIP), jnp.bfloat16),
                pltpu.VMEM((STRIP, STRIP), jnp.bfloat16),
            ],
        ),
        out_shape=[jax.ShapeDtypeStruct((half, features), jnp.bfloat16)] * 2
        + [
            jax.ShapeDtypeStruct((places, features), jnp.bfloat16),
            jax.ShapeDtypeStruct((places, units), jnp.float32),
            jax.ShapeDtypeStruct((places, units), jnp.bfloat16),
        ]
        + [jax.ShapeDtypeStruct((places, units), jnp.bfloat16)] * turn,
        input_output_aliases={len(inputs) + number: 2 + number for number in range(len(kept))},
        compiler_params=pltpu.CompilerParams(dimension_semantics=("arbitrary",), vmem_limit_bytes=VMEM_BYTES),
        cost_estimate=layer_cost(tokens, features, units),
        name="forward_layer",
    )(*inputs, *kept)


def backward_kernel(down_steps, base, local_count, flags, grad_ref, proj_ref, *rest):
    downs, ups = rest[:STREAMS], rest[STREAMS : 2 * STREAMS]
    part_own, part_other, kept_grad, kept_upgrad, back = rest[-5:]
    step = pl.program_id(0)
    width = downs[0].shape[0]
    active = flags[base + 4] > 0

    @pl.when(active & (step < down_steps))
    def _():
        @pl.when(step == 0)
        def _():
            kept_grad[...] = grad_ref[...]
            back[...] = split_order(True)

        act_grad = reordered_wide(times_turned(grad_ref, downs), back[...])
        lanes = pl.ds(pl.multiple_of(step * width, width), width)
        proj = proj_ref[:, lanes]
        gate = 1.0 / (1.0 + jnp.exp(-proj))
        kept_upgrad[:, lanes] = (act_grad * gate * (1.0 + proj * (1.0 - gate))).astype(jnp.bfloat16)

    @pl.when(step >= down_steps)
    def _():
        @pl.when(active)
        def _():
            part = reordered(times_turned(kept_upgrad[...], ups).astype(jnp.bfloat16), back[...])
            part_own[...], part_other[...] = core_halves(part, local_count, flags[base + 6])

        @pl.when(jnp.logical_not(active))
        def _():
            part_own[...] = jnp.zeros_like(part_own)
            part_other[...] = jnp.zeros_like(part_other)


def backward_layer(flags, base, local_count, grad, kept_up, w_up, w_down, kept):
    tokens, features = grad.shape
    half = tokens // 2
    units = w_up.shape[1]
    width, depth = min(units, STRIP), 1024
    down_steps, up_steps = units // width, features // depth
    last_down = down_steps - 1
    any_space = [pl.BlockSpec(memory_space=pl.ANY)] * len(kept)

    def down_place(number):
        return lambda step, flags: (flags[base + 4] * jnp.minimum(step, last_down), number)

    def up_place(number):
        return lambda step, flags: (flags[base + 4] * jnp.maximum(step - down_steps, 0), number)

    def part_place(step, flags):
        return (0, jnp.maximum(step - down_steps, 0))

    def kept_place(step, flags):
        return (flags[base + 5], 0)

    inputs = [flags, grad, kept_up, *[w_down] * STREAMS, *[w_up] * STREAMS]
    places = (MICRO + 1) * tokens
    return pl.pallas_call(
        functools.partial(backward_kernel, down_steps, base, local_count),
        grid_spec=pltpu.PrefetchScalarGridSpec(
            num_scalar_prefetch=1,
            grid=(down_steps + up_steps,),
            in_specs=[pl.BlockSpec((tokens, features), lambda step, flags: (0, 0))]
            + [pl.BlockSpec((tokens, units), kept_place)]
            + [pl.BlockSpec((width, features // STREAMS), down_place(number)) for number in range(STREAMS)]
            + [pl.BlockSpec((depth, units // STREAMS), up_place(number)) for number in range(STREAMS)]
            + any_space,
            out_specs=[pl.BlockSpec((half, depth), part_place)] * 2
            + [pl.BlockSpec((tokens, features), kept_place), pl.BlockSpec((tokens, units), kept_place)],
            scratch_shapes=[pltpu.VMEM((STRIP, STRIP), jnp.bfloat16)],
        ),
        out_shape=[jax.ShapeDtypeStruct((half, features), jnp.bfloat16)] * 2
        + [
            jax.ShapeDtypeStruct((places, features), jnp.bfloat16),
            jax.ShapeDtypeStruct((places, units), jnp.bfloat16),
        ],
        input_output_aliases={len(inputs) + number: 2 + number for number in range(len(kept))},
        compiler_params=pltpu.CompilerParams(dimension_semantics=("arbitrary",), vmem_limit_bytes=VMEM_BYTES),
        cost_estimate=layer_cost(tokens, features, units),
        name="backward_layer",
    )(*inputs, *kept)


def put(buffer, value, place):
    return lax.dynamic_update_slice_in_dim(buffer, value, place * value.shape[0], 0)


def take(buffer, place, count):
    return lax.dynamic_slice_in_dim(buffer, place * count, count, 0)


def shards(
    inputs, cotangent, gains, up_blocks, up_index, up_count, down_blocks, down_index, down_count
):
    micro_count, tok_rows, features = inputs.shape
    section_index = lax.axis_index("section")
    section_count = lax.axis_size("section")
    last = section_count - 1
    tp_count = lax.axis_size("tp")
    group_width = FF // tp_count
    total_rows = tok_rows * tp_count
    row_blocks = features // BLOCK
    group_blocks = group_width // BLOCK
    gain = gains[0]
    gathered = all_rows(normalize(inputs[0], gain)[2])
    cot_rows = [all_rows(cotangent[micro]) for micro in range(micro_count)]
    w_up = densify(up_blocks[0], up_index[0], up_count[0], row_blocks, group_blocks)
    w_down = densify(down_blocks[0], down_index[0], down_count[0], group_blocks, row_blocks)
    gathered, cot_rows, w_up, w_down = lax.optimization_barrier((gathered, cot_rows, w_up, w_down))
    live_rows = micro_count * total_rows

    places = micro_count + 1
    kept_fwd = []
    kept_input = jnp.zeros((places * tok_rows, features), jnp.bfloat16)
    kept_output = jnp.zeros((places * tok_rows, features), jnp.bfloat16)
    kept_ingrad = jnp.zeros((places * tok_rows, features), jnp.bfloat16)
    is_last = section_index == last

    rounds = 2 * section_count - 1
    ticks = rounds + micro_count - 1
    current = inputs[0]
    table = []
    for tick in range(ticks):
        micro_fwd = tick - section_index
        micro_bwd = tick - (2 * last - section_index)
        fwd_active = (micro_fwd >= 0) & (micro_fwd < micro_count)
        bwd_active = (micro_bwd >= 0) & (micro_bwd < micro_count) & jnp.logical_not(is_last)
        table += [
            fwd_active,
            fwd_active & jnp.logical_not(is_last),
            jnp.where(fwd_active, micro_fwd, micro_count),
            fwd_active & is_last,
            bwd_active,
            jnp.where(bwd_active, micro_bwd, micro_count),
            lax.axis_index("tp") % 2,
        ]
    flags = jnp.stack([jnp.asarray(entry, jnp.int32) for entry in table])
    flags, gathered = lax.optimization_barrier((flags, gathered))
    for tick in range(ticks):
        base = 7 * tick
        micro_fwd = tick - section_index
        micro_bwd = tick - (2 * last - section_index)
        fwd_active = (micro_fwd >= 0) & (micro_fwd < micro_count)
        bwd_active = (micro_bwd >= 0) & (micro_bwd < micro_count)
        any_fwd = tick <= last + micro_count - 1
        any_bwd = tick >= last
        partial = None
        if tick + 1 == ticks:
            final, gathered = lax.optimization_barrier((final, gathered))
            final_sums = lax.psum_scatter(final, "tp", scatter_dimension=0, tiled=True).astype(jnp.float32)
        if any_fwd:
            place = jnp.where(fwd_active, micro_fwd, micro_count)
            if tick < last:
                *partial, kept_rows, kept_up, kept_hidden = forward_layer(
                    flags, base, tok_rows, gathered, w_up, w_down, kept_fwd
                )
                kept_fwd = [kept_rows, kept_up, kept_hidden]
            else:
                *partial, kept_rows, kept_up, kept_hidden, kept_upgrad = forward_layer(
                    flags, base, tok_rows, gathered, w_up, w_down, kept_fwd, pre_grad
                )
                kept_fwd = [kept_rows, kept_up, kept_hidden, kept_upgrad]
            kept_input = put(kept_input, current, place)
        if tick == 0:
            cot_rows, partial = lax.optimization_barrier((cot_rows, partial))
            kept_grad = jnp.concatenate(cot_rows + [jnp.zeros((total_rows, features), jnp.bfloat16)])
        if tick == 1:
            cot_all, partial = lax.optimization_barrier((kept_grad, partial))
            pre_grad = lax.cond(
                is_last,
                lambda: jnp.dot(cot_all[:live_rows], w_down.T, preferred_element_type=jnp.float32),
                lambda: jnp.zeros((live_rows, group_width), jnp.float32),
            )
        if any_bwd:
            place_bwd = jnp.where(bwd_active, micro_bwd, micro_count)
            incoming = current
            if tick - last < micro_count:
                incoming = jnp.where(is_last, cotangent[tick - last], current)
        if tick > last:
            *back, kept_grad, kept_upgrad = backward_layer(
                flags, base, tok_rows, gathered, kept_up, w_up, w_down, [kept_grad, kept_upgrad]
            )
            if any_fwd:
                back = [jnp.where(is_last, turned, one) for turned, one in zip(partial, back)]
            partial = back
        if tick == last + micro_count:
            hidden, partial = lax.optimization_barrier((kept_hidden, partial))

            def last_sums():
                parts = jnp.dot(hidden[:live_rows], w_down, preferred_element_type=jnp.float32).astype(jnp.bfloat16)
                parts = parts.reshape(micro_count, tp_count, tok_rows, features)
                return parts.swapaxes(0, 1).reshape(live_rows, features)

            final = lax.cond(is_last, last_sums, lambda: jnp.zeros((live_rows, features), jnp.bfloat16))
        sums = row_sums(*partial)
        if tick == 1:
            pre_grad, sums = lax.optimization_barrier((pre_grad, sums))
        if tick == last + micro_count:
            final, sums = lax.optimization_barrier((final, sums))
        if tick + 1 == ticks:
            up_grads = block_grads(kept_rows, kept_upgrad, up_index[0], up_count[0], live_rows)
            sums, up_grads = lax.optimization_barrier((sums, up_grads))
        send = None
        if any_fwd and tick < last + micro_count - 1:
            layer_out = (current.astype(jnp.float32) + sums).astype(jnp.bfloat16)
            kept_output = put(kept_output, layer_out, place)
            send = layer_out
        if any_bwd:
            values, inv_rms, _ = normalize(take(kept_input, place_bwd, tok_rows), gain)
            scaled_grad = sums * gain.astype(jnp.float32)
            norm_term = inv_rms * scaled_grad - values * (inv_rms * inv_rms * inv_rms) * jnp.mean(
                scaled_grad * values, axis=-1, keepdims=True
            )
            grad_in = (incoming.astype(jnp.float32) + norm_term).astype(jnp.bfloat16)
            kept_ingrad = put(kept_ingrad, grad_in, place_bwd)
            send = grad_in if send is None else jnp.where(bwd_active, grad_in, send)
        if tick + 1 == ticks:
            break
        pairs = []
        for micro in range(micro_count):
            done = tick - micro
            if 0 <= done < rounds - 1:
                pairs.append((last - abs(last - done), last - abs(last - done - 1)))
        current = lax.ppermute(send, "section", pairs)
        if tick + 1 < micro_count:
            current = jnp.where(section_index == 0, inputs[tick + 1], current)
        next_fwd = tick + 1 <= last + micro_count - 1
        next_bwd = tick + 1 > last
        source = current
        if next_fwd:
            source = normalize(current, gain)[2]
            if next_bwd:
                source = jnp.where(section_index + micro_count > tick + 1, source, current)
        gathered = all_rows(source)

    down_grads = block_grads(kept_hidden, kept_grad, down_index[0], down_count[0], live_rows)
    final_out = (kept_input[: micro_count * tok_rows].astype(jnp.float32) + final_sums).astype(jnp.bfloat16)
    outputs = jnp.where(is_last, final_out, kept_output[: micro_count * tok_rows])
    shape = (1, micro_count, tok_rows, features)
    return (
        outputs.reshape(shape),
        kept_ingrad[: micro_count * tok_rows].reshape(shape),
        up_grads[None],
        down_grads[None],
    )


def solution(mesh):
    return jax.shard_map(
        shards,
        mesh=mesh,
        in_specs=(
            P(None, "tp", None),
            P(None, "tp", None),
            P("section", None),
            P("section", "tp", None),
            P("section", "tp"),
            P("section", "tp"),
            P("section", "tp", None),
            P("section", "tp"),
            P("section", "tp"),
        ),
        out_specs=(
            P("section", None, "tp", None),
            P("section", None, "tp", None),
            P("section", "tp", None),
            P("section", "tp", None),
        ),
        check_vma=False,
    )
```

```python
import functools

import jax
import jax.numpy as jnp
from jax import lax
from jax.experimental import pallas as pl
from jax.experimental.pallas import tpu as pltpu
from jax.sharding import PartitionSpec as P

FF = 16384
BLOCK = 64
MICRO = 2
STREAMS = 1
PAIR = 2 * BLOCK
HALF = BLOCK // 2
STRIP = 256
VMEM_BYTES = 58 * 2**20

NORM_EPSILON = 1e-05


def slot_step(slots):
    for size in (192, 128, 64, 32, 16):
        if slots % size == 0:
            return size
    return slots


def split_order(rows_split):
    first = lax.broadcasted_iota(jnp.int32, (STRIP, STRIP), 0)
    second = lax.broadcasted_iota(jnp.int32, (STRIP, STRIP), 1)
    split, natural = (first, second) if rows_split else (second, first)
    inner = split % BLOCK
    target = (split - inner) + 2 * (inner % HALF) + inner // HALF
    return (target == natural).astype(jnp.bfloat16)


def densify_kernel(slots, step_slots, index_ref, count_ref, block_ref, out_ref, held, packed, place):
    step = pl.program_id(0)
    load_steps = slots // step_slots
    width = out_ref.shape[1]
    pairs = width // PAIR
    spare = place.shape[0] - 1

    @pl.when(step == 0)
    def _():
        held[slots] = jnp.zeros((HALF, PAIR), jnp.bfloat16)

        @pl.loop(0, spare // 16)
        def _(group):
            for lane in range(16):
                place[group * 16 + lane] = slots

    @pl.when(step < load_steps)
    def _():
        first = step * step_slots
        for start in range(0, step_slots, 16):
            packed[start : start + 16] = block_ref[start : start + 16, :].reshape(16, HALF, PAIR)
        held[pl.ds(first, step_slots)] = packed[...]

        @pl.loop(0, step_slots // 16)
        def _(group):
            start = pl.multiple_of(group * 16, 16)
            for lane in range(16):
                slot = first + start + lane
                place[jnp.where(slot < count_ref[0], index_ref[slot], spare)] = slot

    @pl.when(step >= load_steps)
    def _():
        strip = step - load_steps
        lane = lax.broadcasted_iota(jnp.int32, (HALF, PAIR), 1)
        low = lane < BLOCK
        for row in range(STRIP // BLOCK):
            for col in range(pairs):
                pair = (strip * (STRIP // BLOCK) + row) * pairs + col
                left = held[place[2 * pair]]
                right = held[place[2 * pair + 1]]
                top = row * BLOCK
                lanes = slice(col * PAIR, (col + 1) * PAIR)
                crossed = pltpu.roll(jnp.where(low, right, left), BLOCK, 1)
                out_ref[top : top + HALF, lanes] = jnp.where(low, left, crossed)
                out_ref[top + HALF : top + BLOCK, lanes] = jnp.where(low, crossed, right)


def densify(blocks, block_index, live_count, row_blocks, col_blocks):
    slots = blocks.shape[0]
    step_slots = slot_step(slots)
    load_steps = slots // step_slots
    width = min(col_blocks * BLOCK, 2048)
    across = col_blocks * BLOCK // width
    strips = row_blocks * BLOCK // STRIP
    if across > 1:
        piece_blocks = width // BLOCK
        row, col = block_index // col_blocks, block_index % col_blocks
        strip, row = row // 4, row % 4
        block_index = ((strip * across + col // piece_blocks) * 4 + row) * piece_blocks + col % piece_blocks

    def out_place(step, index, count):
        spot = jnp.maximum(step - load_steps, 0)
        return (spot // across, spot % across)

    return pl.pallas_call(
        functools.partial(densify_kernel, slots, step_slots),
        grid_spec=pltpu.PrefetchScalarGridSpec(
            num_scalar_prefetch=2,
            grid=(load_steps + strips * across,),
            in_specs=[
                pl.BlockSpec((step_slots, BLOCK * BLOCK), lambda step, index, count: (jnp.minimum(step, load_steps - 1), 0))
            ],
            out_specs=pl.BlockSpec((STRIP, width), out_place),
            scratch_shapes=[
                pltpu.VMEM((slots + 1, HALF, PAIR), jnp.bfloat16),
                pltpu.VMEM((step_slots, HALF, PAIR), jnp.bfloat16),
                pltpu.SMEM((row_blocks * col_blocks + 1,), jnp.int32),
            ],
        ),
        out_shape=jax.ShapeDtypeStruct((row_blocks * BLOCK, col_blocks * BLOCK), jnp.bfloat16),
        compiler_params=pltpu.CompilerParams(
            dimension_semantics=("arbitrary",), vmem_limit_bytes=VMEM_BYTES
        ),
        name="densify",
    )(block_index, live_count, blocks)


def block_grads_kernel(strips, step_slots, index_ref, count_ref, left_ref, right_ref, out_ref, dense, packed):
    step = pl.program_id(0)
    width = right_ref.shape[1]
    pairs = width // PAIR

    @pl.when(step < strips)
    def _():
        left = left_ref[...].T
        high = left.shape[0] // BLOCK
        piece = min(width, 512)

        @pl.loop(0, width // piece)
        def _(number):
            lanes = pl.ds(pl.multiple_of(number * piece, piece), piece)
            product = jnp.dot(left, right_ref[:, lanes], preferred_element_type=jnp.float32).astype(jnp.bfloat16)
            for row in range(high):
                for col in range(piece // PAIR):
                    pair = (step * high + row) * pairs + number * (piece // PAIR) + col
                    cut = slice(col * PAIR, (col + 1) * PAIR)
                    dense[2 * pair] = product[row * BLOCK : row * BLOCK + HALF, cut]
                    dense[2 * pair + 1] = product[row * BLOCK + HALF : (row + 1) * BLOCK, cut]

    @pl.when(step >= strips)
    def _():
        first = (step - strips) * step_slots
        lane = lax.broadcasted_iota(jnp.int32, (HALF, PAIR), 1)
        low = lane < BLOCK

        @pl.loop(0, step_slots // 16)
        def _(group):
            start = pl.multiple_of(group * 16, 16)
            for one in range(16):
                slot = first + start + one
                spot = index_ref[slot]
                keep = dense[spot]
                other = pltpu.roll(dense[spot ^ 1], BLOCK, 1)
                picked = jnp.where(low == (spot % 2 == 0), keep, other)
                packed[one] = jnp.where(slot < count_ref[0], picked, jnp.zeros_like(picked))
            out_ref[pl.ds(start, 16), :] = packed[...].reshape(16, BLOCK * BLOCK)


def block_grads(left, right, block_index, live_count, tokens):
    rows = left.shape[1]
    cols = right.shape[1]
    slots = block_index.shape[0]
    step_slots = slot_step(slots)
    strip = min(rows, 1024 if rows > cols else STRIP)
    strips = rows // strip
    return pl.pallas_call(
        functools.partial(block_grads_kernel, strips, step_slots),
        grid_spec=pltpu.PrefetchScalarGridSpec(
            num_scalar_prefetch=2,
            grid=(strips + slots // step_slots,),
            in_specs=[
                pl.BlockSpec((tokens, strip), lambda step, index, count: (0, jnp.minimum(step, strips - 1))),
                pl.BlockSpec((tokens, cols), lambda step, index, count: (0, 0)),
            ],
            out_specs=pl.BlockSpec(
                (step_slots, BLOCK * BLOCK), lambda step, index, count: (jnp.maximum(step - strips, 0), 0)
            ),
            scratch_shapes=[
                pltpu.VMEM((rows * cols // (HALF * PAIR), HALF, PAIR), jnp.bfloat16),
                pltpu.VMEM((16, HALF, PAIR), jnp.bfloat16),
            ],
        ),
        out_shape=jax.ShapeDtypeStruct((slots, BLOCK * BLOCK), jnp.bfloat16),
        compiler_params=pltpu.CompilerParams(
            dimension_semantics=("arbitrary",), vmem_limit_bytes=VMEM_BYTES
        ),
        cost_estimate=pl.CostEstimate(
            flops=6 * tokens * rows * cols, bytes_accessed=6 * rows * cols, transcendentals=0
        ),
        name="block_grads",
    )(block_index, live_count, left, right)


def normalize(activ_rows, gain):
    values = activ_rows.astype(jnp.float32)
    inv_rms = lax.rsqrt(jnp.mean(values * values, axis=-1, keepdims=True) + NORM_EPSILON)
    return (values, inv_rms, (values * inv_rms * gain.astype(jnp.float32)).astype(jnp.bfloat16))


def same_core():
    count = lax.axis_size("tp")
    return [list(range(core, count, 2)) for core in range(2)]


def other_core(array):
    return lax.ppermute(array, "tp", [(index, index ^ 1) for index in range(lax.axis_size("tp"))])


def all_rows(local_rows):
    return lax.all_gather(local_rows, "tp", axis=0, tiled=True)


def row_sums(part_own, part_other):
    chip = (part_own.astype(jnp.float32) + other_core(part_other).astype(jnp.float32)).astype(jnp.bfloat16)
    return lax.psum_scatter(
        chip, "tp", scatter_dimension=0, tiled=True, axis_index_groups=same_core()
    ).astype(jnp.float32)


def reordered(values, order, dtype=jnp.bfloat16):
    groups = [
        jnp.dot(values[:, start : start + STRIP], order, preferred_element_type=jnp.float32).astype(dtype)
        for start in range(0, values.shape[1], STRIP)
    ]
    return groups[0] if len(groups) == 1 else jnp.concatenate(groups, axis=1)


def reordered_wide(values, order):
    high = values.astype(jnp.bfloat16)
    low = (values - high.astype(jnp.float32)).astype(jnp.bfloat16)
    return reordered(high, order, jnp.float32) + reordered(low, order, jnp.float32)


def times_turned(left, refs):
    transposed = (((1,), (1,)), ((), ()))
    width = refs[0].shape[1]
    total = None
    for number, ref in enumerate(refs):
        part = lax.dot_general(
            left[:, number * width : (number + 1) * width], ref[...], transposed, preferred_element_type=jnp.float32
        )
        total = part if total is None else total + part
    return total


def core_halves(part, local_count, core):
    pieces = [part[start : start + local_count] for start in range(0, part.shape[0], local_count)]
    even = jnp.concatenate(pieces[0::2], axis=0)
    odd = jnp.concatenate(pieces[1::2], axis=0)
    return jnp.where(core == 0, even, odd), jnp.where(core == 0, odd, even)


def forward_kernel(up_steps, turn, base, local_count, flags, rows_ref, *rest):
    ups, downs, rest = rest[:STREAMS], rest[STREAMS : 2 * STREAMS], rest[2 * STREAMS :]
    outs = rest[len(rest) - 8 - turn :]
    part_own, part_other, kept_rows, kept_up, kept_hidden = outs[:5]
    total, order, back = outs[-3:]
    step = pl.program_id(0)
    depth = ups[0].shape[0]
    up_active, down_active, turn_active = flags[base + 0] > 0, flags[base + 1] > 0, flags[base + 3] > 0

    @pl.when(up_active & (step < up_steps))
    def _():
        @pl.when(step == 0)
        def _():
            total[...] = jnp.zeros_like(total)
            order[...] = split_order(False)
            back[...] = split_order(True)

        features = pl.ds(pl.multiple_of(step * depth, depth), depth)
        rows = reordered(rows_ref[:, features], order[...])
        kept_rows[:, features] = rows
        width = ups[0].shape[1]
        for number, ref in enumerate(ups):
            lanes = slice(number * width, (number + 1) * width)
            total[:, lanes] += jnp.dot(rows, ref[...], preferred_element_type=jnp.float32)

        @pl.when(step == up_steps - 1)
        def _():
            proj = total[...]
            kept_up[...] = proj
            gate = 1.0 / (1.0 + jnp.exp(-proj))
            kept_hidden[...] = reordered((proj * gate).astype(jnp.bfloat16), order[...])
            if turn:
                pre_ref, kept_upgrad = rest[0], outs[5]
                act_grad = reordered_wide(pre_ref[...], back[...])
                kept_upgrad[...] = (act_grad * gate * (1.0 + proj * (1.0 - gate))).astype(jnp.bfloat16)

    @pl.when(step >= up_steps)
    def _():
        @pl.when(down_active)
        def _():
            width = downs[0].shape[1]
            hidden = kept_hidden[...]
            for number, ref in enumerate(downs):
                part = jnp.dot(hidden, ref[...], preferred_element_type=jnp.float32).astype(jnp.bfloat16)
                lanes = slice(number * width, (number + 1) * width)
                part_own[:, lanes], part_other[:, lanes] = core_halves(part, local_count, flags[base + 6])

        if turn:

            @pl.when(turn_active)
            def _():
                part = reordered(times_turned(outs[5][...], ups).astype(jnp.bfloat16), back[...])
                part_own[...], part_other[...] = core_halves(part, local_count, flags[base + 6])

        @pl.when(jnp.logical_not(down_active | turn_active))
        def _():
            part_own[...] = jnp.zeros_like(part_own)
            part_other[...] = jnp.zeros_like(part_other)


def layer_cost(tokens, features, units):
    return pl.CostEstimate(flops=4 * tokens * features * units, bytes_accessed=4 * features * units, transcendentals=0)


def forward_layer(flags, base, local_count, rows, w_up, w_down, kept, pre=None):
    turn = pre is not None
    tokens, features = rows.shape
    half = tokens // 2
    units = w_up.shape[1]
    depth = 1024
    up_steps = down_steps = features // depth
    last_up = up_steps - 1
    up_width, down_width = units // STREAMS, depth // STREAMS
    any_space = [pl.BlockSpec(memory_space=pl.ANY)] * len(kept)

    def up_place(number):
        def place(step, flags):
            plain = flags[base + 0] * jnp.minimum(step, last_up)
            return (jnp.where(flags[base + 3] > 0, step % up_steps, plain) if turn else plain, number)

        return place

    def down_place(number):
        return lambda step, flags: (0, STREAMS * flags[base + 1] * jnp.maximum(step - up_steps, 0) + number)

    def part_place(step, flags):
        return (0, jnp.maximum(step - up_steps, 0))

    def kept_place(step, flags):
        return (flags[base + 2], 0)

    pre_spec = [pl.BlockSpec((tokens, units), lambda step, flags: (jnp.minimum(flags[base + 2], MICRO - 1), 0))] * turn
    inputs = [flags, rows, *[w_up] * STREAMS, *[w_down] * STREAMS, *[pre] * turn]
    places = (MICRO + 1) * tokens
    return pl.pallas_call(
        functools.partial(forward_kernel, up_steps, turn, base, local_count),
        grid_spec=pltpu.PrefetchScalarGridSpec(
            num_scalar_prefetch=1,
            grid=(up_steps + down_steps,),
            in_specs=[pl.BlockSpec((tokens, features), lambda step, flags: (0, 0))]
            + [pl.BlockSpec((depth, up_width), up_place(number)) for number in range(STREAMS)]
            + [pl.BlockSpec((units, down_width), down_place(number)) for number in range(STREAMS)]
            + pre_spec
            + any_space,
            out_specs=[pl.BlockSpec((half, depth), part_place)] * 2
            + [
                pl.BlockSpec((tokens, features), kept_place),
                pl.BlockSpec((tokens, units), kept_place),
                pl.BlockSpec((tokens, units), kept_place),
            ]
            + [pl.BlockSpec((tokens, units), kept_place)] * turn,
            scratch_shapes=[
                pltpu.VMEM((tokens, units), jnp.float32),
                pltpu.VMEM((STRIP, STRIP), jnp.bfloat16),
                pltpu.VMEM((STRIP, STRIP), jnp.bfloat16),
            ],
        ),
        out_shape=[jax.ShapeDtypeStruct((half, features), jnp.bfloat16)] * 2
        + [
            jax.ShapeDtypeStruct((places, features), jnp.bfloat16),
            jax.ShapeDtypeStruct((places, units), jnp.float32),
            jax.ShapeDtypeStruct((places, units), jnp.bfloat16),
        ]
        + [jax.ShapeDtypeStruct((places, units), jnp.bfloat16)] * turn,
        input_output_aliases={len(inputs) + number: 2 + number for number in range(len(kept))},
        compiler_params=pltpu.CompilerParams(dimension_semantics=("arbitrary",), vmem_limit_bytes=VMEM_BYTES),
        cost_estimate=layer_cost(tokens, features, units),
        name="forward_layer",
    )(*inputs, *kept)


def backward_kernel(down_steps, base, local_count, flags, grad_ref, proj_ref, *rest):
    downs, ups = rest[:STREAMS], rest[STREAMS : 2 * STREAMS]
    part_own, part_other, kept_grad, kept_upgrad, back = rest[-5:]
    step = pl.program_id(0)
    width = downs[0].shape[0]
    active = flags[base + 4] > 0

    @pl.when(active & (step < down_steps))
    def _():
        @pl.when(step == 0)
        def _():
            kept_grad[...] = grad_ref[...]
            back[...] = split_order(True)

        act_grad = reordered_wide(times_turned(grad_ref, downs), back[...])
        lanes = pl.ds(pl.multiple_of(step * width, width), width)
        proj = proj_ref[:, lanes]
        gate = 1.0 / (1.0 + jnp.exp(-proj))
        kept_upgrad[:, lanes] = (act_grad * gate * (1.0 + proj * (1.0 - gate))).astype(jnp.bfloat16)

    @pl.when(step >= down_steps)
    def _():
        @pl.when(active)
        def _():
            part = reordered(times_turned(kept_upgrad[...], ups).astype(jnp.bfloat16), back[...])
            part_own[...], part_other[...] = core_halves(part, local_count, flags[base + 6])

        @pl.when(jnp.logical_not(active))
        def _():
            part_own[...] = jnp.zeros_like(part_own)
            part_other[...] = jnp.zeros_like(part_other)


def backward_layer(flags, base, local_count, grad, kept_up, w_up, w_down, kept):
    tokens, features = grad.shape
    half = tokens // 2
    units = w_up.shape[1]
    width, depth = min(units, STRIP), 1024
    down_steps, up_steps = units // width, features // depth
    last_down = down_steps - 1
    any_space = [pl.BlockSpec(memory_space=pl.ANY)] * len(kept)

    def down_place(number):
        return lambda step, flags: (flags[base + 4] * jnp.minimum(step, last_down), number)

    def up_place(number):
        return lambda step, flags: (flags[base + 4] * jnp.maximum(step - down_steps, 0), number)

    def part_place(step, flags):
        return (0, jnp.maximum(step - down_steps, 0))

    def kept_place(step, flags):
        return (flags[base + 5], 0)

    inputs = [flags, grad, kept_up, *[w_down] * STREAMS, *[w_up] * STREAMS]
    places = (MICRO + 1) * tokens
    return pl.pallas_call(
        functools.partial(backward_kernel, down_steps, base, local_count),
        grid_spec=pltpu.PrefetchScalarGridSpec(
            num_scalar_prefetch=1,
            grid=(down_steps + up_steps,),
            in_specs=[pl.BlockSpec((tokens, features), lambda step, flags: (0, 0))]
            + [pl.BlockSpec((tokens, units), kept_place)]
            + [pl.BlockSpec((width, features // STREAMS), down_place(number)) for number in range(STREAMS)]
            + [pl.BlockSpec((depth, units // STREAMS), up_place(number)) for number in range(STREAMS)]
            + any_space,
            out_specs=[pl.BlockSpec((half, depth), part_place)] * 2
            + [pl.BlockSpec((tokens, features), kept_place), pl.BlockSpec((tokens, units), kept_place)],
            scratch_shapes=[pltpu.VMEM((STRIP, STRIP), jnp.bfloat16)],
        ),
        out_shape=[jax.ShapeDtypeStruct((half, features), jnp.bfloat16)] * 2
        + [
            jax.ShapeDtypeStruct((places, features), jnp.bfloat16),
            jax.ShapeDtypeStruct((places, units), jnp.bfloat16),
        ],
        input_output_aliases={len(inputs) + number: 2 + number for number in range(len(kept))},
        compiler_params=pltpu.CompilerParams(dimension_semantics=("arbitrary",), vmem_limit_bytes=VMEM_BYTES),
        cost_estimate=layer_cost(tokens, features, units),
        name="backward_layer",
    )(*inputs, *kept)


def put(buffer, value, place):
    return lax.dynamic_update_slice_in_dim(buffer, value, place * value.shape[0], 0)


def take(buffer, place, count):
    return lax.dynamic_slice_in_dim(buffer, place * count, count, 0)


def shards(
    inputs, cotangent, gains, up_blocks, up_index, up_count, down_blocks, down_index, down_count
):
    micro_count, tok_rows, features = inputs.shape
    section_index = lax.axis_index("section")
    section_count = lax.axis_size("section")
    last = section_count - 1
    tp_count = lax.axis_size("tp")
    group_width = FF // tp_count
    total_rows = tok_rows * tp_count
    row_blocks = features // BLOCK
    group_blocks = group_width // BLOCK
    gain = gains[0]
    gathered = all_rows(normalize(inputs[0], gain)[2])
    cot_rows = [all_rows(cotangent[micro]) for micro in range(micro_count)]
    w_up = densify(up_blocks[0], up_index[0], up_count[0], row_blocks, group_blocks)
    w_down = densify(down_blocks[0], down_index[0], down_count[0], group_blocks, row_blocks)
    gathered, cot_rows, w_up, w_down = lax.optimization_barrier((gathered, cot_rows, w_up, w_down))
    live_rows = micro_count * total_rows

    places = micro_count + 1
    kept_fwd = []
    kept_input = jnp.zeros((places * tok_rows, features), jnp.bfloat16)
    kept_output = jnp.zeros((places * tok_rows, features), jnp.bfloat16)
    kept_ingrad = jnp.zeros((places * tok_rows, features), jnp.bfloat16)
    is_last = section_index == last

    rounds = 2 * section_count - 1
    ticks = rounds + micro_count - 1
    current = inputs[0]
    table = []
    for tick in range(ticks):
        micro_fwd = tick - section_index
        micro_bwd = tick - (2 * last - section_index)
        fwd_active = (micro_fwd >= 0) & (micro_fwd < micro_count)
        bwd_active = (micro_bwd >= 0) & (micro_bwd < micro_count) & jnp.logical_not(is_last)
        table += [
            fwd_active,
            fwd_active & jnp.logical_not(is_last),
            jnp.where(fwd_active, micro_fwd, micro_count),
            fwd_active & is_last,
            bwd_active,
            jnp.where(bwd_active, micro_bwd, micro_count),
            lax.axis_index("tp") % 2,
        ]
    flags = jnp.stack([jnp.asarray(entry, jnp.int32) for entry in table])
    flags, gathered = lax.optimization_barrier((flags, gathered))
    for tick in range(ticks):
        base = 7 * tick
        micro_fwd = tick - section_index
        micro_bwd = tick - (2 * last - section_index)
        fwd_active = (micro_fwd >= 0) & (micro_fwd < micro_count)
        bwd_active = (micro_bwd >= 0) & (micro_bwd < micro_count)
        any_fwd = tick <= last + micro_count - 1
        any_bwd = tick >= last
        partial = None
        if tick + 1 == ticks:
            final, gathered = lax.optimization_barrier((final, gathered))
            final_sums = lax.psum_scatter(final, "tp", scatter_dimension=0, tiled=True).astype(jnp.float32)
        if any_fwd:
            place = jnp.where(fwd_active, micro_fwd, micro_count)
            if tick < last:
                *partial, kept_rows, kept_up, kept_hidden = forward_layer(
                    flags, base, tok_rows, gathered, w_up, w_down, kept_fwd
                )
                kept_fwd = [kept_rows, kept_up, kept_hidden]
            else:
                *partial, kept_rows, kept_up, kept_hidden, kept_upgrad = forward_layer(
                    flags, base, tok_rows, gathered, w_up, w_down, kept_fwd, pre_grad
                )
                kept_fwd = [kept_rows, kept_up, kept_hidden, kept_upgrad]
            kept_input = put(kept_input, current, place)
        if tick == 0:
            cot_rows, partial = lax.optimization_barrier((cot_rows, partial))
            kept_grad = jnp.concatenate(cot_rows + [jnp.zeros((total_rows, features), jnp.bfloat16)])
        if tick == 1:
            cot_all, partial = lax.optimization_barrier((kept_grad, partial))
            pre_grad = lax.cond(
                is_last,
                lambda: jnp.dot(cot_all[:live_rows], w_down.T, preferred_element_type=jnp.float32),
                lambda: jnp.zeros((live_rows, group_width), jnp.float32),
            )
        if any_bwd:
            place_bwd = jnp.where(bwd_active, micro_bwd, micro_count)
            incoming = current
            if tick - last < micro_count:
                incoming = jnp.where(is_last, cotangent[tick - last], current)
        if tick > last:
            *back, kept_grad, kept_upgrad = backward_layer(
                flags, base, tok_rows, gathered, kept_up, w_up, w_down, [kept_grad, kept_upgrad]
            )
            if any_fwd:
                back = [jnp.where(is_last, turned, one) for turned, one in zip(partial, back)]
            partial = back
        if tick == last + micro_count:
            hidden, partial = lax.optimization_barrier((kept_hidden, partial))

            def last_sums():
                parts = jnp.dot(hidden[:live_rows], w_down, preferred_element_type=jnp.float32).astype(jnp.bfloat16)
                parts = parts.reshape(micro_count, tp_count, tok_rows, features)
                return parts.swapaxes(0, 1).reshape(live_rows, features)

            final = lax.cond(is_last, last_sums, lambda: jnp.zeros((live_rows, features), jnp.bfloat16))
        sums = row_sums(*partial)
        if tick == 1:
            pre_grad, sums = lax.optimization_barrier((pre_grad, sums))
        if tick == last + micro_count:
            final, sums = lax.optimization_barrier((final, sums))
        if tick + 1 == ticks:
            up_grads = block_grads(kept_rows, kept_upgrad, up_index[0], up_count[0], live_rows)
            sums, up_grads = lax.optimization_barrier((sums, up_grads))
        send = None
        if any_fwd and tick < last + micro_count - 1:
            layer_out = (current.astype(jnp.float32) + sums).astype(jnp.bfloat16)
            kept_output = put(kept_output, layer_out, place)
            send = layer_out
        if any_bwd:
            values, inv_rms, _ = normalize(take(kept_input, place_bwd, tok_rows), gain)
            scaled_grad = sums * gain.astype(jnp.float32)
            norm_term = inv_rms * scaled_grad - values * (inv_rms * inv_rms * inv_rms) * jnp.mean(
                scaled_grad * values, axis=-1, keepdims=True
            )
            grad_in = (incoming.astype(jnp.float32) + norm_term).astype(jnp.bfloat16)
            kept_ingrad = put(kept_ingrad, grad_in, place_bwd)
            send = grad_in if send is None else jnp.where(bwd_active, grad_in, send)
        if tick + 1 == ticks:
            break
        pairs = []
        for micro in range(micro_count):
            done = tick - micro
            if 0 <= done < rounds - 1:
                pairs.append((last - abs(last - done), last - abs(last - done - 1)))
        current = lax.ppermute(send, "section", pairs)
        if tick + 1 < micro_count:
            current = jnp.where(section_index == 0, inputs[tick + 1], current)
        next_fwd = tick + 1 <= last + micro_count - 1
        next_bwd = tick + 1 > last
        source = current
        if next_fwd:
            source = normalize(current, gain)[2]
            if next_bwd:
                source = jnp.where(section_index + micro_count > tick + 1, source, current)
        gathered = all_rows(source)

    down_grads = block_grads(kept_hidden, kept_grad, down_index[0], down_count[0], live_rows)
    final_out = (kept_input[: micro_count * tok_rows].astype(jnp.float32) + final_sums).astype(jnp.bfloat16)
    outputs = jnp.where(is_last, final_out, kept_output[: micro_count * tok_rows])
    shape = (1, micro_count, tok_rows, features)
    return (
        outputs.reshape(shape),
        kept_ingrad[: micro_count * tok_rows].reshape(shape),
        up_grads[None],
        down_grads[None],
    )


def solution(mesh):
    return jax.shard_map(
        shards,
        mesh=mesh,
        in_specs=(
            P(None, "tp", None),
            P(None, "tp", None),
            P("section", None),
            P("section", "tp", None),
            P("section", "tp"),
            P("section", "tp"),
            P("section", "tp", None),
            P("section", "tp"),
            P("section", "tp"),
        ),
        out_specs=(
            P("section", None, "tp", None),
            P("section", None, "tp", None),
            P("section", "tp", None),
            P("section", "tp", None),
        ),
        check_vma=False,
    )
```

```python
import functools

import jax
import jax.numpy as jnp
from jax import lax
from jax.experimental import pallas as pl
from jax.experimental.pallas import tpu as pltpu
from jax.sharding import PartitionSpec as P

FF = 16384
BLOCK = 64
MICRO = 2
STREAMS = 1
PAIR = 2 * BLOCK
HALF = BLOCK // 2
STRIP = 256
VMEM_BYTES = 58 * 2**20

NORM_EPSILON = 1e-05


def slot_step(slots):
    for size in (192, 128, 64, 32, 16):
        if slots % size == 0:
            return size
    return slots


def split_order(rows_split):
    first = lax.broadcasted_iota(jnp.int32, (STRIP, STRIP), 0)
    second = lax.broadcasted_iota(jnp.int32, (STRIP, STRIP), 1)
    split, natural = (first, second) if rows_split else (second, first)
    inner = split % BLOCK
    target = (split - inner) + 2 * (inner % HALF) + inner // HALF
    return (target == natural).astype(jnp.bfloat16)


def densify_kernel(slots, step_slots, index_ref, count_ref, block_ref, out_ref, held, packed, place):
    step = pl.program_id(0)
    load_steps = slots // step_slots
    width = out_ref.shape[1]
    pairs = width // PAIR
    spare = place.shape[0] - 1

    @pl.when(step == 0)
    def _():
        held[slots] = jnp.zeros((HALF, PAIR), jnp.bfloat16)

        @pl.loop(0, spare // 16)
        def _(group):
            for lane in range(16):
                place[group * 16 + lane] = slots

    @pl.when(step < load_steps)
    def _():
        first = step * step_slots
        for start in range(0, step_slots, 16):
            packed[start : start + 16] = block_ref[start : start + 16, :].reshape(16, HALF, PAIR)
        held[pl.ds(first, step_slots)] = packed[...]

        @pl.loop(0, step_slots // 16)
        def _(group):
            start = pl.multiple_of(group * 16, 16)
            for lane in range(16):
                slot = first + start + lane
                place[jnp.where(slot < count_ref[0], index_ref[slot], spare)] = slot

    @pl.when(step >= load_steps)
    def _():
        strip = step - load_steps
        lane = lax.broadcasted_iota(jnp.int32, (HALF, PAIR), 1)
        low = lane < BLOCK
        for row in range(STRIP // BLOCK):
            for col in range(pairs):
                pair = (strip * (STRIP // BLOCK) + row) * pairs + col
                left = held[place[2 * pair]]
                right = held[place[2 * pair + 1]]
                top = row * BLOCK
                lanes = slice(col * PAIR, (col + 1) * PAIR)
                crossed = pltpu.roll(jnp.where(low, right, left), BLOCK, 1)
                out_ref[top : top + HALF, lanes] = jnp.where(low, left, crossed)
                out_ref[top + HALF : top + BLOCK, lanes] = jnp.where(low, crossed, right)


def densify(blocks, block_index, live_count, row_blocks, col_blocks):
    slots = blocks.shape[0]
    step_slots = slot_step(slots)
    load_steps = slots // step_slots
    width = min(col_blocks * BLOCK, 2048)
    across = col_blocks * BLOCK // width
    strips = row_blocks * BLOCK // STRIP
    if across > 1:
        piece_blocks = width // BLOCK
        row, col = block_index // col_blocks, block_index % col_blocks
        strip, row = row // 4, row % 4
        block_index = ((strip * across + col // piece_blocks) * 4 + row) * piece_blocks + col % piece_blocks

    def out_place(step, index, count):
        spot = jnp.maximum(step - load_steps, 0)
        return (spot // across, spot % across)

    return pl.pallas_call(
        functools.partial(densify_kernel, slots, step_slots),
        grid_spec=pltpu.PrefetchScalarGridSpec(
            num_scalar_prefetch=2,
            grid=(load_steps + strips * across,),
            in_specs=[
                pl.BlockSpec((step_slots, BLOCK * BLOCK), lambda step, index, count: (jnp.minimum(step, load_steps - 1), 0))
            ],
            out_specs=pl.BlockSpec((STRIP, width), out_place),
            scratch_shapes=[
                pltpu.VMEM((slots + 1, HALF, PAIR), jnp.bfloat16),
                pltpu.VMEM((step_slots, HALF, PAIR), jnp.bfloat16),
                pltpu.SMEM((row_blocks * col_blocks + 1,), jnp.int32),
            ],
        ),
        out_shape=jax.ShapeDtypeStruct((row_blocks * BLOCK, col_blocks * BLOCK), jnp.bfloat16),
        compiler_params=pltpu.CompilerParams(
            dimension_semantics=("arbitrary",), vmem_limit_bytes=VMEM_BYTES
        ),
        name="densify",
    )(block_index, live_count, blocks)


def block_grads_kernel(strips, step_slots, index_ref, count_ref, left_ref, right_ref, out_ref, dense, packed):
    step = pl.program_id(0)
    width = right_ref.shape[1]
    pairs = width // PAIR

    @pl.when(step < strips)
    def _():
        left = left_ref[...].T
        high = left.shape[0] // BLOCK
        piece = min(width, 512)

        @pl.loop(0, width // piece)
        def _(number):
            lanes = pl.ds(pl.multiple_of(number * piece, piece), piece)
            product = jnp.dot(left, right_ref[:, lanes], preferred_element_type=jnp.float32).astype(jnp.bfloat16)
            for row in range(high):
                for col in range(piece // PAIR):
                    pair = (step * high + row) * pairs + number * (piece // PAIR) + col
                    cut = slice(col * PAIR, (col + 1) * PAIR)
                    dense[2 * pair] = product[row * BLOCK : row * BLOCK + HALF, cut]
                    dense[2 * pair + 1] = product[row * BLOCK + HALF : (row + 1) * BLOCK, cut]

    @pl.when(step >= strips)
    def _():
        first = (step - strips) * step_slots
        lane = lax.broadcasted_iota(jnp.int32, (HALF, PAIR), 1)
        low = lane < BLOCK

        @pl.loop(0, step_slots // 16)
        def _(group):
            start = pl.multiple_of(group * 16, 16)
            for one in range(16):
                slot = first + start + one
                spot = index_ref[slot]
                keep = dense[spot]
                other = pltpu.roll(dense[spot ^ 1], BLOCK, 1)
                picked = jnp.where(low == (spot % 2 == 0), keep, other)
                packed[one] = jnp.where(slot < count_ref[0], picked, jnp.zeros_like(picked))
            out_ref[pl.ds(start, 16), :] = packed[...].reshape(16, BLOCK * BLOCK)


def block_grads(left, right, block_index, live_count, tokens):
    rows = left.shape[1]
    cols = right.shape[1]
    slots = block_index.shape[0]
    step_slots = slot_step(slots)
    strip = min(rows, 1024)
    strips = rows // strip
    return pl.pallas_call(
        functools.partial(block_grads_kernel, strips, step_slots),
        grid_spec=pltpu.PrefetchScalarGridSpec(
            num_scalar_prefetch=2,
            grid=(strips + slots // step_slots,),
            in_specs=[
                pl.BlockSpec((tokens, strip), lambda step, index, count: (0, jnp.minimum(step, strips - 1))),
                pl.BlockSpec((tokens, cols), lambda step, index, count: (0, 0)),
            ],
            out_specs=pl.BlockSpec(
                (step_slots, BLOCK * BLOCK), lambda step, index, count: (jnp.maximum(step - strips, 0), 0)
            ),
            scratch_shapes=[
                pltpu.VMEM((rows * cols // (HALF * PAIR), HALF, PAIR), jnp.bfloat16),
                pltpu.VMEM((16, HALF, PAIR), jnp.bfloat16),
            ],
        ),
        out_shape=jax.ShapeDtypeStruct((slots, BLOCK * BLOCK), jnp.bfloat16),
        compiler_params=pltpu.CompilerParams(
            dimension_semantics=("arbitrary",), vmem_limit_bytes=VMEM_BYTES
        ),
        cost_estimate=pl.CostEstimate(
            flops=6 * tokens * rows * cols, bytes_accessed=6 * rows * cols, transcendentals=0
        ),
        name="block_grads",
    )(block_index, live_count, left, right)


def normalize(activ_rows, gain):
    values = activ_rows.astype(jnp.float32)
    inv_rms = lax.rsqrt(jnp.mean(values * values, axis=-1, keepdims=True) + NORM_EPSILON)
    return (values, inv_rms, (values * inv_rms * gain.astype(jnp.float32)).astype(jnp.bfloat16))


def same_core():
    count = lax.axis_size("tp")
    return [list(range(core, count, 2)) for core in range(2)]


def other_core(array):
    return lax.ppermute(array, "tp", [(index, index ^ 1) for index in range(lax.axis_size("tp"))])


def all_rows(local_rows):
    return lax.all_gather(local_rows, "tp", axis=0, tiled=True)


def row_sums(part_own, part_other):
    chip = (part_own.astype(jnp.float32) + other_core(part_other).astype(jnp.float32)).astype(jnp.bfloat16)
    return lax.psum_scatter(
        chip, "tp", scatter_dimension=0, tiled=True, axis_index_groups=same_core()
    ).astype(jnp.float32)


def reordered(values, order, dtype=jnp.bfloat16):
    groups = [
        jnp.dot(values[:, start : start + STRIP], order, preferred_element_type=jnp.float32).astype(dtype)
        for start in range(0, values.shape[1], STRIP)
    ]
    return groups[0] if len(groups) == 1 else jnp.concatenate(groups, axis=1)


def reordered_wide(values, order):
    high = values.astype(jnp.bfloat16)
    low = (values - high.astype(jnp.float32)).astype(jnp.bfloat16)
    return reordered(high, order, jnp.float32) + reordered(low, order, jnp.float32)


def times_turned(left, refs):
    transposed = (((1,), (1,)), ((), ()))
    width = refs[0].shape[1]
    total = None
    for number, ref in enumerate(refs):
        part = lax.dot_general(
            left[:, number * width : (number + 1) * width], ref[...], transposed, preferred_element_type=jnp.float32
        )
        total = part if total is None else total + part
    return total


def core_halves(part, local_count, core):
    pieces = [part[start : start + local_count] for start in range(0, part.shape[0], local_count)]
    even = jnp.concatenate(pieces[0::2], axis=0)
    odd = jnp.concatenate(pieces[1::2], axis=0)
    return jnp.where(core == 0, even, odd), jnp.where(core == 0, odd, even)


def forward_kernel(up_steps, turn, base, local_count, flags, rows_ref, *rest):
    ups, downs, rest = rest[:STREAMS], rest[STREAMS : 2 * STREAMS], rest[2 * STREAMS :]
    outs = rest[len(rest) - 8 - turn :]
    part_own, part_other, kept_rows, kept_up, kept_hidden = outs[:5]
    total, order, back = outs[-3:]
    step = pl.program_id(0)
    depth = ups[0].shape[0]
    up_active, down_active, turn_active = flags[base + 0] > 0, flags[base + 1] > 0, flags[base + 3] > 0

    @pl.when(up_active & (step < up_steps))
    def _():
        @pl.when(step == 0)
        def _():
            total[...] = jnp.zeros_like(total)
            order[...] = split_order(False)
            back[...] = split_order(True)

        features = pl.ds(pl.multiple_of(step * depth, depth), depth)
        rows = reordered(rows_ref[:, features], order[...])
        kept_rows[:, features] = rows
        width = ups[0].shape[1]
        for number, ref in enumerate(ups):
            lanes = slice(number * width, (number + 1) * width)
            total[:, lanes] += jnp.dot(rows, ref[...], preferred_element_type=jnp.float32)

        @pl.when(step == up_steps - 1)
        def _():
            proj = total[...]
            kept_up[...] = proj
            gate = 1.0 / (1.0 + jnp.exp(-proj))
            kept_hidden[...] = reordered((proj * gate).astype(jnp.bfloat16), order[...])
            if turn:
                pre_ref, kept_upgrad = rest[0], outs[5]
                act_grad = reordered_wide(pre_ref[...], back[...])
                kept_upgrad[...] = (act_grad * gate * (1.0 + proj * (1.0 - gate))).astype(jnp.bfloat16)

    @pl.when(step >= up_steps)
    def _():
        @pl.when(down_active)
        def _():
            width = downs[0].shape[1]
            hidden = kept_hidden[...]
            for number, ref in enumerate(downs):
                part = jnp.dot(hidden, ref[...], preferred_element_type=jnp.float32).astype(jnp.bfloat16)
                lanes = slice(number * width, (number + 1) * width)
                part_own[:, lanes], part_other[:, lanes] = core_halves(part, local_count, flags[base + 6])

        if turn:

            @pl.when(turn_active)
            def _():
                part = reordered(times_turned(outs[5][...], ups).astype(jnp.bfloat16), back[...])
                part_own[...], part_other[...] = core_halves(part, local_count, flags[base + 6])

        @pl.when(jnp.logical_not(down_active | turn_active))
        def _():
            part_own[...] = jnp.zeros_like(part_own)
            part_other[...] = jnp.zeros_like(part_other)


def layer_cost(tokens, features, units):
    return pl.CostEstimate(flops=4 * tokens * features * units, bytes_accessed=4 * features * units, transcendentals=0)


def forward_layer(flags, base, local_count, rows, w_up, w_down, kept, pre=None):
    turn = pre is not None
    tokens, features = rows.shape
    half = tokens // 2
    units = w_up.shape[1]
    depth = 1024
    up_steps = down_steps = features // depth
    last_up = up_steps - 1
    up_width, down_width = units // STREAMS, depth // STREAMS
    any_space = [pl.BlockSpec(memory_space=pl.ANY)] * len(kept)

    def up_place(number):
        def place(step, flags):
            plain = flags[base + 0] * jnp.minimum(step, last_up)
            return (jnp.where(flags[base + 3] > 0, step % up_steps, plain) if turn else plain, number)

        return place

    def down_place(number):
        return lambda step, flags: (0, STREAMS * flags[base + 1] * jnp.maximum(step - up_steps, 0) + number)

    def part_place(step, flags):
        return (0, jnp.maximum(step - up_steps, 0))

    def kept_place(step, flags):
        return (flags[base + 2], 0)

    pre_spec = [pl.BlockSpec((tokens, units), lambda step, flags: (jnp.minimum(flags[base + 2], MICRO - 1), 0))] * turn
    inputs = [flags, rows, *[w_up] * STREAMS, *[w_down] * STREAMS, *[pre] * turn]
    places = (MICRO + 1) * tokens
    return pl.pallas_call(
        functools.partial(forward_kernel, up_steps, turn, base, local_count),
        grid_spec=pltpu.PrefetchScalarGridSpec(
            num_scalar_prefetch=1,
            grid=(up_steps + down_steps,),
            in_specs=[pl.BlockSpec((tokens, features), lambda step, flags: (0, 0))]
            + [pl.BlockSpec((depth, up_width), up_place(number)) for number in range(STREAMS)]
            + [pl.BlockSpec((units, down_width), down_place(number)) for number in range(STREAMS)]
            + pre_spec
            + any_space,
            out_specs=[pl.BlockSpec((half, depth), part_place)] * 2
            + [
                pl.BlockSpec((tokens, features), kept_place),
                pl.BlockSpec((tokens, units), kept_place),
                pl.BlockSpec((tokens, units), kept_place),
            ]
            + [pl.BlockSpec((tokens, units), kept_place)] * turn,
            scratch_shapes=[
                pltpu.VMEM((tokens, units), jnp.float32),
                pltpu.VMEM((STRIP, STRIP), jnp.bfloat16),
                pltpu.VMEM((STRIP, STRIP), jnp.bfloat16),
            ],
        ),
        out_shape=[jax.ShapeDtypeStruct((half, features), jnp.bfloat16)] * 2
        + [
            jax.ShapeDtypeStruct((places, features), jnp.bfloat16),
            jax.ShapeDtypeStruct((places, units), jnp.float32),
            jax.ShapeDtypeStruct((places, units), jnp.bfloat16),
        ]
        + [jax.ShapeDtypeStruct((places, units), jnp.bfloat16)] * turn,
        input_output_aliases={len(inputs) + number: 2 + number for number in range(len(kept))},
        compiler_params=pltpu.CompilerParams(dimension_semantics=("arbitrary",), vmem_limit_bytes=VMEM_BYTES),
        cost_estimate=layer_cost(tokens, features, units),
        name="forward_layer",
    )(*inputs, *kept)


def backward_kernel(down_steps, base, local_count, flags, grad_ref, proj_ref, *rest):
    downs, ups = rest[:STREAMS], rest[STREAMS : 2 * STREAMS]
    part_own, part_other, kept_grad, kept_upgrad, back = rest[-5:]
    step = pl.program_id(0)
    width = downs[0].shape[0]
    active = flags[base + 4] > 0

    @pl.when(active & (step < down_steps))
    def _():
        @pl.when(step == 0)
        def _():
            kept_grad[...] = grad_ref[...]
            back[...] = split_order(True)

        act_grad = reordered_wide(times_turned(grad_ref, downs), back[...])
        lanes = pl.ds(pl.multiple_of(step * width, width), width)
        proj = proj_ref[:, lanes]
        gate = 1.0 / (1.0 + jnp.exp(-proj))
        kept_upgrad[:, lanes] = (act_grad * gate * (1.0 + proj * (1.0 - gate))).astype(jnp.bfloat16)

    @pl.when(step >= down_steps)
    def _():
        @pl.when(active)
        def _():
            part = reordered(times_turned(kept_upgrad[...], ups).astype(jnp.bfloat16), back[...])
            part_own[...], part_other[...] = core_halves(part, local_count, flags[base + 6])

        @pl.when(jnp.logical_not(active))
        def _():
            part_own[...] = jnp.zeros_like(part_own)
            part_other[...] = jnp.zeros_like(part_other)


def backward_layer(flags, base, local_count, grad, kept_up, w_up, w_down, kept):
    tokens, features = grad.shape
    half = tokens // 2
    units = w_up.shape[1]
    width, depth = min(units, STRIP), 1024
    down_steps, up_steps = units // width, features // depth
    last_down = down_steps - 1
    any_space = [pl.BlockSpec(memory_space=pl.ANY)] * len(kept)

    def down_place(number):
        return lambda step, flags: (flags[base + 4] * jnp.minimum(step, last_down), number)

    def up_place(number):
        return lambda step, flags: (flags[base + 4] * jnp.maximum(step - down_steps, 0), number)

    def part_place(step, flags):
        return (0, jnp.maximum(step - down_steps, 0))

    def kept_place(step, flags):
        return (flags[base + 5], 0)

    inputs = [flags, grad, kept_up, *[w_down] * STREAMS, *[w_up] * STREAMS]
    places = (MICRO + 1) * tokens
    return pl.pallas_call(
        functools.partial(backward_kernel, down_steps, base, local_count),
        grid_spec=pltpu.PrefetchScalarGridSpec(
            num_scalar_prefetch=1,
            grid=(down_steps + up_steps,),
            in_specs=[pl.BlockSpec((tokens, features), lambda step, flags: (0, 0))]
            + [pl.BlockSpec((tokens, units), kept_place)]
            + [pl.BlockSpec((width, features // STREAMS), down_place(number)) for number in range(STREAMS)]
            + [pl.BlockSpec((depth, units // STREAMS), up_place(number)) for number in range(STREAMS)]
            + any_space,
            out_specs=[pl.BlockSpec((half, depth), part_place)] * 2
            + [pl.BlockSpec((tokens, features), kept_place), pl.BlockSpec((tokens, units), kept_place)],
            scratch_shapes=[pltpu.VMEM((STRIP, STRIP), jnp.bfloat16)],
        ),
        out_shape=[jax.ShapeDtypeStruct((half, features), jnp.bfloat16)] * 2
        + [
            jax.ShapeDtypeStruct((places, features), jnp.bfloat16),
            jax.ShapeDtypeStruct((places, units), jnp.bfloat16),
        ],
        input_output_aliases={len(inputs) + number: 2 + number for number in range(len(kept))},
        compiler_params=pltpu.CompilerParams(dimension_semantics=("arbitrary",), vmem_limit_bytes=VMEM_BYTES),
        cost_estimate=layer_cost(tokens, features, units),
        name="backward_layer",
    )(*inputs, *kept)


def put(buffer, value, place):
    return lax.dynamic_update_slice_in_dim(buffer, value, place * value.shape[0], 0)


def take(buffer, place, count):
    return lax.dynamic_slice_in_dim(buffer, place * count, count, 0)


def shards(
    inputs, cotangent, gains, up_blocks, up_index, up_count, down_blocks, down_index, down_count
):
    micro_count, tok_rows, features = inputs.shape
    section_index = lax.axis_index("section")
    section_count = lax.axis_size("section")
    last = section_count - 1
    tp_count = lax.axis_size("tp")
    group_width = FF // tp_count
    total_rows = tok_rows * tp_count
    row_blocks = features // BLOCK
    group_blocks = group_width // BLOCK
    gain = gains[0]
    gathered = all_rows(normalize(inputs[0], gain)[2])
    cot_rows = [all_rows(cotangent[micro]) for micro in range(micro_count)]
    w_up = densify(up_blocks[0], up_index[0], up_count[0], row_blocks, group_blocks)
    w_down = densify(down_blocks[0], down_index[0], down_count[0], group_blocks, row_blocks)
    gathered, cot_rows, w_up, w_down = lax.optimization_barrier((gathered, cot_rows, w_up, w_down))
    live_rows = micro_count * total_rows

    places = micro_count + 1
    kept_fwd = []
    kept_input = jnp.zeros((places * tok_rows, features), jnp.bfloat16)
    kept_output = jnp.zeros((places * tok_rows, features), jnp.bfloat16)
    kept_ingrad = jnp.zeros((places * tok_rows, features), jnp.bfloat16)
    is_last = section_index == last

    rounds = 2 * section_count - 1
    ticks = rounds + micro_count - 1
    current = inputs[0]
    table = []
    for tick in range(ticks):
        micro_fwd = tick - section_index
        micro_bwd = tick - (2 * last - section_index)
        fwd_active = (micro_fwd >= 0) & (micro_fwd < micro_count)
        bwd_active = (micro_bwd >= 0) & (micro_bwd < micro_count) & jnp.logical_not(is_last)
        table += [
            fwd_active,
            fwd_active & jnp.logical_not(is_last),
            jnp.where(fwd_active, micro_fwd, micro_count),
            fwd_active & is_last,
            bwd_active,
            jnp.where(bwd_active, micro_bwd, micro_count),
            lax.axis_index("tp") % 2,
        ]
    flags = jnp.stack([jnp.asarray(entry, jnp.int32) for entry in table])
    flags, gathered = lax.optimization_barrier((flags, gathered))
    for tick in range(ticks):
        base = 7 * tick
        micro_fwd = tick - section_index
        micro_bwd = tick - (2 * last - section_index)
        fwd_active = (micro_fwd >= 0) & (micro_fwd < micro_count)
        bwd_active = (micro_bwd >= 0) & (micro_bwd < micro_count)
        any_fwd = tick <= last + micro_count - 1
        any_bwd = tick >= last
        partial = None
        if tick + 1 == ticks:
            final, gathered = lax.optimization_barrier((final, gathered))
            final_sums = lax.psum_scatter(final, "tp", scatter_dimension=0, tiled=True).astype(jnp.float32)
        if any_fwd:
            place = jnp.where(fwd_active, micro_fwd, micro_count)
            if tick < last:
                *partial, kept_rows, kept_up, kept_hidden = forward_layer(
                    flags, base, tok_rows, gathered, w_up, w_down, kept_fwd
                )
                kept_fwd = [kept_rows, kept_up, kept_hidden]
            else:
                *partial, kept_rows, kept_up, kept_hidden, kept_upgrad = forward_layer(
                    flags, base, tok_rows, gathered, w_up, w_down, kept_fwd, pre_grad
                )
                kept_fwd = [kept_rows, kept_up, kept_hidden, kept_upgrad]
            kept_input = put(kept_input, current, place)
        if tick == 0:
            cot_rows, partial = lax.optimization_barrier((cot_rows, partial))
            kept_grad = jnp.concatenate(cot_rows + [jnp.zeros((total_rows, features), jnp.bfloat16)])
        if tick == 1:
            cot_all, partial = lax.optimization_barrier((kept_grad, partial))
            pre_grad = lax.cond(
                is_last,
                lambda: jnp.dot(cot_all[:live_rows], w_down.T, preferred_element_type=jnp.float32),
                lambda: jnp.zeros((live_rows, group_width), jnp.float32),
            )
        if any_bwd:
            place_bwd = jnp.where(bwd_active, micro_bwd, micro_count)
            incoming = current
            if tick - last < micro_count:
                incoming = jnp.where(is_last, cotangent[tick - last], current)
        if tick > last:
            *back, kept_grad, kept_upgrad = backward_layer(
                flags, base, tok_rows, gathered, kept_up, w_up, w_down, [kept_grad, kept_upgrad]
            )
            if any_fwd:
                back = [jnp.where(is_last, turned, one) for turned, one in zip(partial, back)]
            partial = back
        if tick == last + micro_count:
            hidden, partial = lax.optimization_barrier((kept_hidden, partial))

            def last_sums():
                parts = jnp.dot(hidden[:live_rows], w_down, preferred_element_type=jnp.float32).astype(jnp.bfloat16)
                parts = parts.reshape(micro_count, tp_count, tok_rows, features)
                return parts.swapaxes(0, 1).reshape(live_rows, features)

            final = lax.cond(is_last, last_sums, lambda: jnp.zeros((live_rows, features), jnp.bfloat16))
        sums = row_sums(*partial)
        if tick == 1:
            pre_grad, sums = lax.optimization_barrier((pre_grad, sums))
        if tick == last + micro_count:
            final, sums = lax.optimization_barrier((final, sums))
        if tick + 1 == ticks:
            up_grads = block_grads(kept_rows, kept_upgrad, up_index[0], up_count[0], live_rows)
            sums, up_grads = lax.optimization_barrier((sums, up_grads))
        send = None
        if any_fwd and tick < last + micro_count - 1:
            layer_out = (current.astype(jnp.float32) + sums).astype(jnp.bfloat16)
            kept_output = put(kept_output, layer_out, place)
            send = layer_out
        if any_bwd:
            values, inv_rms, _ = normalize(take(kept_input, place_bwd, tok_rows), gain)
            scaled_grad = sums * gain.astype(jnp.float32)
            norm_term = inv_rms * scaled_grad - values * (inv_rms * inv_rms * inv_rms) * jnp.mean(
                scaled_grad * values, axis=-1, keepdims=True
            )
            grad_in = (incoming.astype(jnp.float32) + norm_term).astype(jnp.bfloat16)
            kept_ingrad = put(kept_ingrad, grad_in, place_bwd)
            send = grad_in if send is None else jnp.where(bwd_active, grad_in, send)
        if tick + 1 == ticks:
            break
        pairs = []
        for micro in range(micro_count):
            done = tick - micro
            if 0 <= done < rounds - 1:
                pairs.append((last - abs(last - done), last - abs(last - done - 1)))
        current = lax.ppermute(send, "section", pairs)
        if tick + 1 < micro_count:
            current = jnp.where(section_index == 0, inputs[tick + 1], current)
        next_fwd = tick + 1 <= last + micro_count - 1
        next_bwd = tick + 1 > last
        source = current
        if next_fwd:
            source = normalize(current, gain)[2]
            if next_bwd:
                source = jnp.where(section_index + micro_count > tick + 1, source, current)
        gathered = all_rows(source)

    down_grads = block_grads(kept_hidden, kept_grad, down_index[0], down_count[0], live_rows)
    final_out = (kept_input[: micro_count * tok_rows].astype(jnp.float32) + final_sums).astype(jnp.bfloat16)
    outputs = jnp.where(is_last, final_out, kept_output[: micro_count * tok_rows])
    shape = (1, micro_count, tok_rows, features)
    return (
        outputs.reshape(shape),
        kept_ingrad[: micro_count * tok_rows].reshape(shape),
        up_grads[None],
        down_grads[None],
    )


def solution(mesh):
    return jax.shard_map(
        shards,
        mesh=mesh,
        in_specs=(
            P(None, "tp", None),
            P(None, "tp", None),
            P("section", None),
            P("section", "tp", None),
            P("section", "tp"),
            P("section", "tp"),
            P("section", "tp", None),
            P("section", "tp"),
            P("section", "tp"),
        ),
        out_specs=(
            P("section", None, "tp", None),
            P("section", None, "tp", None),
            P("section", "tp", None),
            P("section", "tp", None),
        ),
        check_vma=False,
    )
```
